128 devices in a mesh: section: 2 (over core), dev: 64 (over y, z, x).
Axes of the slice: x: 4, y: 4, z: 4, core: 2. Of those that a mesh axis runs over, the one named last changes fastest.
Arguments:
- inputs: bfloat16 [2, 8192, 1024], P(None, 'dev'), may hold values from -6 to 6
- lengths: int32 [2, 64, 4], P(None, 'dev'), may hold values from 1 to 64, 128 in all within a row
- expand_weight: bfloat16 [1024, 4, 1024], P(None, None, 'section'), may hold values from -0.1875 to 0.1875
- mixing_weight: bfloat16 [1024, 1024], P('section'), may hold values from -0.1875 to 0.1875
- projection: bfloat16 [1024, 256], replicated, may hold values from -0.375 to 0.375
- saved_rows: bfloat16 [2, 8192, 256], P(None, 'dev'), may hold values from -103 to 103
- cluster_ids: int32 [2, 8192], P(None, 'dev'), may hold values from 0 to 4095, as said below
- item_ids: int32 [2, 8192], P(None, 'dev'), may hold values from 0 to 511
- top_table: bfloat16 [4096, 256], P('section'), may hold values from -4 to 4
- codebook: bfloat16 [4096, 512, 256], P('dev', 'section'), may hold values from -4 to 4
Outputs:
- grad_inputs: bfloat16 [2, 8192, 1024], P(None, 'dev')
- grad_expand: float32 [1024, 4, 1024], P('dev', None, 'section')
- grad_mixing: float32 [1024, 1024], P('section', 'dev')
- grad_table: float32 [4096, 256], P(('section', 'dev'))
- grad_codebook: bfloat16 [4096, 512, 256], P('dev', 'section')
The draws below stay inside these ranges and needn't reach their ends.
Inputs may be any that keep to these rules, and one draw needn't show every extreme that they name: `cluster_ids`: cluster k belongs to owner k // 64. The 128 rows of one device of dev name clusters of one owner at most 4 times, and in each micro-batch one owner is named exactly 4 times by the rows of every device. The 4 lengths of one device sum to 128.
All inputs are finite; a program needn't handle non-finite values.
Results may differ from the reference program's by a relative error of at most 0.014.
Values may be sent and summed in bfloat16 or wider, within the bound.
No kernel may reach another device: no remote copies, remote signals or barrier semaphores. Data moves between devices by JAX's collectives and lax.ppermute only.
A program may use at most 192 MiB of HBM per device.

```python
import math
import jax
import jax.numpy as jnp
import numpy as np
from jax import lax

D_MODEL = 1024
HEAD_DIM = 128
HEAD_WIDTH = 256
ITEMS = 512
CL_DEV = 64
ROW_DEV = 128
MICRO = 2
SEQS = 4
SEQ_MOST = 64
ROWS = 8192
CLUSTERS = 4096
CAP = 4
N_SECTION = 2
N_DEV = 64


def routing(key):
    owners = CLUSTERS // CL_DEV
    slot_count = owners * CAP
    sub_keys = jax.random.split(jax.random.fold_in(key, 11), 5)
    hot_owner = jax.random.randint(sub_keys[0], (MICRO, 1, 1), 0, owners).astype(jnp.int32)
    rank_keys = jax.random.split(sub_keys[1], MICRO * owners)
    slot_ranks = jax.vmap(lambda single: jax.random.permutation(single, slot_count))(rank_keys)
    slot_ranks = slot_ranks.reshape(MICRO, owners, slot_count).astype(jnp.int32)
    slot_owner = (jnp.arange(slot_count, dtype=jnp.int32) // CAP).reshape(1, 1, slot_count)
    scores = slot_ranks + jnp.where(slot_owner == hot_owner, slot_count, 0).astype(jnp.int32)
    picked = lax.top_k(scores, ROW_DEV)[1].astype(jnp.int32)
    shuffle_keys = jax.random.split(sub_keys[2], MICRO * owners)
    shuffle = jax.vmap(lambda single: jax.random.permutation(single, ROW_DEV))(shuffle_keys)
    picked = jnp.take_along_axis(picked, shuffle.reshape(MICRO, owners, ROW_DEV).astype(jnp.int32), axis=2)
    owner_ids = picked // CAP
    local_ids = jax.random.randint(sub_keys[3], owner_ids.shape, 0, CL_DEV).astype(jnp.int32)
    clusters = (owner_ids * CL_DEV + local_ids).reshape(MICRO, owners * ROW_DEV).astype(jnp.int32)
    item_draw = jax.random.randint(sub_keys[4], clusters.shape, 0, ITEMS).astype(jnp.int32)
    return (clusters, item_draw)


def table_draw(key):
    sub_keys = jax.random.split(jax.random.fold_in(key, 22), 3)
    base_draw = jax.random.truncated_normal(sub_keys[0], -5.0, 5.0, (CLUSTERS, HEAD_WIDTH), jnp.float32)
    pair_scale = jnp.exp(jax.random.uniform(sub_keys[2], (CLUSTERS // 2, 1), jnp.float32, 0.0, math.log(10.0)))
    pair_scale = jnp.repeat(pair_scale, 2, axis=0)
    odd_rows = (jnp.arange(CLUSTERS) % 2 == 1)[:, None]
    mixed_rows = jnp.where(odd_rows, base_draw, base_draw)
    return mixed_rows * pair_scale / math.sqrt(HEAD_WIDTH)


def draw_cluster_ids(key, part):
    return routing(key)[0]


def draw_item_ids(key, part):
    return routing(key)[1]


def draw_top_table(key, part):
    return table_draw(key).astype(jnp.bfloat16)


def draw_codebook(key, part):
    key = jax.random.fold_in(key, 5)
    sub_keys = jax.random.split(key, 2)
    base_draw = jax.random.truncated_normal(sub_keys[0], -5.0, 5.0, (CLUSTERS, ITEMS, HEAD_WIDTH), jnp.float32)
    item_scale = jnp.exp(jax.random.uniform(sub_keys[1], (CLUSTERS, ITEMS, 1), jnp.float32, 0.0, math.log(10.0)))
    books = base_draw * item_scale / math.sqrt(HEAD_WIDTH)
    return books.astype(jnp.bfloat16)


def draw_saved_rows(key, part):
    key = jax.random.fold_in(key, 3)
    sub_keys = jax.random.split(key, 4)
    base_draw = jax.random.truncated_normal(sub_keys[0], -5.0, 5.0, (MICRO, ROWS, HEAD_WIDTH), jnp.float32)
    row_scale = jnp.exp(jax.random.uniform(sub_keys[1], (MICRO, ROWS, 1), jnp.float32, math.log(0.03), math.log(0.3)))
    common = 0.15 * jax.random.truncated_normal(sub_keys[3], -4.0, 4.0, (1, 1, HEAD_WIDTH), jnp.float32)
    drawn = base_draw * row_scale + common
    return drawn.astype(jnp.bfloat16)


def block_levels(stream_key, shape, cuts, smallest, top_value):
    gain, own = 1.0, jax.random.fold_in(stream_key, 6)
    for axis_at, blocks in cuts:
        draws = jnp.exp(jax.random.uniform(jax.random.fold_in(own, axis_at), (blocks,), jnp.float32, smallest / len(cuts), top_value / len(cuts)))
        gain = gain * jnp.repeat(draws, shape[axis_at] // blocks).reshape([-1 if axis == axis_at else 1 for axis in range(len(shape))])
    return gain


def length_profile(count, total, limit, skew):
    portions = [(1 << 20) // math.isqrt(rank ** skew) + 1 for rank in range(2, count + 1)]
    surplus, counts = total - limit - (count - 1), [1] * (count - 1)
    while surplus > 0:
        free = [i for i in range(count - 1) if counts[i] < limit]
        mass, left = sum([portions[i] for i in free]), surplus
        for i in free:
            more = min(limit - counts[i], max(1, left * portions[i] // mass), surplus)
            counts[i] = counts[i] + more
            surplus = surplus - more
    return np.array([limit] + counts)


def ragged_sizes(own_key, amount, total, reach, skew):
    if amount == 2:
        one = jax.random.randint(own_key, (), max(1, total - reach), min(reach, total - 1) + 1)
        return jnp.stack([one, total - one])
    tallies = jnp.asarray(length_profile(amount, total, reach, skew), jnp.int32)
    twos = (amount - 1) // 2
    giver, sink = tallies[1:1 + 2 * twos:2], tallies[2:2 + 2 * twos:2]
    room = jnp.minimum(giver - 1, reach - sink)
    passed = jax.random.randint(jax.random.fold_in(own_key, 1), (twos,), 0, 1 << 20) % (room + 1)
    tallies = tallies.at[1:1 + 2 * twos:2].set(giver - passed).at[2:2 + 2 * twos:2].set(sink + passed)
    return tallies[jax.random.permutation(jax.random.fold_in(own_key, 2), amount)]


def scatter_about(own_key, shape, spread, bound, cuts=(), held_as=jnp.bfloat16):
    factor_of = block_levels(own_key, shape, cuts, -0.22, 0.18) if cuts else 1.0
    values = jax.random.normal(own_key, shape, jnp.float32) * spread * factor_of
    return jnp.minimum(jnp.maximum(values, -bound), bound).astype(held_as)


def setup_inputs(seed: int = 0) -> dict:
    splits = jax.random.split(jax.random.key(seed), 11)
    inputs = scatter_about(splits[0], (MICRO, ROWS, D_MODEL), 1.0, 6.0, ((1, 64),))
    lengths = jax.vmap(lambda own: ragged_sizes(own, SEQS, ROW_DEV, SEQ_MOST, 2))(jax.random.split(splits[1], MICRO * N_DEV)).reshape((MICRO, N_DEV, SEQS)).astype(jnp.int32)
    expand_weight = scatter_about(splits[2], (D_MODEL, 4, D_MODEL), D_MODEL ** -0.5, 0.1875, ((2, 2),))
    mixing_weight = scatter_about(splits[3], (D_MODEL, D_MODEL), D_MODEL ** -0.5, 0.1875, ((0, 2),))
    projection = scatter_about(splits[4], (D_MODEL, HEAD_WIDTH), HEAD_WIDTH ** -0.5, 0.375)
    saved_rows = draw_saved_rows(jax.random.fold_in(splits[10], 71), 0)
    cluster_ids = draw_cluster_ids(jax.random.fold_in(splits[10], 71), 0)
    item_ids = draw_item_ids(jax.random.fold_in(splits[10], 71), 0)
    top_table = draw_top_table(jax.random.fold_in(splits[10], 71), 0)
    codebook = draw_codebook(jax.random.fold_in(splits[10], 71), 0)
    return dict(inputs=inputs, lengths=lengths, expand_weight=expand_weight, mixing_weight=mixing_weight, projection=projection, saved_rows=saved_rows, cluster_ids=cluster_ids, item_ids=item_ids, top_table=top_table, codebook=codebook)


eps = 1e-05
highest = lax.Precision.HIGHEST

def silu_grad(argument):
    logistic = jax.nn.sigmoid(argument)
    return logistic * (1.0 + argument * (1.0 - logistic))

def seg_mask(lengths_row, count):
    seg_ends = jnp.cumsum(lengths_row, dtype=jnp.int32)
    positions = jnp.arange(count, dtype=jnp.int32)
    segment = lax.optimization_barrier(jnp.sum((positions[:, None] >= seg_ends[None, :]).astype(jnp.int32), axis=1, dtype=jnp.int32))
    same_seq = segment[:, None] == segment[None, :]
    causal = positions[None, :] <= positions[:, None]
    return jnp.where(same_seq & causal, 1.0, 0.0).astype(jnp.float32)

def layer_norm(argument):
    row_mean = lax.optimization_barrier(jnp.mean(argument, axis=-1, keepdims=True))
    centered = argument - row_mean
    variance = lax.optimization_barrier(jnp.mean(centered * centered, axis=-1, keepdims=True))
    inverse = lax.rsqrt(variance + eps)
    return (centered * inverse, inverse)

def norm_back(incoming, normed, inverse):
    mean_in = lax.optimization_barrier(jnp.mean(incoming, axis=-1, keepdims=True))
    mean_dot = lax.optimization_barrier(jnp.mean(incoming * normed, axis=-1, keepdims=True))
    return (incoming - mean_in - normed * mean_dot) * inverse

def rounded(argument):
    return lax.optimization_barrier(argument.astype(jnp.bfloat16)).astype(jnp.float32)

def contract_rows(left, right):
    return lax.dot_general(left, right, (((0,), (0,)), ((), ())), preferred_element_type=jnp.float32)

def contract_cols(left, right):
    return lax.dot_general(left, right, (((1,), (1,)), ((), ())), preferred_element_type=jnp.float32)

def trunk_grads(inputs, lengths, expand_weight, mixing_weight, out_grad):
    row_count, model_width = inputs.shape
    block_count = lengths.shape[0]
    block_rows = row_count // block_count
    col_count = expand_weight.shape[2]
    head_count = col_count // HEAD_DIM
    normed, inverse = layer_norm(inputs.astype(jnp.float32))
    normed_b = normed.astype(jnp.bfloat16)
    flat_in = expand_weight.reshape(model_width, 4 * col_count)
    pre_act = jnp.dot(normed_b, flat_in, preferred_element_type=jnp.float32)
    activated = rounded(jax.nn.silu(pre_act))

    def split_heads(part):
        return part.reshape(block_count, block_rows, head_count, HEAD_DIM)
    gate_part = activated[:, :col_count]
    value_heads = split_heads(activated[:, col_count:2 * col_count])
    query_heads = split_heads(activated[:, 2 * col_count:3 * col_count])
    key_heads = split_heads(activated[:, 3 * col_count:])
    masks = jax.vmap(lambda lengths_row: seg_mask(lengths_row, block_rows))(lengths)[:, None]
    scores = jnp.einsum('bihk,bjhk->bhij', query_heads, key_heads, precision=highest)
    attention = rounded(jax.nn.silu(scores) * masks / SEQ_MOST)
    mixed_out = jnp.einsum('bhij,bjhk->bihk', attention, value_heads, precision=highest)
    out_normed, inverse_mid = layer_norm(mixed_out)
    normed_flat = out_normed.reshape(row_count, col_count)
    product = (normed_flat * gate_part).astype(jnp.bfloat16)
    grad_product = contract_cols(out_grad, mixing_weight)
    grad_mix = contract_rows(product, out_grad)
    grad_gate = grad_product * normed_flat
    grad_onorm = split_heads(grad_product * gate_part)
    grad_mixed = rounded(norm_back(grad_onorm, out_normed, inverse_mid))
    grad_attention = jnp.einsum('bihk,bjhk->bhij', grad_mixed, value_heads, precision=highest)
    grad_values = jnp.einsum('bhij,bihk->bjhk', attention, grad_mixed, precision=highest)
    grad_scores = rounded(grad_attention * silu_grad(scores) * masks / SEQ_MOST)
    grad_query = jnp.einsum('bhij,bjhk->bihk', grad_scores, key_heads, precision=highest)
    grad_keys = jnp.einsum('bhij,bihk->bjhk', grad_scores, query_heads, precision=highest)
    grad_acts = jnp.concatenate([grad_gate, grad_values.reshape(row_count, col_count), grad_query.reshape(row_count, col_count), grad_keys.reshape(row_count, col_count)], axis=1)
    grad_pre = (grad_acts * silu_grad(pre_act)).astype(jnp.bfloat16)
    grad_exp = contract_rows(normed_b, grad_pre).reshape(model_width, 4, col_count)
    grad_normed = contract_cols(grad_pre, flat_in)
    return (grad_normed, grad_exp, grad_mix, normed, inverse)

def top_grads(saved, targets, top_table):
    logits = contract_cols(saved, top_table)
    row_peak = lax.optimization_barrier(jnp.max(logits, axis=1, keepdims=True))
    top_probs = jnp.exp(logits - row_peak)
    top_probs = top_probs / lax.optimization_barrier(jnp.sum(top_probs, axis=1, keepdims=True))
    top_hits = jnp.where(jnp.arange(CLUSTERS, dtype=jnp.int32)[None, :] == targets[:, None], 1.0, 0.0)
    top_grad = (top_probs - top_hits).astype(jnp.bfloat16)
    row_top = jnp.dot(top_grad, top_table, preferred_element_type=jnp.float32)
    return (row_top, contract_rows(top_grad, saved))

def leaf_grads(saved, targets, chosen, codebook, books_grad):
    half_items = ITEMS // N_SECTION

    def leaf_step(carry, piece):
        part_rows, part_targets, part_chosen = piece
        book_rows = codebook[part_targets].astype(jnp.float32)
        rows_f = part_rows.astype(jnp.float32)
        scores = jnp.einsum('bid,bd->bi', book_rows, rows_f, precision=highest)
        row_peak = lax.optimization_barrier(jnp.max(scores, axis=1, keepdims=True))
        leaf_probs = jnp.exp(scores - row_peak)
        leaf_probs = leaf_probs / lax.optimization_barrier(jnp.sum(leaf_probs, axis=1, keepdims=True))
        leaf_hits = jnp.where(jnp.arange(ITEMS, dtype=jnp.int32)[None, :] == part_chosen[:, None], 1.0, 0.0)
        leaf_grad = rounded(leaf_probs - leaf_hits)
        leaf_back = jnp.zeros((part_rows.shape[0], HEAD_WIDTH), jnp.float32)
        for half_index in range(N_SECTION):
            low = half_index * half_items
            term = jnp.einsum('bi,bid->bd', leaf_grad[:, low:low + half_items], book_rows[:, low:low + half_items], precision=highest)
            leaf_back = leaf_back + rounded(term)
        outer = leaf_grad[:, :, None] * rows_f[:, None, :]
        return (carry.at[part_targets].add(outer), leaf_back)
    pieces = (saved.reshape(-1, ROW_DEV, HEAD_WIDTH), targets.reshape(-1, ROW_DEV), chosen.reshape(-1, ROW_DEV))
    books_grad, backs = lax.scan(leaf_step, books_grad, pieces)
    return (books_grad, backs.reshape(saved.shape[0], HEAD_WIDTH))

def reference(inputs, lengths, expand_weight, mixing_weight, projection, saved_rows, cluster_ids, item_ids, top_table, codebook):
    books_grad = jnp.zeros((CLUSTERS, ITEMS, HEAD_WIDTH), jnp.float32)
    grad_expand = jnp.zeros((D_MODEL, 4, D_MODEL), jnp.float32)
    grad_mixing = jnp.zeros((D_MODEL, D_MODEL), jnp.float32)
    grad_table = jnp.zeros((CLUSTERS, HEAD_WIDTH), jnp.float32)
    input_grads = []
    for micro_index in range(MICRO):
        saved = saved_rows[micro_index]
        targets = cluster_ids[micro_index]
        row_top, step_table = top_grads(saved, targets, top_table)
        books_grad, leaf_back = leaf_grads(saved, targets, item_ids[micro_index], codebook, books_grad)
        row_grad = (row_top + leaf_back).astype(jnp.bfloat16)
        out_grad = contract_cols(row_grad, projection).astype(jnp.bfloat16)
        grad_normed, step_expand, step_mixing, normed, inverse = trunk_grads(inputs[micro_index], lengths[micro_index], expand_weight, mixing_weight, out_grad)
        input_grads.append((out_grad.astype(jnp.float32) + norm_back(grad_normed, normed, inverse)).astype(jnp.bfloat16))
        grad_expand = grad_expand + step_expand
        grad_mixing = grad_mixing + step_mixing
        grad_table = grad_table + step_table
    return (jnp.stack(input_grads), grad_expand, grad_mixing, grad_table, books_grad.astype(jnp.bfloat16))
```

```python
import functools

import jax
import jax.numpy as jnp
from jax import lax
from jax.experimental import pallas as pl
from jax.experimental.pallas import tpu as pltpu
from jax.sharding import Mesh
from jax.sharding import PartitionSpec as P

HEAD_DIM = 128
SEQ_MOST = 64
CAP = 4
eps = 1e-05
DEV = ("y", "z", "x")
f32 = jnp.float32
bf16 = jnp.bfloat16


def swap(part):
    return lax.ppermute(part, "section", [(0, 1), (1, 0)])


def shifted(part, step):
    count = lax.axis_size("x")
    return lax.ppermute(part, "x", [(i, (i + step) % count) for i in range(count)])


def silu_grad(argument):
    logistic = jax.nn.sigmoid(argument)
    return logistic * (1.0 + argument * (1.0 - logistic))


def seg_mask(lengths_row, count):
    seg_ends = jnp.cumsum(lengths_row, dtype=jnp.int32)
    positions = jnp.arange(count, dtype=jnp.int32)
    segment = jnp.sum(
        (positions[:, None] >= seg_ends[None, :]).astype(jnp.int32), axis=1, dtype=jnp.int32
    )
    same_seq = segment[:, None] == segment[None, :]
    causal = positions[None, :] <= positions[:, None]
    return jnp.where(same_seq & causal, 1.0, 0.0).astype(f32)


def layer_norm(argument):
    row_mean = jnp.mean(argument, axis=-1, keepdims=True)
    centered = argument - row_mean
    variance = jnp.mean(centered * centered, axis=-1, keepdims=True)
    inverse = lax.rsqrt(variance + eps)
    return (centered * inverse, inverse)


def norm_back(incoming, normed, inverse):
    mean_in = jnp.mean(incoming, axis=-1, keepdims=True)
    mean_dot = jnp.mean(incoming * normed, axis=-1, keepdims=True)
    return (incoming - mean_in - normed * mean_dot) * inverse


def dot(left, right, dims):
    return lax.dot_general(left, right, (dims, ((), ())), preferred_element_type=f32)


NN = ((1,), (0,))
NT = ((1,), (1,))
TN = ((0,), (0,))


def leaf_scores_kernel(group, got_ref, book_ref, out_ref, stat_ref):
    step = pl.program_id(0)
    width = book_ref.shape[2]

    @pl.when(step == 0)
    def _():
        out_ref[...] = jnp.zeros_like(out_ref)

    rows = got_ref[:, :width]
    codes = got_ref[:, width : width + 1].astype(f32)
    total = out_ref[...]
    for k in range(group):
        mine = codes == (step * group + k + 1).astype(f32)
        total += dot(jnp.where(mine, rows, jnp.zeros_like(rows)), book_ref[k], NT)
    out_ref[...] = total

    @pl.when(step == pl.num_programs(0) - 1)
    def _():
        peak = jnp.max(total, axis=1, keepdims=True)
        mass = jnp.sum(jnp.exp(total - peak), axis=1, keepdims=True)
        lane = lax.broadcasted_iota(jnp.int32, stat_ref.shape, 1)
        stat_ref[...] = jnp.where(lane == 0, peak, mass)


def leaf_back_kernel(group, sec_ref, got_ref, score_ref, mine_ref, other_ref, book_ref, back_ref, grad_ref, total_ref):
    step = pl.program_id(0)
    width = book_ref.shape[2]
    codes = got_ref[:, width : width + 1].astype(f32)

    @pl.when(step == 0)
    def _():
        high = got_ref[:, width + 1 : width + 2].astype(f32)
        low = got_ref[:, width + 2 : width + 3].astype(jnp.int32)
        peak_a, mass_a = mine_ref[:, 0:1], mine_ref[:, 1:2]
        peak_b, mass_b = other_ref[:, 0:1], other_ref[:, 1:2]
        peak = jnp.maximum(peak_a, peak_b)
        mass = mass_a * jnp.exp(peak_a - peak) + mass_b * jnp.exp(peak_b - peak)
        probs = jnp.exp(score_ref[...] - peak) / mass
        item = lax.broadcasted_iota(jnp.int32, probs.shape, 1)
        hit = (item == low) & (high == sec_ref[0].astype(f32))
        grad = jnp.where(codes > 0, probs - jnp.where(hit, 1.0, 0.0), 0.0)
        grad_ref[...] = grad.astype(bf16)
        total_ref[...] = jnp.zeros_like(total_ref)

    grads = grad_ref[...]
    total = total_ref[...]
    for k in range(group):
        mine = codes == (step * group + k + 1).astype(f32)
        total += dot(jnp.where(mine, grads, jnp.zeros_like(grads)), book_ref[k], NN)
    total_ref[...] = total

    @pl.when(step == pl.num_programs(0) - 1)
    def _():
        back_ref[...] = total.astype(bf16)


def leaf_book_kernel(group, got_ref, grad_ref, out_ref, turned_ref):
    step = pl.program_id(0)
    width = out_ref.shape[2]

    @pl.when(step == 0)
    def _():
        turned_ref[...] = grad_ref[...].astype(f32).T.astype(bf16)

    rows = got_ref[:, :width]
    codes = got_ref[:, width : width + 1].astype(f32)
    for k in range(group):
        mine = codes == (step * group + k + 1).astype(f32)
        out_ref[k] = dot(turned_ref[...], jnp.where(mine, rows, jnp.zeros_like(rows)), NN).astype(bf16)


def whole(shape):
    return pl.BlockSpec(shape, lambda i: (0,) * len(shape))


def params():
    return pltpu.CompilerParams(dimension_semantics=("arbitrary",), vmem_limit_bytes=40 * 2**20)


def leaf_scores(got, book):
    books, items, width = book.shape
    slots = got.shape[0]
    group = 8
    return pl.pallas_call(
        functools.partial(leaf_scores_kernel, group),
        grid=(books // group,),
        in_specs=[whole(got.shape), pl.BlockSpec((group, items, width), lambda i: (i, 0, 0))],
        out_specs=[whole((slots, items)), whole((slots, 128))],
        out_shape=[jax.ShapeDtypeStruct((slots, items), f32), jax.ShapeDtypeStruct((slots, 128), f32)],
        compiler_params=params(),
        cost_estimate=pl.CostEstimate(flops=2 * slots * books * items * width, bytes_accessed=books * items * width * 2, transcendentals=0),
        name="leaf_scores",
    )(got, book)


def leaf_back(section, got, scores, mine, other, book):
    books, items, width = book.shape
    slots = got.shape[0]
    group = 8
    return pl.pallas_call(
        functools.partial(leaf_back_kernel, group),
        grid=(books // group,),
        in_specs=[
            pl.BlockSpec(memory_space=pltpu.SMEM),
            whole(got.shape),
            whole(scores.shape),
            whole(mine.shape),
            whole(other.shape),
            pl.BlockSpec((group, items, width), lambda i: (i, 0, 0)),
        ],
        out_specs=[whole((slots, width)), whole((slots, items))],
        out_shape=[jax.ShapeDtypeStruct((slots, width), bf16), jax.ShapeDtypeStruct((slots, items), bf16)],
        scratch_shapes=[pltpu.VMEM((slots, width), f32)],
        compiler_params=params(),
        cost_estimate=pl.CostEstimate(flops=2 * slots * books * items * width, bytes_accessed=books * items * width * 2, transcendentals=0),
        name="leaf_back",
    )(section, got, scores, mine, other, book)


def leaf_book(got, grads, books, width):
    slots, items = grads.shape
    group = 8
    return pl.pallas_call(
        functools.partial(leaf_book_kernel, group),
        grid=(books // group,),
        in_specs=[whole(got.shape), whole(grads.shape)],
        out_specs=pl.BlockSpec((group, items, width), lambda i: (i, 0, 0)),
        out_shape=jax.ShapeDtypeStruct((books, items, width), bf16),
        scratch_shapes=[pltpu.VMEM((items, slots), bf16)],
        compiler_params=params(),
        cost_estimate=pl.CostEstimate(flops=2 * slots * books * items * width, bytes_accessed=books * items * width * 2, transcendentals=0),
        name="leaf_book",
    )(got, grads)


def body(
    inputs,
    lengths,
    expand_weight,
    mixing_weight,
    projection,
    saved_rows,
    cluster_ids,
    item_ids,
    top_table,
    codebook,
):
    micro_count, row_count, model_width = inputs.shape
    total_rows = micro_count * row_count
    owners = lax.axis_size(DEV)
    group = lax.axis_size("x")
    section = lax.axis_index("section")
    my_x = lax.axis_index("x")
    half_clusters, head_width = top_table.shape
    local_books, half_items, _ = codebook.shape
    col_count = expand_weight.shape[2]
    head_count = col_count // HEAD_DIM
    slot_each = micro_count * CAP
    slot_count = owners * slot_each

    owner_ids = cluster_ids // local_books
    marks = (owner_ids[:, :, None] == jnp.arange(owners, dtype=jnp.int32)).astype(bf16)
    place = jnp.arange(row_count, dtype=jnp.int32)
    before = (place[None, :] < place[:, None]).astype(bf16)
    earlier = jnp.einsum("ij,mjo->mio", before, marks, preferred_element_type=f32)
    rank = jnp.sum(earlier * marks.astype(f32), axis=2).astype(jnp.int32)
    slot_ids = owner_ids * slot_each + jnp.arange(micro_count, dtype=jnp.int32)[:, None] * CAP + rank
    slot_ids = slot_ids.reshape(total_rows)
    saved = saved_rows.reshape(total_rows, head_width)
    targets = cluster_ids.reshape(total_rows)
    chosen = item_ids.reshape(total_rows)
    lane = jnp.arange(128, dtype=jnp.int32)[None, :]
    codes = jnp.where(
        lane == 0,
        (targets % local_books + 1)[:, None],
        jnp.where(lane == 1, (chosen // half_items)[:, None], jnp.where(lane == 2, (chosen % half_items)[:, None], 0)),
    )
    extended = jnp.concatenate([saved, codes.astype(bf16)], axis=1)
    pick = (slot_ids[:, None] == jnp.arange(slot_count, dtype=jnp.int32)[None, :]).astype(bf16)
    sent = dot(pick, extended, TN).astype(bf16)
    got = lax.all_to_all(sent.reshape(owners, slot_each, -1), DEV, 0, 0, tiled=True).reshape(slot_count, -1)

    logits = dot(saved, top_table, NT)
    peak = jnp.max(logits, axis=1, keepdims=True)
    mass = jnp.sum(jnp.exp(logits - peak), axis=1, keepdims=True)
    peak_b, mass_b = swap((peak, mass))
    both = jnp.maximum(peak, peak_b)
    mass = mass * jnp.exp(peak - both) + mass_b * jnp.exp(peak_b - both)
    hits = jnp.arange(half_clusters, dtype=jnp.int32)[None, :] + section * half_clusters == targets[:, None]
    top_grad = (jnp.exp(logits - both) / mass - jnp.where(hits, 1.0, 0.0)).astype(bf16)
    row_top = dot(top_grad, top_table, NN)
    table_part = dot(top_grad, saved, TN).astype(bf16)

    flat_inputs = inputs.reshape(total_rows, model_width)
    normed, inverse = layer_norm(flat_inputs.astype(f32))
    normed_b = normed.astype(bf16)
    normed_all = [normed_b] + [shifted(normed_b, s) for s in range(1, group)]
    flat_in = expand_weight.reshape(model_width, 4 * col_count)
    pre_act = dot(normed_b, flat_in, NN)
    activated = jax.nn.silu(pre_act).astype(bf16)
    gate_part = activated[:, :col_count].astype(f32)

    def heads(part):
        return part.reshape(micro_count, row_count, head_count, HEAD_DIM)

    value_heads = heads(activated[:, col_count : 2 * col_count])
    query_heads = heads(activated[:, 2 * col_count : 3 * col_count])
    key_heads = heads(activated[:, 3 * col_count :])
    seq_mask = jax.vmap(lambda one: seg_mask(one, row_count))(lengths[:, 0])[:, None]

    def ein(spec, left, right):
        return jnp.einsum(spec, left, right, preferred_element_type=f32)

    scores = ein("mihk,mjhk->mhij", query_heads, key_heads)
    attention = (jax.nn.silu(scores) * seq_mask / SEQ_MOST).astype(bf16)
    mixed_out = ein("mhij,mjhk->mihk", attention, value_heads)
    out_normed, inverse_mid = layer_norm(mixed_out)
    normed_flat = out_normed.reshape(total_rows, col_count)
    product = (normed_flat * gate_part).astype(bf16)
    product_all = [product] + [shifted(product, s) for s in range(1, group)]

    leaf, stats = leaf_scores(got, codebook)
    back, leaf_grad = leaf_back(section.reshape(1), got, leaf, stats, swap(stats), codebook)
    returned = lax.all_to_all(back.reshape(owners, slot_each, head_width), DEV, 0, 0, tiled=True)
    book_grads = leaf_book(got, leaf_grad, local_books, head_width)

    row_part = row_top + dot(pick, returned.reshape(slot_count, head_width), NN)
    row_grad = (row_part + swap(row_part)).astype(bf16)
    out_grad = dot(row_grad, projection, NT).astype(bf16)
    turned = projection.reshape(owners, group, -1, head_width).swapaxes(0, 1).reshape(group, -1, head_width)
    out_turned = jnp.einsum("rd,gcd->grc", row_grad, turned, preferred_element_type=f32).astype(bf16)

    def exchange(parts):
        pieces = [lax.dynamic_index_in_dim(parts, my_x, 0, False)]
        for s in range(1, group):
            piece = lax.dynamic_index_in_dim(parts, (my_x + s) % group, 0, False)
            pieces.append(shifted(piece, s))
        return pieces

    out_pieces = exchange(out_turned)

    grad_product = dot(out_grad, mixing_weight, NT)
    grad_gate = grad_product * normed_flat
    grad_onorm = heads(grad_product * gate_part)
    grad_mixed = norm_back(grad_onorm, out_normed, inverse_mid).astype(bf16)
    grad_attention = ein("mihk,mjhk->mhij", grad_mixed, value_heads)
    grad_values = ein("mhij,mihk->mjhk", attention, grad_mixed)
    grad_scores = (grad_attention * silu_grad(scores) * seq_mask / SEQ_MOST).astype(bf16)
    grad_query = ein("mhij,mjhk->mihk", grad_scores, key_heads)
    grad_keys = ein("mhij,mihk->mjhk", grad_scores, query_heads)
    acts = [grad_gate, grad_values, grad_query, grad_keys]
    slope = silu_grad(pre_act)
    grad_pre = jnp.stack(
        [
            (part.reshape(total_rows, col_count) * slope[:, i * col_count : (i + 1) * col_count]).astype(bf16)
            for i, part in enumerate(acts)
        ]
    )
    pre_pieces = exchange(grad_pre)
    grad_part = sum(dot(grad_pre[i], expand_weight[:, i], NT) for i in range(4))
    grad_normed = grad_part + swap(grad_part)
    grad_inputs = (out_grad.astype(f32) + norm_back(grad_normed, normed, inverse)).astype(bf16)

    expand_part = sum(dot(a, b, TN) for a, b in zip(normed_all, pre_pieces)).astype(bf16)
    mixing_part = sum(dot(b, a, TN) for a, b in zip(product_all, out_pieces)).astype(bf16)
    sizes = [model_width // owners, mixing_part.shape[0] // owners, half_clusters * head_width // col_count // owners]
    packed = jnp.concatenate(
        [part.reshape(owners, size, col_count) for part, size in zip((expand_part, mixing_part, table_part), sizes)], axis=1
    )
    arrived = lax.all_to_all(packed, DEV, 0, 0, tiled=True)
    arrived = arrived.astype(f32).reshape(owners // group, group, -1, col_count)
    first, second = sizes[0], sizes[0] + sizes[1]
    weights = jnp.sum(arrived[:, :, :second], axis=0)
    share_expand = weights[:, :first].swapaxes(0, 1)
    share_mixing = weights[:, first:].reshape(-1, col_count).T
    share_table = jnp.sum(arrived[:, :, second:], axis=(0, 1)).reshape(-1, head_width)
    return (
        grad_inputs.reshape(inputs.shape),
        share_expand,
        share_mixing,
        share_table,
        book_grads,
    )


def solution(mesh):
    grid = Mesh(mesh.devices.reshape(2, 4, 4, 4), ("section",) + DEV)
    return jax.shard_map(
        body,
        mesh=grid,
        in_specs=(
            P(None, DEV, None),
            P(None, DEV, None),
            P(None, None, "section"),
            P("section", None),
            P(),
            P(None, DEV, None),
            P(None, DEV),
            P(None, DEV),
            P("section", None),
            P(DEV, "section", None),
        ),
        out_specs=(
            P(None, DEV, None),
            P(DEV, None, "section"),
            P("section", DEV),
            P(("section",) + DEV, None),
            P(DEV, "section", None),
        ),
        check_vma=False,
    )
```

```python
import functools

import jax
import jax.numpy as jnp
from jax import lax
from jax.experimental import pallas as pl
from jax.experimental.pallas import tpu as pltpu
from jax.sharding import Mesh
from jax.sharding import PartitionSpec as P

HEAD_DIM = 128
SEQ_MOST = 64
SEQS = 4
CAP = 4
eps = 1e-05
DEV = ("y", "z", "x")
f32 = jnp.float32
bf16 = jnp.bfloat16
NN = ((1,), (0,))
NT = ((1,), (1,))
TN = ((0,), (0,))


def swap(part):
    return lax.ppermute(part, "section", [(0, 1), (1, 0)])


def shifted(part, axis, step):
    count = lax.axis_size(axis)
    return lax.ppermute(part, axis, [(i, (i + step) % count) for i in range(count)])


def member():
    return lax.rem(lax.axis_index("x"), 2) + 2 * lax.rem(lax.axis_index("y"), 2)


def from_member(part, other):
    count = lax.axis_size("x")
    flip = count * (other // 2) + other % 2
    return lax.ppermute(part, ("y", "x"), [(i, i ^ flip) for i in range(lax.axis_size("y") * count)])


def dot(left, right, dims):
    return lax.dot_general(left, right, (dims, ((), ())), preferred_element_type=f32)


def iota(shape, dim):
    return lax.broadcasted_iota(jnp.int32, shape, dim)


def row_norm(argument):
    row_mean = jnp.mean(argument, axis=-1, keepdims=True)
    centered = argument - row_mean
    variance = jnp.mean(centered * centered, axis=-1, keepdims=True)
    inverse = lax.rsqrt(variance + eps)
    return (centered * inverse, inverse)


def norm_back(incoming, normed, inverse):
    mean_in = jnp.mean(incoming, axis=-1, keepdims=True)
    mean_dot = jnp.mean(incoming * normed, axis=-1, keepdims=True)
    return (incoming - mean_in - normed * mean_dot) * inverse


def call(kernel, name, outs, args, kinds, after=(), scratch=(), limit=56, flops=0, token=False):
    in_kinds, out_kinds = kinds.split()
    if token:
        outs, out_kinds = [*outs, ((8, 128), f32)], out_kinds + "V"
    assert len(in_kinds) == len(args) and len(out_kinds) == len(outs), name
    spaces = {"V": pltpu.VMEM, "S": pltpu.SMEM, "H": pl.ANY, "R": pl.ANY}
    held = [pltpu.VMEM(a.shape, a.dtype) for a, k in zip(args, in_kinds) if k == "H"]
    held += [pltpu.VMEM(s, d) for (s, d), k in zip(outs, out_kinds) if k == "H"]
    sems = [pltpu.SemaphoreType.DMA((len(held),))] if held else []

    def run(*refs):
        ins = list(refs[: len(args)])
        refs = refs[len(args) + len(after) :]
        results = list(refs[: len(outs)])
        buffers = list(refs[len(outs) : len(outs) + len(held)])
        rest = refs[len(outs) + len(held) + len(sems) :]
        sem = refs[len(outs) + len(held)] if held else None
        count = 0
        first, last = [], []
        for i, kind in enumerate(in_kinds):
            if kind == "H":
                first.append(pltpu.make_async_copy(ins[i], buffers[count], sem.at[count]))
                first[-1].start()
                ins[i] = buffers[count]
                count += 1
        for i, kind in enumerate(out_kinds):
            if kind == "H":
                last.append(pltpu.make_async_copy(buffers[count], results[i], sem.at[count]))
                results[i] = buffers[count]
                count += 1
        for copy in first:
            copy.wait()
        if token:
            results.pop()[...] = jnp.zeros((8, 128), f32)
        kernel(*ins, *results, *rest)
        for copy in last:
            copy.start()
        for copy in last:
            copy.wait()

    return pl.pallas_call(
        run,
        in_specs=[pl.BlockSpec(memory_space=spaces[k]) for k in in_kinds] + [pl.BlockSpec(memory_space=pl.ANY)] * len(after),
        out_specs=[pl.BlockSpec(memory_space=spaces[k]) for k in out_kinds],
        out_shape=[jax.ShapeDtypeStruct(s, d) for s, d in outs],
        scratch_shapes=held + sems + list(scratch),
        compiler_params=pltpu.CompilerParams(vmem_limit_bytes=limit * 2**20),
        cost_estimate=pl.CostEstimate(flops=flops, bytes_accessed=0, transcendentals=0),
        name=name,
    )(*args, *after)


def one_hot(slots_row, count):
    return jnp.where(iota((count, slots_row.shape[1]), 0) == slots_row, 1.0, 0.0).astype(bf16)


def dispatch_kernel(owners, books, half, cluster_ref, item_ref, saved_ref, sent_ref, slot_ref, mark_ref):
    micro, rows = cluster_ref.shape
    width = saved_ref.shape[2]
    each = micro * CAP
    before = jnp.where(iota((rows, rows), 0) < iota((rows, rows), 1), 1.0, 0.0).astype(bf16)
    same = jnp.where(iota((rows, rows), 0) == iota((rows, rows), 1), 1.0, 0.0).astype(bf16)
    kind = iota((128, rows), 0)
    rows_out, codes_out = 0.0, 0.0
    for m in range(micro):
        target, item = cluster_ref[m : m + 1], item_ref[m : m + 1]
        owner, local = target // books, target % books
        marks = jnp.where(iota((owners, rows), 0) == owner, 1.0, 0.0)
        earlier = dot(marks.astype(bf16), before, NN)
        rank = jnp.sum(earlier * marks, axis=0, keepdims=True).astype(jnp.int32)
        slot = owner * each + m * CAP + rank
        slot_ref[m : m + 1] = slot
        code = jnp.where(
            kind == 0,
            local + 1,
            jnp.where(kind == 1, item // half, jnp.where(kind == 2, item % half, jnp.where(kind == 3, owner, 0))),
        )
        code = code.astype(f32).astype(bf16)
        pick = one_hot(slot, owners * each)
        rows_out += dot(pick, saved_ref[m], NN)
        codes_out += dot(pick, code, NT)
        turned = dot(same, code, NT)
        mark_ref[m * rows : (m + 1) * rows] = jnp.broadcast_to(
            turned[:, 3:4] * books + turned[:, 0:1] - 1.0, (rows, 128)
        )
    sent_ref[:, :width] = rows_out.astype(bf16)
    sent_ref[:, width:] = codes_out.astype(bf16)


def top_logits_kernel(saved_ref, table_ref, logit_ref, stat_ref):
    logits = dot(saved_ref[...], table_ref[...], NT)
    logit_ref[...] = logits
    peak = jnp.max(logits, axis=1, keepdims=True)
    mass = jnp.sum(jnp.exp(logits - peak), axis=1, keepdims=True)
    stat_ref[...] = jnp.where(iota(stat_ref.shape, 1) == 0, peak, mass)


def joined(mine_ref, other_ref):
    peak_a, mass_a = mine_ref[:, 0:1], mine_ref[:, 1:2]
    peak_b, mass_b = other_ref[:, 0:1], other_ref[:, 1:2]
    peak = jnp.maximum(peak_a, peak_b)
    return peak, mass_a * jnp.exp(peak_a - peak) + mass_b * jnp.exp(peak_b - peak)


def top_grad_kernel(group, own, logit_ref, mine_ref, other_ref, mark_ref, table_ref, saved_ref, *out_refs):
    row_ref, grad_refs = out_refs[0], out_refs[1:]
    half = table_ref.shape[0]
    quarter = half // group
    piece = own // group
    base = lax.axis_index("section") * half
    me = lax.axis_index("z")
    peak, mass = joined(mine_ref, other_ref)
    target = mark_ref[:, 0:1].astype(jnp.int32) - base
    total = 0.0
    column = iota((mark_ref.shape[0], quarter), 1)
    for q in range(group):
        index = (column // piece) * own + q * piece + column % piece
        cols = pl.ds(q * quarter, quarter)
        probs = jnp.exp(logit_ref[:, cols] - peak) / mass
        grad = (probs - jnp.where(index == target, 1.0, 0.0)).astype(bf16)
        total += dot(grad, table_ref[cols, :], NN)
        for s in range(group):

            @pl.when(lax.rem(me + s, group) == q)
            def _(s=s, grad=grad):
                grad_refs[s][:, :quarter] = grad
                grad_refs[s][:, quarter:] = saved_ref[...]

    row_ref[...] = total


def table_kernel(owners, *refs):
    *in_refs, out_ref = refs
    quarter = in_refs[0].shape[1] - 256
    total = sum(dot(r[:, :quarter], r[:, quarter:], TN) for r in in_refs)
    left = total[:, :128].reshape(owners, -1, 128)
    right = total[:, 128:].reshape(owners, -1, 128)
    out_ref[...] = jnp.concatenate([left, right], axis=1).astype(bf16)


def masked_product(code_ref, left_ref, width, book_ref, out_ref, dims, group, ready):
    lines = 256
    out_ref[...] = jnp.zeros_like(out_ref)

    def step(i, carry):
        ready(i)
        books = book_ref[pl.ds(i * group, group)]
        if dims == NT:
            right = jnp.concatenate([books[k] for k in range(group)], axis=1)
        else:
            right = books.reshape(-1, books.shape[2])
        for r in range(0, out_ref.shape[0], lines):
            some = pl.ds(r, lines)
            left, code = left_ref[some, :width], code_ref[some, :]
            parts = []
            for k in range(group):
                here = code == (i * group + k + 1).astype(f32).astype(bf16)
                parts.append(jnp.where(here, left, jnp.zeros_like(left)))
            out_ref[some, :] += dot(jnp.concatenate(parts, axis=1), right, dims)
        return carry

    lax.fori_loop(0, book_ref.shape[0] // group, step, 0)


GROUP_LIMIT = 40
BOOK_GROUP = 16
BOOK_COPIES = 4


def leaf_scores_kernel(got_in, book_in, out_ref, stat_ref, got_ref, book_ref, code_ref, got_sem, sem):
    width = book_ref.shape[2]
    steps = book_ref.shape[0] // BOOK_GROUP
    piece = BOOK_GROUP // BOOK_COPIES

    def copies(i):
        for j in range(BOOK_COPIES):
            some = pl.ds(i * BOOK_GROUP + j * piece, piece)
            yield pltpu.make_async_copy(book_in.at[some], book_ref.at[some], sem.at[i, j])

    got_copy = pltpu.make_async_copy(got_in, got_ref, got_sem)
    got_copy.start()
    for i in range(2):
        for copy in copies(i):
            copy.start()
    got_copy.wait()
    code_ref[...] = jnp.broadcast_to(got_ref[:, width : width + 1], code_ref.shape)

    def ready(i):
        for copy in copies(i):
            copy.wait()

        @pl.when(i + 2 < steps)
        def _():
            for copy in copies(i + 2):
                copy.start()

    masked_product(code_ref, got_ref, width, book_ref, out_ref, NT, BOOK_GROUP, ready)
    scores = out_ref[...]
    peak = jnp.max(scores, axis=1, keepdims=True)
    mass = jnp.sum(jnp.exp(scores - peak), axis=1, keepdims=True)
    stat_ref[...] = jnp.where(iota(stat_ref.shape, 1) == 0, peak, mass)


def leaf_back_kernel(got_ref, score_ref, mine_ref, other_ref, book_ref, back_ref, grad_ref, code_ref, total_ref):
    items, width = book_ref.shape[1:]
    code = got_ref[:, width : width + 1]
    code_ref[...] = jnp.broadcast_to(code, code_ref.shape)
    high = got_ref[:, width + 1 : width + 2].astype(f32).astype(jnp.int32)
    low = got_ref[:, width + 2 : width + 3].astype(f32).astype(jnp.int32)
    peak, mass = joined(mine_ref, other_ref)
    probs = jnp.exp(score_ref[...] - peak) / mass
    hit = (iota(probs.shape, 1) == low) & (high == lax.axis_index("section"))
    grad = jnp.where(code.astype(f32) > 0, probs - jnp.where(hit, 1.0, 0.0), 0.0)
    grad_ref[...] = grad.astype(bf16)
    masked_product(code_ref, grad_ref, items, book_ref, total_ref, NN, 32, lambda i: None)
    back_ref[...] = total_ref[...].astype(bf16)


def leaf_book_kernel(got_ref, grad_ref, out_ref, code_ref, turned_ref, held_ref, sem):
    books, items, width = out_ref.shape
    group = books // sem.shape[0]
    slots = got_ref.shape[0]
    turned_ref[...] = grad_ref[...].astype(f32).T.astype(bf16)
    code_ref[...] = jnp.broadcast_to(got_ref[:, width : width + 1].astype(f32), (slots, items)).T.astype(bf16)
    rows = got_ref[:, :width]
    copies = []
    for i in range(books // group):
        some = pl.ds(i * group, group)
        turned, code = turned_ref[...], code_ref[...]
        parts = []
        for k in range(group):
            here = code == (i * group + k + 1)
            parts.append(jnp.where(here, turned, jnp.zeros_like(turned)))
        grads = dot(jnp.concatenate(parts, axis=0), rows, NN)
        held_ref[some] = grads.reshape(group, items, width).astype(bf16)
        copies.append(pltpu.make_async_copy(held_ref.at[some], out_ref.at[some], sem.at[i]))
        copies[-1].start()
    for copy in copies:
        copy.wait()


def leaf_scores(got, book, after):
    books, items, width = book.shape
    slots = got.shape[0]
    return call(
        leaf_scores_kernel,
        "leaf_scores",
        [((slots, items), f32), ((slots, 128), f32), (got.shape, bf16), (book.shape, bf16)],
        (got, book),
        "RR VVVV", limit=42,
        flops=2 * slots * books * items * width,
        scratch=[
            pltpu.VMEM((slots, width), bf16),
            pltpu.SemaphoreType.DMA,
            pltpu.SemaphoreType.DMA((books // BOOK_GROUP, BOOK_COPIES)),
        ],
        after=after,
    )


def leaf_back(got, scores, mine, other, book, after):
    books, items, width = book.shape
    slots = got.shape[0]
    return call(
        leaf_back_kernel,
        "leaf_back",
        [((slots, width), bf16), ((slots, items), bf16)],
        (got, scores, mine, other, book),
        "VVVVV HH",
        limit=28,
        scratch=[pltpu.VMEM((slots, items), bf16), pltpu.VMEM((slots, width), f32)],
        after=after,
    )


def leaf_book(got, grads, books, width, after):
    slots, items = grads.shape
    group = 4
    return call(
        leaf_book_kernel,
        "leaf_book",
        [((books, items, width), bf16)],
        (got, grads),
        "HH R",
        scratch=[
            pltpu.VMEM((items, slots), bf16),
            pltpu.VMEM((items, slots), bf16),
            pltpu.VMEM((books, items, width), bf16),
            pltpu.SemaphoreType.DMA((books // group,)),
        ],
        after=after,
    )[0]


def slope_of(argument, logistic):
    return logistic * (1.0 + argument * (1.0 - logistic))


def norms_kernel(length_ref, input_ref, out_ref):
    micro, rows, width = input_ref.shape
    for m in range(micro):
        out_ref[m * rows : (m + 1) * rows] = row_norm(input_ref[m].astype(f32))[0].astype(bf16)
    seqs = length_ref.shape[2]
    lane = iota((16, width), 1)
    held = jnp.zeros((16, width), f32)
    for m in range(micro):
        for i in range(seqs):
            held = jnp.where(lane == m * seqs + i, length_ref[m, 0, i].astype(f32), held)
    out_ref[micro * rows :] = held.astype(bf16)


def seq_mask(sizes, rows):
    row, col = iota((rows, rows), 0), iota((rows, rows), 1)
    row_seg, col_seg, end = 0, 0, 0
    for size in sizes:
        end = end + size
        row_seg += jnp.where(row >= end, 1, 0)
        col_seg += jnp.where(col >= end, 1, 0)
    return jnp.where((row_seg == col_seg) & (col <= row), 1.0 / SEQ_MOST, 0.0)


def held_sizes(held, m):
    held = held.astype(f32)[0:1].astype(jnp.int32)
    return [held[:, m * SEQS + i : m * SEQS + i + 1] for i in range(SEQS)]


def attend_all(acts, masks):
    scores = [dot(query, key, NT) for _, _, query, key in acts]
    logistics = [jax.nn.sigmoid(score) for score in scores]
    attention = [(a * b * mask).astype(bf16) for a, b, mask in zip(scores, logistics, masks)]
    mixed = [dot(a, act[1], NN) for a, act in zip(attention, acts)]
    back = [slope_of(a, b) * mask for a, b, mask in zip(scores, logistics, masks)]
    normed = [row_norm(one) for one in mixed]
    return [(a, b, n, jnp.broadcast_to(i, n.shape)) for a, b, (n, i) in zip(attention, back, normed)]


def my_head():
    return pl.ds(pl.multiple_of(member() * HEAD_DIM, HEAD_DIM), HEAD_DIM)


def group_forward_kernel(*refs):
    *norm_ins, weight_in, act_ref, slope_ref, att_ref, back_ref, out_ref, inverse_ref, prod_ref = refs[:-3]
    weight_ref, norm_ref, sem = refs[-3:]
    pairs = [(weight_in.at[:, :, my_head()], weight_ref)] + [(one, norm_ref.at[s]) for s, one in enumerate(norm_ins)]
    copies = [pltpu.make_async_copy(a, b, sem.at[i]) for i, (a, b) in enumerate(pairs)]
    for copy in copies:
        copy.start()
    for copy in copies:
        copy.wait()
    rows = att_ref.shape[1]
    total = out_ref.shape[0] // len(norm_ins)
    weight = jnp.concatenate([weight_ref[t] for t in range(4)], axis=1)
    acts, masks, spans = [], [], []
    for s in range(len(norm_ins)):
        for m in range(total // rows):
            lines = pl.ds(s * total + m * rows, rows)
            pre_act = dot(norm_ref[s, m * rows : (m + 1) * rows, :], weight, NN)
            logistic = jax.nn.sigmoid(pre_act)
            act = (pre_act * logistic).astype(bf16)
            act_ref[lines, :] = act
            slope_ref[lines, :] = slope_of(pre_act, logistic)
            spans.append(lines)
            masks.append(seq_mask(held_sizes(norm_ref[s, total:, :128], m), rows))
            acts.append([act[:, t * HEAD_DIM : (t + 1) * HEAD_DIM] for t in range(4)])
    for lines, act, result in zip(spans, acts, attend_all(acts, masks)):
        att_ref[lines, :], back_ref[lines, :], out_ref[lines, :], inverse_ref[lines, :] = result
        prod_ref[lines, :] = (result[2] * act[0].astype(f32)).astype(bf16)


def attend_back_all(incoming, acts, results):
    mixed = [
        norm_back(a * act[0].astype(f32), normed, inverse).astype(bf16)
        for a, act, (_, _, normed, inverse) in zip(incoming, acts, results)
    ]
    grads = [dot(a, act[1], NT) for a, act in zip(mixed, acts)]
    values = [dot(result[0], a, TN) for result, a in zip(results, mixed)]
    grads = [(a * result[1]).astype(bf16) for a, result in zip(grads, results)]
    queries = [dot(a, act[3], NN) for a, act in zip(grads, acts)]
    keys = [dot(a, act[2], TN) for a, act in zip(grads, acts)]
    gates = [a * result[2] for a, result in zip(incoming, results)]
    return list(zip(gates, values, queries, keys))


def rows_kernel(slot_ref, returned_ref, top_ref, out_ref):
    micro, rows = slot_ref.shape
    for m in range(micro):
        lines = pl.ds(m * rows, rows)
        pick = one_hot(slot_ref[m : m + 1], returned_ref.shape[0])
        out_ref[lines, :] = top_ref[lines, :] + dot(pick, returned_ref[...], TN)


def add_kernel(mine_ref, other_ref, out_ref):
    out_ref[...] = (mine_ref[...] + other_ref[...]).astype(bf16)


def trunk_kernel(length_ref, norm_ref, row_ref, proj_ref, mix_ref, weight_in, og_ref, part_ref, pre_ref, weight_ref, sem):
    copies = [pltpu.make_async_copy(weight_in.at[t], weight_ref.at[t], sem.at[t]) for t in range(4)]
    for copy in copies:
        copy.start()
    rows = HEAD_DIM
    total, cols = row_ref.shape[0], weight_ref.shape[2]
    out_grad = dot(row_ref[...], proj_ref[...], NT).astype(bf16)
    og_ref[...] = out_grad
    grad_product = dot(out_grad, mix_ref[...], NT)
    for copy in copies:
        copy.wait()
    for m in range(total // rows):
        lines = pl.ds(m * rows, rows)
        normed = norm_ref[lines, :]
        acts, slopes = [], []
        for t in range(4):
            pre_act = dot(normed, weight_ref[t], NN)
            logistic = jax.nn.sigmoid(pre_act)
            acts.append((pre_act * logistic).astype(bf16))
            slopes.append(slope_of(pre_act, logistic))
        heads = [slice(h * HEAD_DIM, (h + 1) * HEAD_DIM) for h in range(cols // HEAD_DIM)]
        acts = [[act[:, lanes] for act in acts] for lanes in heads]
        masks = [seq_mask([length_ref[m, 0, i] for i in range(SEQS)], rows)] * len(heads)
        incoming = [grad_product[m * rows : (m + 1) * rows, lanes] for lanes in heads]
        for lanes, grads in zip(heads, attend_back_all(incoming, acts, attend_all(acts, masks))):
            for t, grad in enumerate(grads):
                pre_ref[t, lines, lanes] = (grad * slopes[t][:, lanes]).astype(bf16)
    part_ref[...] = sum(dot(pre_ref[t], weight_ref[t], NT) for t in range(4))


def inputs_kernel(input_ref, og_ref, mine_ref, other_ref, out_ref):
    micro, rows, _ = input_ref.shape
    for m in range(micro):
        lines = pl.ds(m * rows, rows)
        normed, inverse = row_norm(input_ref[m].astype(f32))
        grad = norm_back(mine_ref[lines, :] + other_ref[lines, :], normed, inverse)
        out_ref[m] = (og_ref[lines, :].astype(f32) + grad).astype(bf16)


def weights_kernel(group, owners, *refs):
    row_refs, norm_refs = refs[:group], refs[group : 2 * group]
    act_ref, slope_ref, att_ref, back_ref, out_ref, inverse_ref, prod_ref, proj_ref, mix_ref, table_ref, packed_ref = refs[2 * group :]
    total = row_refs[0].shape[0]
    rows = att_ref.shape[1]
    cols = act_ref.shape[1]
    count = total // rows
    mix = mix_ref[my_head(), :]
    mixing, expand = 0.0, 0.0
    spans, incoming = [], []
    for s in range(group):
        out_grad = dot(row_refs[s][...], proj_ref[...], NT).astype(bf16)
        mixing += dot(out_grad, prod_ref[s * total : (s + 1) * total, :], TN)
        grad_product = dot(out_grad, mix, NT)
        for m in range(count):
            spans.append(pl.ds(s * total + m * rows, rows))
            incoming.append(grad_product[m * rows : (m + 1) * rows])
    packed_ref[:, :, cols : cols + HEAD_DIM] = mixing.reshape(owners, -1, HEAD_DIM).astype(bf16)
    packed_ref[:, :, cols + HEAD_DIM :] = table_ref[...]
    acts = [[act_ref[lines, t * HEAD_DIM : (t + 1) * HEAD_DIM] for t in range(4)] for lines in spans]
    results = [(att_ref[lines, :], back_ref[lines, :], out_ref[lines, :], inverse_ref[lines, :]) for lines in spans]
    grads = attend_back_all(incoming, acts, results)
    pre = [(jnp.concatenate(grad, axis=1) * slope_ref[lines, :]).astype(bf16) for grad, lines in zip(grads, spans)]
    for s in range(group):
        expand += dot(norm_refs[s][:total, :], jnp.concatenate(pre[s * count : (s + 1) * count], axis=0), TN)
    packed_ref[:, :, :cols] = expand.reshape(owners, -1, cols).astype(bf16)


def final_kernel(group, in_ref, expand_ref, mixing_ref, table_ref):
    cols = expand_ref.shape[2]
    side = range(group)
    for g in side:
        sources = [(y * group + z) * group + x for y in side for z in side for x in side if x % 2 + 2 * (y % 2) == g]
        total = sum(in_ref[i, :, : cols + HEAD_DIM].astype(f32) for i in sources)
        head = pl.ds(g * HEAD_DIM, HEAD_DIM)
        for t in range(4):
            expand_ref[:, t, head] = total[:, t * HEAD_DIM : (t + 1) * HEAD_DIM]
        mixing_ref[:, head] = total[:, cols:]
    lanes = pl.ds(cols + HEAD_DIM, HEAD_DIM)
    for z in side:
        total = sum(in_ref[(y * group + z) * group + x, :, lanes].astype(f32) for y in side for x in side)
        half = total.shape[0] // 2
        table_ref[z * half : (z + 1) * half, :HEAD_DIM] = total[:half]
        table_ref[z * half : (z + 1) * half, HEAD_DIM:] = total[half:]


def body(
    inputs,
    lengths,
    expand_weight,
    mixing_weight,
    projection,
    saved_rows,
    cluster_ids,
    item_ids,
    top_table,
    codebook,
):
    micro, rows, model_width = inputs.shape
    total = micro * rows
    owners = lax.axis_size(DEV)
    group = lax.axis_size("x")
    half_clusters, width = top_table.shape
    books, items, _ = codebook.shape
    cols = expand_weight.shape[2]
    slots = owners * micro * CAP
    own = half_clusters // owners
    saved = saved_rows.reshape(total, width)

    sent, slot_ids, marks = call(
        functools.partial(dispatch_kernel, owners, books, items),
        "dispatch",
        [((slots, width + 128), bf16), ((micro, rows), jnp.int32), ((total, 128), f32)],
        (cluster_ids, item_ids, saved_rows),
        "HHH HVH", limit=56,
    )
    got = lax.all_to_all(sent.reshape(owners, slots // owners, -1), DEV, 0, 0, tiled=True).reshape(slots, -1)

    (normed,) = call(
        norms_kernel,
        "norms",
        [((total + 16, model_width), bf16)],
        (lengths, inputs),
        "SV V",
        limit=28,
        after=(slot_ids,),
    )
    normed_all = [normed] + [from_member(normed, s) for s in range(1, group)]
    table = top_table.reshape(owners, group, own // group, width).swapaxes(0, 1).reshape(half_clusters, width)
    logits, stats = call(
        top_logits_kernel,
        "top_logits",
        [((total, half_clusters), f32), ((total, 128), f32)],
        (saved, table),
        "HH VV",
        limit=40,
        after=(slot_ids,),
    )
    row_top, *top_grads, top_token = call(
        functools.partial(top_grad_kernel, group, own),
        "top_grads",
        [((total, width), f32)] + [((total, half_clusters // group + width), bf16)] * group,
        (logits, stats, swap(stats), marks, table, saved),
        "VVVHHH " + "H" * (1 + group),
        limit=40,
        token=True,
    )
    top_all = [top_grads[0]] + [shifted(top_grads[s], "z", s) for s in range(1, group)]

    leaf, leaf_stats, got_held, book_held = leaf_scores(got, codebook, (top_token, normed[:8, :128]))
    back, leaf_grad = leaf_back(
        got_held, leaf, leaf_stats, swap(leaf_stats), book_held, ()
    )
    returned = lax.all_to_all(back.reshape(owners, slots // owners, width), DEV, 0, 0, tiled=True)

    late_weight, _ = lax.optimization_barrier((expand_weight, back))
    weight = lax.optimization_barrier(late_weight.swapaxes(0, 1))
    window_token = sum((a[:8, :128] for a in normed_all[1:]), weight[0, :8, :128])
    table_part, table_token = call(
        functools.partial(table_kernel, owners),
        "table_part",
        [((owners, 16, 128), bf16)],
        top_all,
        "H" * group + " H",
        after=(back, window_token),
        token=True,
    )

    (row_part,) = call(
        rows_kernel,
        "rows",
        [((total, width), f32)],
        (slot_ids, returned.reshape(slots, width), row_top),
        "VHH V", limit=28,
        after=(table_token,),
    )
    (row_grad,) = call(add_kernel, "row_grad", [((total, width), bf16)], (row_part, swap(row_part)), "VV V", limit=28)
    row_all = [row_grad] + [from_member(row_grad, s) for s in range(1, group)]

    group_rows = group * total
    group_forward = call(
        group_forward_kernel,
        "group_forward",
        [
            ((group_rows, 4 * HEAD_DIM), bf16),
            ((group_rows, 4 * HEAD_DIM), f32),
            ((group_rows, rows), bf16),
            ((group_rows, rows), f32),
            ((group_rows, HEAD_DIM), f32),
            ((group_rows, HEAD_DIM), f32),
            ((group_rows, HEAD_DIM), bf16),
        ],
        (*normed_all, weight),
        "R" * (group + 1) + " " + "V" * 7,
        limit=GROUP_LIMIT,
        after=(row_grad,),
        scratch=[
            pltpu.VMEM((4, model_width, HEAD_DIM), bf16),
            pltpu.VMEM((group, total + 16, model_width), bf16),
            pltpu.SemaphoreType.DMA((group + 1,)),
        ],
    )

    (packed,) = call(
        functools.partial(weights_kernel, group, owners),
        "weight_parts",
        [((owners, model_width // owners, cols + 2 * HEAD_DIM), bf16)],
        (*row_all, *normed_all, *group_forward, projection, mixing_weight, table_part),
        "V" * (2 * group + 10) + " H",
        limit=28,
    )
    arrived = lax.all_to_all(packed, DEV, 0, 0, tiled=True)

    out_grad, grad_part = call(
        trunk_kernel,
        "trunk",
        [((total, model_width), bf16), ((total, model_width), f32)],
        (lengths, normed, row_grad, projection, mixing_weight, weight),
        "SHHHHR VV",
        limit=48,
        scratch=[pltpu.VMEM((4, total, cols), bf16), pltpu.VMEM(weight.shape, bf16), pltpu.SemaphoreType.DMA((4,))],
        after=(packed,),
    )
    (grad_inputs,) = call(
        inputs_kernel, "input_grads", [(inputs.shape, bf16)], (inputs, out_grad, grad_part, swap(grad_part)), "HVVV H", limit=48
    )
    book_grads = leaf_book(got, leaf_grad, books, width, (packed,))
    share = model_width // owners
    expand, mixing, table_share = call(
        functools.partial(final_kernel, group),
        "weight_sums",
        [((share, 4, cols), f32), ((share, cols), f32), ((own, width), f32)],
        (arrived,),
        "V HHH",
        limit=28,
    )
    return grad_inputs, expand, mixing.T, table_share, book_grads


def solution(mesh):
    grid = Mesh(mesh.devices.reshape(2, 4, 4, 4), ("section",) + DEV)
    return jax.shard_map(
        body,
        mesh=grid,
        in_specs=(
            P(None, DEV, None),
            P(None, DEV, None),
            P(None, None, "section"),
            P("section", None),
            P(),
            P(None, DEV, None),
            P(None, DEV),
            P(None, DEV),
            P("section", None),
            P(DEV, "section", None),
        ),
        out_specs=(
            P(None, DEV, None),
            P(DEV, None, "section"),
            P("section", DEV),
            P(("section",) + DEV, None),
            P(DEV, "section", None),
        ),
        check_vma=False,
    )
```

```python
import functools

import jax
import jax.numpy as jnp
from jax import lax
from jax.experimental import pallas as pl
from jax.experimental.pallas import tpu as pltpu
from jax.sharding import Mesh
from jax.sharding import PartitionSpec as P

HEAD_DIM = 128
SEQ_MOST = 64
SEQS = 4
CAP = 4
eps = 1e-05
DEV = ("y", "z", "x")
f32 = jnp.float32
bf16 = jnp.bfloat16
NN = ((1,), (0,))
NT = ((1,), (1,))
TN = ((0,), (0,))


def swap(part):
    return lax.ppermute(part, "section", [(0, 1), (1, 0)])


def member(axis):
    return lax.rem(lax.axis_index("x"), 2) + 2 * lax.rem(lax.axis_index(axis), 2)


def from_member(part, axis, other):
    count = lax.axis_size("x")
    flip = count * (other // 2) + other % 2
    return lax.ppermute(part, (axis, "x"), [(i, i ^ flip) for i in range(lax.axis_size(axis) * count)])


def dot(left, right, dims):
    return lax.dot_general(left, right, (dims, ((), ())), preferred_element_type=f32)


def iota(shape, dim):
    return lax.broadcasted_iota(jnp.int32, shape, dim)


def row_norm(argument):
    row_mean = jnp.mean(argument, axis=-1, keepdims=True)
    centered = argument - row_mean
    variance = jnp.mean(centered * centered, axis=-1, keepdims=True)
    inverse = lax.rsqrt(variance + eps)
    return (centered * inverse, inverse)


def norm_back(incoming, normed, inverse):
    mean_in = jnp.mean(incoming, axis=-1, keepdims=True)
    mean_dot = jnp.mean(incoming * normed, axis=-1, keepdims=True)
    return (incoming - mean_in - normed * mean_dot) * inverse


def call(kernel, name, outs, args, kinds, after=(), scratch=(), limit=56, flops=0, token=False):
    in_kinds, out_kinds = kinds.split()
    if token:
        outs, out_kinds = [*outs, ((8, 128), f32)], out_kinds + "V"
    assert len(in_kinds) == len(args) and len(out_kinds) == len(outs), name
    spaces = {"V": pltpu.VMEM, "S": pltpu.SMEM, "H": pl.ANY, "R": pl.ANY}
    held = [pltpu.VMEM(a.shape, a.dtype) for a, k in zip(args, in_kinds) if k == "H"]
    held += [pltpu.VMEM(s, d) for (s, d), k in zip(outs, out_kinds) if k == "H"]
    sems = [pltpu.SemaphoreType.DMA((len(held),))] if held else []

    def run(*refs):
        ins = list(refs[: len(args)])
        refs = refs[len(args) + len(after) :]
        results = list(refs[: len(outs)])
        buffers = list(refs[len(outs) : len(outs) + len(held)])
        rest = refs[len(outs) + len(held) + len(sems) :]
        sem = refs[len(outs) + len(held)] if held else None
        count = 0
        first, last = [], []
        for i, kind in enumerate(in_kinds):
            if kind == "H":
                first.append(pltpu.make_async_copy(ins[i], buffers[count], sem.at[count]))
                first[-1].start()
                ins[i] = buffers[count]
                count += 1
        for i, kind in enumerate(out_kinds):
            if kind == "H":
                last.append(pltpu.make_async_copy(buffers[count], results[i], sem.at[count]))
                results[i] = buffers[count]
                count += 1
        for copy in first:
            copy.wait()
        if token:
            results.pop()[...] = jnp.zeros((8, 128), f32)
        kernel(*ins, *results, *rest)
        for copy in last:
            copy.start()
        for copy in last:
            copy.wait()

    return pl.pallas_call(
        run,
        in_specs=[pl.BlockSpec(memory_space=spaces[k]) for k in in_kinds] + [pl.BlockSpec(memory_space=pl.ANY)] * len(after),
        out_specs=[pl.BlockSpec(memory_space=spaces[k]) for k in out_kinds],
        out_shape=[jax.ShapeDtypeStruct(s, d) for s, d in outs],
        scratch_shapes=held + sems + list(scratch),
        compiler_params=pltpu.CompilerParams(vmem_limit_bytes=limit * 2**20),
        cost_estimate=pl.CostEstimate(flops=flops, bytes_accessed=0, transcendentals=0),
        name=name,
    )(*args, *after)


def one_hot(slots_row, count):
    return jnp.where(iota((count, slots_row.shape[1]), 0) == slots_row, 1.0, 0.0).astype(bf16)


def dispatch_kernel(owners, books, half, cluster_ref, item_ref, saved_ref, sent_ref, slot_ref, mark_ref):
    micro, rows = cluster_ref.shape
    width = saved_ref.shape[2]
    each = micro * CAP
    before = jnp.where(iota((rows, rows), 0) < iota((rows, rows), 1), 1.0, 0.0).astype(bf16)
    same = jnp.where(iota((rows, rows), 0) == iota((rows, rows), 1), 1.0, 0.0).astype(bf16)
    kind = iota((128, rows), 0)
    rows_out, codes_out = 0.0, 0.0
    for m in range(micro):
        target, item = cluster_ref[m : m + 1], item_ref[m : m + 1]
        owner, local = target // books, target % books
        marks = jnp.where(iota((owners, rows), 0) == owner, 1.0, 0.0)
        earlier = dot(marks.astype(bf16), before, NN)
        rank = jnp.sum(earlier * marks, axis=0, keepdims=True).astype(jnp.int32)
        slot = owner * each + m * CAP + rank
        slot_ref[m : m + 1] = slot
        code = jnp.where(
            kind == 0,
            local + 1,
            jnp.where(kind == 1, item // half, jnp.where(kind == 2, item % half, jnp.where(kind == 3, owner, 0))),
        )
        code = code.astype(f32).astype(bf16)
        pick = one_hot(slot, owners * each)
        rows_out += dot(pick, saved_ref[m], NN)
        codes_out += dot(pick, code, NT)
        turned = dot(same, code, NT)
        mark_ref[m * rows : (m + 1) * rows] = jnp.broadcast_to(
            turned[:, 3:4] * books + turned[:, 0:1] - 1.0, (rows, 128)
        )
    sent_ref[:, :width] = rows_out.astype(bf16)
    sent_ref[:, width:] = codes_out.astype(bf16)


def top_logits_kernel(group, owners, saved_ref, table_ref, logit_ref, stat_ref, turned_ref):
    half, width = table_ref.shape
    rows = table_ref[...].astype(f32).reshape(owners, group, half // owners // group, width)
    turned = jnp.concatenate([rows[:, q].reshape(half // group, width) for q in range(group)], axis=0).astype(bf16)
    turned_ref[...] = turned
    logits = dot(saved_ref[...], turned, NT)
    logit_ref[...] = logits
    peak = jnp.max(logits, axis=1, keepdims=True)
    mass = jnp.sum(jnp.exp(logits - peak), axis=1, keepdims=True)
    stat_ref[...] = jnp.where(iota(stat_ref.shape, 1) == 0, peak, mass)


def joined(mine_ref, other_ref):
    peak_a, mass_a = mine_ref[:, 0:1], mine_ref[:, 1:2]
    peak_b, mass_b = other_ref[:, 0:1], other_ref[:, 1:2]
    peak = jnp.maximum(peak_a, peak_b)
    return peak, mass_a * jnp.exp(peak_a - peak) + mass_b * jnp.exp(peak_b - peak)


def top_grad_kernel(group, own, logit_ref, mine_ref, other_ref, mark_ref, table_ref, saved_ref, *out_refs):
    row_ref, grad_refs = out_refs[0], out_refs[1:]
    half = table_ref.shape[0]
    quarter = half // group
    piece = own // group
    base = lax.axis_index("section") * half
    me = member("z")
    peak, mass = joined(mine_ref, other_ref)
    target = mark_ref[:, 0:1].astype(jnp.int32) - base
    total = 0.0
    column = iota((mark_ref.shape[0], quarter), 1)
    for q in range(group):
        index = (column // piece) * own + q * piece + column % piece
        cols = pl.ds(q * quarter, quarter)
        probs = jnp.exp(logit_ref[:, cols] - peak) / mass
        grad = (probs - jnp.where(index == target, 1.0, 0.0)).astype(bf16)
        total += dot(grad, table_ref[cols, :], NN)
        for s in range(group):

            @pl.when(lax.bitwise_xor(me, s) == q)
            def _(s=s, grad=grad):
                grad_refs[s][:, :quarter] = grad
                grad_refs[s][:, quarter:] = saved_ref[...]

    row_ref[...] = total


def table_kernel(owners, *refs):
    *in_refs, out_ref = refs
    quarter = in_refs[0].shape[1] - 256
    total = sum(dot(r[:, :quarter], r[:, quarter:], TN) for r in in_refs)
    left = total[:, :128].reshape(owners, -1, 128)
    right = total[:, 128:].reshape(owners, -1, 128)
    out_ref[...] = jnp.concatenate([left, right], axis=1).astype(bf16)


def masked_product(code_ref, left_ref, width, book_ref, out_ref, dims, group, ready):
    lines = 256
    out_ref[...] = jnp.zeros_like(out_ref)

    def step(i, carry):
        ready(i)
        books = book_ref[pl.ds(i * group, group)]
        if dims == NT:
            right = jnp.concatenate([books[k] for k in range(group)], axis=1)
        else:
            right = books.reshape(-1, books.shape[2])
        for r in range(0, out_ref.shape[0], lines):
            some = pl.ds(r, lines)
            left, code = left_ref[some, :width], code_ref[some, :]
            parts = []
            for k in range(group):
                here = code == (i * group + k + 1).astype(f32).astype(bf16)
                parts.append(jnp.where(here, left, jnp.zeros_like(left)))
            out_ref[some, :] += dot(jnp.concatenate(parts, axis=1), right, dims)
        return carry

    lax.fori_loop(0, book_ref.shape[0] // group, step, 0)


GROUP_LIMIT = 40
BOOK_GROUP = 16
BOOK_COPIES = 4


def leaf_scores_kernel(got_in, book_in, out_ref, stat_ref, got_ref, book_ref, code_ref, got_sem, sem):
    width = book_ref.shape[2]
    steps = book_ref.shape[0] // BOOK_GROUP
    piece = BOOK_GROUP // BOOK_COPIES

    def copies(i):
        for j in range(BOOK_COPIES):
            some = pl.ds(i * BOOK_GROUP + j * piece, piece)
            yield pltpu.make_async_copy(book_in.at[some], book_ref.at[some], sem.at[i, j])

    got_copy = pltpu.make_async_copy(got_in, got_ref, got_sem)
    got_copy.start()
    for i in range(2):
        for copy in copies(i):
            copy.start()
    got_copy.wait()
    code_ref[...] = jnp.broadcast_to(got_ref[:, width : width + 1], code_ref.shape)

    def ready(i):
        for copy in copies(i):
            copy.wait()

        @pl.when(i + 2 < steps)
        def _():
            for copy in copies(i + 2):
                copy.start()

    masked_product(code_ref, got_ref, width, book_ref, out_ref, NT, BOOK_GROUP, ready)
    scores = out_ref[...]
    peak = jnp.max(scores, axis=1, keepdims=True)
    mass = jnp.sum(jnp.exp(scores - peak), axis=1, keepdims=True)
    stat_ref[...] = jnp.where(iota(stat_ref.shape, 1) == 0, peak, mass)


def leaf_back_kernel(got_ref, score_ref, mine_ref, other_ref, book_ref, back_ref, grad_ref, code_ref, total_ref):
    items, width = book_ref.shape[1:]
    code = got_ref[:, width : width + 1]
    code_ref[...] = jnp.broadcast_to(code, code_ref.shape)
    high = got_ref[:, width + 1 : width + 2].astype(f32).astype(jnp.int32)
    low = got_ref[:, width + 2 : width + 3].astype(f32).astype(jnp.int32)
    peak, mass = joined(mine_ref, other_ref)
    probs = jnp.exp(score_ref[...] - peak) / mass
    hit = (iota(probs.shape, 1) == low) & (high == lax.axis_index("section"))
    grad = jnp.where(code.astype(f32) > 0, probs - jnp.where(hit, 1.0, 0.0), 0.0)
    grad_ref[...] = grad.astype(bf16)
    masked_product(code_ref, grad_ref, items, book_ref, total_ref, NN, 32, lambda i: None)
    back_ref[...] = total_ref[...].astype(bf16)


def leaf_book_kernel(got_ref, grad_ref, out_ref, code_ref, turned_ref, held_ref, sem):
    books, items, width = out_ref.shape
    group = books // sem.shape[0]
    slots = got_ref.shape[0]
    turned_ref[...] = grad_ref[...].astype(f32).T.astype(bf16)
    code_ref[...] = jnp.broadcast_to(got_ref[:, width : width + 1].astype(f32), (slots, items)).T.astype(bf16)
    rows = got_ref[:, :width]
    copies = []
    for i in range(books // group):
        some = pl.ds(i * group, group)
        turned, code = turned_ref[...], code_ref[...]
        parts = []
        for k in range(group):
            here = code == (i * group + k + 1)
            parts.append(jnp.where(here, turned, jnp.zeros_like(turned)))
        grads = dot(jnp.concatenate(parts, axis=0), rows, NN)
        held_ref[some] = grads.reshape(group, items, width).astype(bf16)
        copies.append(pltpu.make_async_copy(held_ref.at[some], out_ref.at[some], sem.at[i]))
        copies[-1].start()
    for copy in copies:
        copy.wait()


def leaf_scores(got, book, after):
    books, items, width = book.shape
    slots = got.shape[0]
    return call(
        leaf_scores_kernel,
        "leaf_scores",
        [((slots, items), f32), ((slots, 128), f32), (got.shape, bf16), (book.shape, bf16)],
        (got, book),
        "RR VVVV", limit=42,
        flops=2 * slots * books * items * width,
        scratch=[
            pltpu.VMEM((slots, width), bf16),
            pltpu.SemaphoreType.DMA,
            pltpu.SemaphoreType.DMA((books // BOOK_GROUP, BOOK_COPIES)),
        ],
        after=after,
    )


def leaf_back(got, scores, mine, other, book, after):
    books, items, width = book.shape
    slots = got.shape[0]
    return call(
        leaf_back_kernel,
        "leaf_back",
        [((slots, width), bf16), ((slots, items), bf16)],
        (got, scores, mine, other, book),
        "VVVVV HH",
        limit=28,
        scratch=[pltpu.VMEM((slots, items), bf16), pltpu.VMEM((slots, width), f32)],
        after=after,
    )


def leaf_book(got, grads, books, width, after):
    slots, items = grads.shape
    group = 4
    return call(
        leaf_book_kernel,
        "leaf_book",
        [((books, items, width), bf16)],
        (got, grads),
        "HH R",
        scratch=[
            pltpu.VMEM((items, slots), bf16),
            pltpu.VMEM((items, slots), bf16),
            pltpu.VMEM((books, items, width), bf16),
            pltpu.SemaphoreType.DMA((books // group,)),
        ],
        after=after,
    )[0]


def slope_of(argument, logistic):
    return logistic * (1.0 + argument * (1.0 - logistic))


def norms_kernel(length_ref, input_ref, out_ref):
    micro, rows, width = input_ref.shape
    for m in range(micro):
        out_ref[m * rows : (m + 1) * rows] = row_norm(input_ref[m].astype(f32))[0].astype(bf16)
    seqs = length_ref.shape[2]
    lane = iota((16, width), 1)
    held = jnp.zeros((16, width), f32)
    for m in range(micro):
        for i in range(seqs):
            held = jnp.where(lane == m * seqs + i, length_ref[m, 0, i].astype(f32), held)
    out_ref[micro * rows :] = held.astype(bf16)


def seq_mask(sizes, rows):
    row, col = iota((rows, rows), 0), iota((rows, rows), 1)
    row_seg, col_seg, end = 0, 0, 0
    for size in sizes:
        end = end + size
        row_seg += jnp.where(row >= end, 1, 0)
        col_seg += jnp.where(col >= end, 1, 0)
    return jnp.where((row_seg == col_seg) & (col <= row), 1.0 / SEQ_MOST, 0.0)


def held_sizes(held, m):
    held = held.astype(f32)[0:1].astype(jnp.int32)
    return [held[:, m * SEQS + i : m * SEQS + i + 1] for i in range(SEQS)]


def attend_all(acts, masks):
    scores = [dot(query, key, NT) for _, _, query, key in acts]
    logistics = [jax.nn.sigmoid(score) for score in scores]
    attention = [(a * b * mask).astype(bf16) for a, b, mask in zip(scores, logistics, masks)]
    mixed = [dot(a, act[1], NN) for a, act in zip(attention, acts)]
    back = [slope_of(a, b) * mask for a, b, mask in zip(scores, logistics, masks)]
    normed = [row_norm(one) for one in mixed]
    return [(a, b, n, jnp.broadcast_to(i, n.shape)) for a, b, (n, i) in zip(attention, back, normed)]


def my_head():
    return pl.ds(pl.multiple_of(member("y") * HEAD_DIM, HEAD_DIM), HEAD_DIM)


def head_weight_kernel(weight_in, out_ref, part_ref, flat_ref, sem):
    copy = pltpu.make_async_copy(weight_in.at[:, :, my_head()], part_ref, sem)
    copy.start()
    copy.wait()
    flat_ref[...] = part_ref[...].astype(f32).reshape(flat_ref.shape)
    depth, parts = weight_in.shape[:2]
    for t in range(parts):
        out_ref[:, t * HEAD_DIM : (t + 1) * HEAD_DIM] = flat_ref[pl.ds(t, depth, stride=parts), :].astype(bf16)


def group_forward_kernel(*refs):
    *norm_ins, weight_in, act_ref, slope_ref, att_ref, back_ref, out_ref, inverse_ref, prod_ref = refs[:-3]
    weight_ref, norm_ref, sem = refs[-3:]
    pairs = [(weight_in, weight_ref)] + [(one, norm_ref.at[s]) for s, one in enumerate(norm_ins)]
    copies = [pltpu.make_async_copy(a, b, sem.at[i]) for i, (a, b) in enumerate(pairs)]
    for copy in copies:
        copy.start()
    for copy in copies:
        copy.wait()
    rows = att_ref.shape[1]
    total = out_ref.shape[0] // len(norm_ins)
    weight = weight_ref[...]
    acts, masks, spans = [], [], []
    for s in range(len(norm_ins)):
        for m in range(total // rows):
            lines = pl.ds(s * total + m * rows, rows)
            pre_act = dot(norm_ref[s, m * rows : (m + 1) * rows, :], weight, NN)
            logistic = jax.nn.sigmoid(pre_act)
            act = (pre_act * logistic).astype(bf16)
            act_ref[lines, :] = act
            slope_ref[lines, :] = slope_of(pre_act, logistic)
            spans.append(lines)
            masks.append(seq_mask(held_sizes(norm_ref[s, total:, :128], m), rows))
            acts.append([act[:, t * HEAD_DIM : (t + 1) * HEAD_DIM] for t in range(4)])
    for lines, act, result in zip(spans, acts, attend_all(acts, masks)):
        att_ref[lines, :], back_ref[lines, :], out_ref[lines, :], inverse_ref[lines, :] = result
        prod_ref[lines, :] = (result[2] * act[0].astype(f32)).astype(bf16)


def attend_back_all(incoming, acts, results):
    mixed = [
        norm_back(a * act[0].astype(f32), normed, inverse).astype(bf16)
        for a, act, (_, _, normed, inverse) in zip(incoming, acts, results)
    ]
    grads = [dot(a, act[1], NT) for a, act in zip(mixed, acts)]
    values = [dot(result[0], a, TN) for result, a in zip(results, mixed)]
    grads = [(a * result[1]).astype(bf16) for a, result in zip(grads, results)]
    queries = [dot(a, act[3], NN) for a, act in zip(grads, acts)]
    keys = [dot(a, act[2], TN) for a, act in zip(grads, acts)]
    gates = [a * result[2] for a, result in zip(incoming, results)]
    return list(zip(gates, values, queries, keys))


def rows_kernel(slot_ref, returned_ref, top_ref, out_ref):
    micro, rows = slot_ref.shape
    for m in range(micro):
        lines = pl.ds(m * rows, rows)
        pick = one_hot(slot_ref[m : m + 1], returned_ref.shape[0])
        out_ref[lines, :] = top_ref[lines, :] + dot(pick, returned_ref[...], TN)


def add_kernel(mine_ref, other_ref, out_ref):
    out_ref[...] = (mine_ref[...] + other_ref[...]).astype(bf16)


def trunk_kernel(length_ref, norm_ref, row_ref, proj_ref, mix_ref, weight_in, og_ref, part_ref, pre_ref, weight_ref, sem):
    copies = [pltpu.make_async_copy(weight_in.at[t], weight_ref.at[t], sem.at[t]) for t in range(4)]
    for copy in copies:
        copy.start()
    rows = HEAD_DIM
    total, cols = row_ref.shape[0], weight_ref.shape[2]
    out_grad = dot(row_ref[...], proj_ref[...], NT).astype(bf16)
    og_ref[...] = out_grad
    grad_product = dot(out_grad, mix_ref[...], NT)
    for copy in copies:
        copy.wait()
    for m in range(total // rows):
        lines = pl.ds(m * rows, rows)
        normed = norm_ref[lines, :]
        acts, slopes = [], []
        for t in range(4):
            pre_act = dot(normed, weight_ref[t], NN)
            logistic = jax.nn.sigmoid(pre_act)
            acts.append((pre_act * logistic).astype(bf16))
            slopes.append(slope_of(pre_act, logistic))
        heads = [slice(h * HEAD_DIM, (h + 1) * HEAD_DIM) for h in range(cols // HEAD_DIM)]
        acts = [[act[:, lanes] for act in acts] for lanes in heads]
        masks = [seq_mask([length_ref[m, 0, i] for i in range(SEQS)], rows)] * len(heads)
        incoming = [grad_product[m * rows : (m + 1) * rows, lanes] for lanes in heads]
        for lanes, grads in zip(heads, attend_back_all(incoming, acts, attend_all(acts, masks))):
            for t, grad in enumerate(grads):
                pre_ref[t, lines, lanes] = (grad * slopes[t][:, lanes]).astype(bf16)
    part_ref[...] = sum(dot(pre_ref[t], weight_ref[t], NT) for t in range(4))


def inputs_kernel(input_ref, og_ref, mine_ref, other_ref, out_ref):
    micro, rows, _ = input_ref.shape
    for m in range(micro):
        lines = pl.ds(m * rows, rows)
        normed, inverse = row_norm(input_ref[m].astype(f32))
        grad = norm_back(mine_ref[lines, :] + other_ref[lines, :], normed, inverse)
        out_ref[m] = (og_ref[lines, :].astype(f32) + grad).astype(bf16)


def weights_kernel(group, owners, *refs):
    row_refs, norm_refs = refs[:group], refs[group : 2 * group]
    act_ref, slope_ref, att_ref, back_ref, out_ref, inverse_ref, prod_ref, proj_ref, mix_ref, table_ref, packed_ref = refs[2 * group :]
    total = row_refs[0].shape[0]
    rows = att_ref.shape[1]
    cols = act_ref.shape[1]
    count = total // rows
    mix = mix_ref[my_head(), :]
    mixing, expand = 0.0, 0.0
    spans, incoming = [], []
    for s in range(group):
        out_grad = dot(row_refs[s][...], proj_ref[...], NT).astype(bf16)
        mixing += dot(out_grad, prod_ref[s * total : (s + 1) * total, :], TN)
        grad_product = dot(out_grad, mix, NT)
        for m in range(count):
            spans.append(pl.ds(s * total + m * rows, rows))
            incoming.append(grad_product[m * rows : (m + 1) * rows])
    packed_ref[:, :, cols : cols + HEAD_DIM] = mixing.reshape(owners, -1, HEAD_DIM).astype(bf16)
    packed_ref[:, :, cols + HEAD_DIM :] = table_ref[...]
    acts = [[act_ref[lines, t * HEAD_DIM : (t + 1) * HEAD_DIM] for t in range(4)] for lines in spans]
    results = [(att_ref[lines, :], back_ref[lines, :], out_ref[lines, :], inverse_ref[lines, :]) for lines in spans]
    grads = attend_back_all(incoming, acts, results)
    pre = [(jnp.concatenate(grad, axis=1) * slope_ref[lines, :]).astype(bf16) for grad, lines in zip(grads, spans)]
    for s in range(group):
        expand += dot(norm_refs[s][:total, :], jnp.concatenate(pre[s * count : (s + 1) * count], axis=0), TN)
    packed_ref[:, :, :cols] = expand.reshape(owners, -1, cols).astype(bf16)


def final_kernel(group, in_ref, expand_ref, mixing_ref, table_ref):
    cols = expand_ref.shape[2]
    side = range(group)
    for g in side:
        sources = [(y * group + z) * group + x for y in side for z in side for x in side if x % 2 + 2 * (y % 2) == g]
        total = sum(in_ref[i, :, : cols + HEAD_DIM].astype(f32) for i in sources)
        head = pl.ds(g * HEAD_DIM, HEAD_DIM)
        for t in range(4):
            expand_ref[:, t, head] = total[:, t * HEAD_DIM : (t + 1) * HEAD_DIM]
        mixing_ref[:, head] = total[:, cols:]
    lanes = pl.ds(cols + HEAD_DIM, HEAD_DIM)
    for q in side:
        sources = [(y * group + z) * group + x for y in side for z in side for x in side if x % 2 + 2 * (z % 2) == q]
        total = sum(in_ref[i, :, lanes].astype(f32) for i in sources)
        half = total.shape[0] // 2
        table_ref[q * half : (q + 1) * half, :HEAD_DIM] = total[:half]
        table_ref[q * half : (q + 1) * half, HEAD_DIM:] = total[half:]


def body(
    inputs,
    lengths,
    expand_weight,
    mixing_weight,
    projection,
    saved_rows,
    cluster_ids,
    item_ids,
    top_table,
    codebook,
):
    micro, rows, model_width = inputs.shape
    total = micro * rows
    owners = lax.axis_size(DEV)
    group = lax.axis_size("x")
    half_clusters, width = top_table.shape
    books, items, _ = codebook.shape
    cols = expand_weight.shape[2]
    slots = owners * micro * CAP
    own = half_clusters // owners
    saved = saved_rows.reshape(total, width)

    sent, slot_ids, marks = call(
        functools.partial(dispatch_kernel, owners, books, items),
        "dispatch",
        [((slots, width + 128), bf16), ((micro, rows), jnp.int32), ((total, 128), f32)],
        (cluster_ids, item_ids, saved_rows),
        "HHH HVH", limit=56,
    )
    got = lax.all_to_all(sent.reshape(owners, slots // owners, -1), DEV, 0, 0, tiled=True).reshape(slots, -1)

    (normed,) = call(
        norms_kernel,
        "norms",
        [((total + 16, model_width), bf16)],
        (lengths, inputs),
        "SV V",
        limit=28,
        after=(slot_ids,),
    )
    normed_all = [normed] + [from_member(normed, "y", s) for s in range(1, group)]
    logits, stats, table = call(
        functools.partial(top_logits_kernel, group, owners),
        "top_logits",
        [((total, half_clusters), f32), ((total, 128), f32), (top_table.shape, bf16)],
        (saved, top_table),
        "HH VVV",
        limit=40,
        after=(slot_ids,),
    )
    row_top, *top_grads, top_token = call(
        functools.partial(top_grad_kernel, group, own),
        "top_grads",
        [((total, width), f32)] + [((total, half_clusters // group + width), bf16)] * group,
        (logits, stats, swap(stats), marks, table, saved),
        "VVVHHH " + "H" * (1 + group),
        limit=40,
        token=True,
    )
    top_all = [top_grads[0]] + [from_member(top_grads[s], "z", s) for s in range(1, group)]

    leaf, leaf_stats, got_held, book_held = leaf_scores(got, codebook, (top_token, normed[:8, :128]))
    back, leaf_grad = leaf_back(
        got_held, leaf, leaf_stats, swap(leaf_stats), book_held, ()
    )
    returned = lax.all_to_all(back.reshape(owners, slots // owners, width), DEV, 0, 0, tiled=True)

    head_weight, head_token = call(
        head_weight_kernel,
        "head_weight",
        [((model_width, 4 * HEAD_DIM), bf16)],
        (expand_weight,),
        "R H",
        scratch=[
            pltpu.VMEM((model_width, 4, HEAD_DIM), bf16),
            pltpu.VMEM((model_width * 4, HEAD_DIM), f32),
            pltpu.SemaphoreType.DMA,
        ],
        after=(back, sum(a[:8, :128] for a in normed_all[1:])),
        token=True,
    )

    (row_part,) = call(
        rows_kernel,
        "rows",
        [((total, width), f32)],
        (slot_ids, returned.reshape(slots, width), row_top),
        "VHH V", limit=28,
        after=(head_token,),
    )
    (row_grad,) = call(add_kernel, "row_grad", [((total, width), bf16)], (row_part, swap(row_part)), "VV V", limit=28)
    row_all = [row_grad] + [from_member(row_grad, "y", s) for s in range(1, group)]

    group_rows = group * total
    group_forward = call(
        group_forward_kernel,
        "group_forward",
        [
            ((group_rows, 4 * HEAD_DIM), bf16),
            ((group_rows, 4 * HEAD_DIM), f32),
            ((group_rows, rows), bf16),
            ((group_rows, rows), f32),
            ((group_rows, HEAD_DIM), f32),
            ((group_rows, HEAD_DIM), f32),
            ((group_rows, HEAD_DIM), bf16),
        ],
        (*normed_all, head_weight),
        "R" * (group + 1) + " " + "V" * 7,
        limit=GROUP_LIMIT,
        after=(row_grad,),
        scratch=[
            pltpu.VMEM(head_weight.shape, bf16),
            pltpu.VMEM((group, total + 16, model_width), bf16),
            pltpu.SemaphoreType.DMA((group + 1,)),
        ],
    )

    (table_part,) = call(
        functools.partial(table_kernel, owners),
        "table_part",
        [((owners, 16, 128), bf16)],
        top_all,
        "V" * group + " V",
        limit=16,
        after=(row_grad,),
    )

    (packed,) = call(
        functools.partial(weights_kernel, group, owners),
        "weight_parts",
        [((owners, model_width // owners, cols + 2 * HEAD_DIM), bf16)],
        (*row_all, *normed_all, *group_forward, projection, mixing_weight, table_part),
        "V" * (2 * group + 10) + " H",
        limit=28,
    )
    arrived = lax.all_to_all(packed, DEV, 0, 0, tiled=True)

    late_weight, _ = lax.optimization_barrier((expand_weight, packed))
    weight = late_weight.swapaxes(0, 1)
    out_grad, grad_part = call(
        trunk_kernel,
        "trunk",
        [((total, model_width), bf16), ((total, model_width), f32)],
        (lengths, normed, row_grad, projection, mixing_weight, weight),
        "SHHHHR VV",
        limit=48,
        scratch=[pltpu.VMEM((4, total, cols), bf16), pltpu.VMEM(weight.shape, bf16), pltpu.SemaphoreType.DMA((4,))],
        after=(packed,),
    )
    (grad_inputs,) = call(
        inputs_kernel, "input_grads", [(inputs.shape, bf16)], (inputs, out_grad, grad_part, swap(grad_part)), "HVVV H", limit=48
    )
    book_grads = leaf_book(got, leaf_grad, books, width, (packed,))
    share = model_width // owners
    expand, mixing, table_share = call(
        functools.partial(final_kernel, group),
        "weight_sums",
        [((share, 4, cols), f32), ((share, cols), f32), ((own, width), f32)],
        (arrived,),
        "V HHH",
        limit=28,
    )
    return grad_inputs, expand, mixing.T, table_share, book_grads


def solution(mesh):
    grid = Mesh(mesh.devices.reshape(2, 4, 4, 4), ("section",) + DEV)
    return jax.shard_map(
        body,
        mesh=grid,
        in_specs=(
            P(None, DEV, None),
            P(None, DEV, None),
            P(None, None, "section"),
            P("section", None),
            P(),
            P(None, DEV, None),
            P(None, DEV),
            P(None, DEV),
            P("section", None),
            P(DEV, "section", None),
        ),
        out_specs=(
            P(None, DEV, None),
            P(DEV, None, "section"),
            P("section", DEV),
            P(("section",) + DEV, None),
            P(DEV, "section", None),
        ),
        check_vma=False,
    )
```

```python
import functools

import jax
import jax.numpy as jnp
from jax import lax
from jax.experimental import pallas as pl
from jax.experimental.pallas import tpu as pltpu
from jax.sharding import Mesh
from jax.sharding import PartitionSpec as P

HEAD_DIM = 128
SEQ_MOST = 64
SEQS = 4
CAP = 4
eps = 1e-05
DEV = ("y", "z", "x")
f32 = jnp.float32
bf16 = jnp.bfloat16
NN = ((1,), (0,))
NT = ((1,), (1,))
TN = ((0,), (0,))


def swap(part):
    return lax.ppermute(part, "section", [(0, 1), (1, 0)])


def member(axis):
    return lax.rem(lax.axis_index("x"), 2) + 2 * lax.rem(lax.axis_index(axis), 2)


def from_member(part, axis, other):
    count = lax.axis_size("x")
    flip = count * (other // 2) + other % 2
    return lax.ppermute(part, (axis, "x"), [(i, i ^ flip) for i in range(lax.axis_size(axis) * count)])


def dot(left, right, dims):
    return lax.dot_general(left, right, (dims, ((), ())), preferred_element_type=f32)


def iota(shape, dim):
    return lax.broadcasted_iota(jnp.int32, shape, dim)


def row_norm(argument):
    row_mean = jnp.mean(argument, axis=-1, keepdims=True)
    centered = argument - row_mean
    variance = jnp.mean(centered * centered, axis=-1, keepdims=True)
    inverse = lax.rsqrt(variance + eps)
    return (centered * inverse, inverse)


def norm_back(incoming, normed, inverse):
    mean_in = jnp.mean(incoming, axis=-1, keepdims=True)
    mean_dot = jnp.mean(incoming * normed, axis=-1, keepdims=True)
    return (incoming - mean_in - normed * mean_dot) * inverse


def call(kernel, name, outs, args, kinds, after=(), scratch=(), limit=56, flops=0, token=False):
    in_kinds, out_kinds = kinds.split()
    if token:
        outs, out_kinds = [*outs, ((8, 128), f32)], out_kinds + "V"
    assert len(in_kinds) == len(args) and len(out_kinds) == len(outs), name
    spaces = {"V": pltpu.VMEM, "S": pltpu.SMEM, "H": pl.ANY, "R": pl.ANY}
    held = [pltpu.VMEM(a.shape, a.dtype) for a, k in zip(args, in_kinds) if k == "H"]
    held += [pltpu.VMEM(s, d) for (s, d), k in zip(outs, out_kinds) if k == "H"]
    sems = [pltpu.SemaphoreType.DMA((len(held),))] if held else []

    def run(*refs):
        ins = list(refs[: len(args)])
        refs = refs[len(args) + len(after) :]
        results = list(refs[: len(outs)])
        buffers = list(refs[len(outs) : len(outs) + len(held)])
        rest = refs[len(outs) + len(held) + len(sems) :]
        sem = refs[len(outs) + len(held)] if held else None
        count = 0
        first, last = [], []
        for i, kind in enumerate(in_kinds):
            if kind == "H":
                first.append(pltpu.make_async_copy(ins[i], buffers[count], sem.at[count]))
                first[-1].start()
                ins[i] = buffers[count]
                count += 1
        for i, kind in enumerate(out_kinds):
            if kind == "H":
                last.append(pltpu.make_async_copy(buffers[count], results[i], sem.at[count]))
                results[i] = buffers[count]
                count += 1
        for copy in first:
            copy.wait()
        if token:
            results.pop()[...] = jnp.zeros((8, 128), f32)
        kernel(*ins, *results, *rest)
        for copy in last:
            copy.start()
        for copy in last:
            copy.wait()

    return pl.pallas_call(
        run,
        in_specs=[pl.BlockSpec(memory_space=spaces[k]) for k in in_kinds] + [pl.BlockSpec(memory_space=pl.ANY)] * len(after),
        out_specs=[pl.BlockSpec(memory_space=spaces[k]) for k in out_kinds],
        out_shape=[jax.ShapeDtypeStruct(s, d) for s, d in outs],
        scratch_shapes=held + sems + list(scratch),
        compiler_params=pltpu.CompilerParams(vmem_limit_bytes=limit * 2**20),
        cost_estimate=pl.CostEstimate(flops=flops, bytes_accessed=0, transcendentals=0),
        name=name,
    )(*args, *after)


def one_hot(slots_row, count):
    return jnp.where(iota((count, slots_row.shape[1]), 0) == slots_row, 1.0, 0.0).astype(bf16)


def dispatch_kernel(owners, books, half, cluster_ref, item_ref, saved_ref, sent_ref, slot_ref, mark_ref):
    micro, rows = cluster_ref.shape
    width = saved_ref.shape[2]
    each = micro * CAP
    before = jnp.where(iota((rows, rows), 0) < iota((rows, rows), 1), 1.0, 0.0).astype(bf16)
    same = jnp.where(iota((rows, rows), 0) == iota((rows, rows), 1), 1.0, 0.0).astype(bf16)
    kind = iota((128, rows), 0)
    rows_out, codes_out = 0.0, 0.0
    for m in range(micro):
        target, item = cluster_ref[m : m + 1], item_ref[m : m + 1]
        owner, local = target // books, target % books
        marks = jnp.where(iota((owners, rows), 0) == owner, 1.0, 0.0)
        earlier = dot(marks.astype(bf16), before, NN)
        rank = jnp.sum(earlier * marks, axis=0, keepdims=True).astype(jnp.int32)
        slot = owner * each + m * CAP + rank
        slot_ref[m : m + 1] = slot
        code = jnp.where(
            kind == 0,
            local + 1,
            jnp.where(kind == 1, item // half, jnp.where(kind == 2, item % half, jnp.where(kind == 3, owner, 0))),
        )
        code = code.astype(f32).astype(bf16)
        pick = one_hot(slot, owners * each)
        rows_out += dot(pick, saved_ref[m], NN)
        codes_out += dot(pick, code, NT)
        turned = dot(same, code, NT)
        mark_ref[m * rows : (m + 1) * rows] = jnp.broadcast_to(
            turned[:, 3:4] * books + turned[:, 0:1] - 1.0, (rows, 128)
        )
    sent_ref[:, :width] = rows_out.astype(bf16)
    sent_ref[:, width:] = codes_out.astype(bf16)


def first_kernel(group, owners, length_ref, input_ref, saved_ref, table_ref, norm_ref, logit_ref, stat_ref, turned_ref):
    micro, count, depth = input_ref.shape
    for m in range(micro):
        norm_ref[m * count : (m + 1) * count] = row_norm(input_ref[m].astype(f32))[0].astype(bf16)
    lane = iota((16, depth), 1)
    held = jnp.zeros((16, depth), f32)
    for m in range(micro):
        for i in range(SEQS):
            held = jnp.where(lane == m * SEQS + i, length_ref[m, 0, i].astype(f32), held)
    norm_ref[micro * count :] = held.astype(bf16)
    half, width = table_ref.shape
    rows = table_ref[...].astype(f32).reshape(owners, group, half // owners // group, width)
    turned = jnp.concatenate([rows[:, q].reshape(half // group, width) for q in range(group)], axis=0).astype(bf16)
    turned_ref[...] = turned
    logits = dot(saved_ref[...], turned, NT)
    logit_ref[...] = logits
    peak = jnp.max(logits, axis=1, keepdims=True)
    mass = jnp.sum(jnp.exp(logits - peak), axis=1, keepdims=True)
    stat_ref[...] = jnp.where(iota(stat_ref.shape, 1) == 0, peak, mass)


def joined(mine_ref, other_ref):
    peak_a, mass_a = mine_ref[:, 0:1], mine_ref[:, 1:2]
    peak_b, mass_b = other_ref[:, 0:1], other_ref[:, 1:2]
    peak = jnp.maximum(peak_a, peak_b)
    return peak, mass_a * jnp.exp(peak_a - peak) + mass_b * jnp.exp(peak_b - peak)


def top_grad_kernel(group, own, logit_ref, mine_ref, other_ref, mark_ref, table_ref, saved_ref, *out_refs):
    row_ref, grad_refs = out_refs[0], out_refs[1:]
    half = table_ref.shape[0]
    quarter = half // group
    piece = own // group
    base = lax.axis_index("section") * half
    me = member("z")
    peak, mass = joined(mine_ref, other_ref)
    target = mark_ref[:, 0:1].astype(jnp.int32) - base
    total = 0.0
    column = iota((mark_ref.shape[0], quarter), 1)
    for q in range(group):
        index = (column // piece) * own + q * piece + column % piece
        cols = pl.ds(q * quarter, quarter)
        probs = jnp.exp(logit_ref[:, cols] - peak) / mass
        grad = (probs - jnp.where(index == target, 1.0, 0.0)).astype(bf16)
        total += dot(grad, table_ref[cols, :], NN)
        for s in range(group):

            @pl.when(lax.bitwise_xor(me, s) == q)
            def _(s=s, grad=grad):
                grad_refs[s][:, :quarter] = grad
                grad_refs[s][:, quarter:] = saved_ref[...]

    row_ref[...] = total


def table_kernel(owners, *refs):
    *in_refs, out_ref = refs
    quarter = in_refs[0].shape[1] - 256
    total = sum(dot(r[:, :quarter], r[:, quarter:], TN) for r in in_refs)
    left = total[:, :128].reshape(owners, -1, 128)
    right = total[:, 128:].reshape(owners, -1, 128)
    out_ref[...] = jnp.concatenate([left, right], axis=1).astype(bf16)


def masked_product(code_ref, left_ref, width, book_ref, out_ref, dims, group, ready):
    lines = 256
    out_ref[...] = jnp.zeros_like(out_ref)

    def step(i, carry):
        ready(i)
        books = book_ref[pl.ds(i * group, group)]
        if dims == NT:
            right = jnp.concatenate([books[k] for k in range(group)], axis=1)
        else:
            right = books.reshape(-1, books.shape[2])
        for r in range(0, out_ref.shape[0], lines):
            some = pl.ds(r, lines)
            left, code = left_ref[some, :width], code_ref[some, :]
            parts = []
            for k in range(group):
                here = code == (i * group + k + 1).astype(f32).astype(bf16)
                parts.append(jnp.where(here, left, jnp.zeros_like(left)))
            out_ref[some, :] += dot(jnp.concatenate(parts, axis=1), right, dims)
        return carry

    lax.fori_loop(0, book_ref.shape[0] // group, step, 0)


FIRST_LIMIT = 40
GROUP_LIMIT = 40
BOOK_GROUP = 16
BOOK_COPIES = 4


def leaf_scores_kernel(got_in, book_in, out_ref, stat_ref, got_ref, book_ref, code_ref, got_sem, sem):
    width = book_ref.shape[2]
    steps = book_ref.shape[0] // BOOK_GROUP
    piece = BOOK_GROUP // BOOK_COPIES

    def copies(i):
        for j in range(BOOK_COPIES):
            some = pl.ds(i * BOOK_GROUP + j * piece, piece)
            yield pltpu.make_async_copy(book_in.at[some], book_ref.at[some], sem.at[i, j])

    got_copy = pltpu.make_async_copy(got_in, got_ref, got_sem)
    got_copy.start()
    for i in range(2):
        for copy in copies(i):
            copy.start()
    got_copy.wait()
    code_ref[...] = jnp.broadcast_to(got_ref[:, width : width + 1], code_ref.shape)

    def ready(i):
        for copy in copies(i):
            copy.wait()

        @pl.when(i + 2 < steps)
        def _():
            for copy in copies(i + 2):
                copy.start()

    masked_product(code_ref, got_ref, width, book_ref, out_ref, NT, BOOK_GROUP, ready)
    scores = out_ref[...]
    peak = jnp.max(scores, axis=1, keepdims=True)
    mass = jnp.sum(jnp.exp(scores - peak), axis=1, keepdims=True)
    stat_ref[...] = jnp.where(iota(stat_ref.shape, 1) == 0, peak, mass)


def leaf_back_kernel(got_ref, score_ref, mine_ref, other_ref, book_ref, back_ref, grad_ref, code_ref, total_ref):
    items, width = book_ref.shape[1:]
    code = got_ref[:, width : width + 1]
    code_ref[...] = jnp.broadcast_to(code, code_ref.shape)
    high = got_ref[:, width + 1 : width + 2].astype(f32).astype(jnp.int32)
    low = got_ref[:, width + 2 : width + 3].astype(f32).astype(jnp.int32)
    peak, mass = joined(mine_ref, other_ref)
    probs = jnp.exp(score_ref[...] - peak) / mass
    hit = (iota(probs.shape, 1) == low) & (high == lax.axis_index("section"))
    grad = jnp.where(code.astype(f32) > 0, probs - jnp.where(hit, 1.0, 0.0), 0.0)
    grad_ref[...] = grad.astype(bf16)
    masked_product(code_ref, grad_ref, items, book_ref, total_ref, NN, 32, lambda i: None)
    back_ref[...] = total_ref[...].astype(bf16)


def leaf_book_kernel(got_ref, grad_ref, out_ref, code_ref, turned_ref, held_ref, sem):
    books, items, width = out_ref.shape
    group = books // sem.shape[0]
    slots = got_ref.shape[0]
    turned_ref[...] = grad_ref[...].astype(f32).T.astype(bf16)
    code_ref[...] = jnp.broadcast_to(got_ref[:, width : width + 1].astype(f32), (slots, items)).T.astype(bf16)
    rows = got_ref[:, :width]
    copies = []
    for i in range(books // group):
        some = pl.ds(i * group, group)
        turned, code = turned_ref[...], code_ref[...]
        parts = []
        for k in range(group):
            here = code == (i * group + k + 1)
            parts.append(jnp.where(here, turned, jnp.zeros_like(turned)))
        grads = dot(jnp.concatenate(parts, axis=0), rows, NN)
        held_ref[some] = grads.reshape(group, items, width).astype(bf16)
        copies.append(pltpu.make_async_copy(held_ref.at[some], out_ref.at[some], sem.at[i]))
        copies[-1].start()
    for copy in copies:
        copy.wait()


def leaf_scores(got, book, after):
    books, items, width = book.shape
    slots = got.shape[0]
    return call(
        leaf_scores_kernel,
        "leaf_scores",
        [((slots, items), f32), ((slots, 128), f32), (got.shape, bf16), (book.shape, bf16)],
        (got, book),
        "RR VVVV", limit=42,
        flops=2 * slots * books * items * width,
        scratch=[
            pltpu.VMEM((slots, width), bf16),
            pltpu.SemaphoreType.DMA,
            pltpu.SemaphoreType.DMA((books // BOOK_GROUP, BOOK_COPIES)),
        ],
        after=after,
    )


def leaf_back(got, scores, mine, other, book, after):
    books, items, width = book.shape
    slots = got.shape[0]
    return call(
        leaf_back_kernel,
        "leaf_back",
        [((slots, width), bf16), ((slots, items), bf16)],
        (got, scores, mine, other, book),
        "VVVVV HH",
        limit=28,
        scratch=[pltpu.VMEM((slots, items), bf16), pltpu.VMEM((slots, width), f32)],
        after=after,
    )


def leaf_book(got, grads, books, width, after):
    slots, items = grads.shape
    group = 4
    return call(
        leaf_book_kernel,
        "leaf_book",
        [((books, items, width), bf16)],
        (got, grads),
        "HH R",
        scratch=[
            pltpu.VMEM((items, slots), bf16),
            pltpu.VMEM((items, slots), bf16),
            pltpu.VMEM((books, items, width), bf16),
            pltpu.SemaphoreType.DMA((books // group,)),
        ],
        after=after,
    )[0]


def slope_of(argument, logistic):
    return logistic * (1.0 + argument * (1.0 - logistic))


def seq_mask(sizes, rows):
    row, col = iota((rows, rows), 0), iota((rows, rows), 1)
    row_seg, col_seg, end = 0, 0, 0
    for size in sizes:
        end = end + size
        row_seg += jnp.where(row >= end, 1, 0)
        col_seg += jnp.where(col >= end, 1, 0)
    return jnp.where((row_seg == col_seg) & (col <= row), 1.0 / SEQ_MOST, 0.0)


def held_sizes(held, m):
    held = held.astype(f32)[0:1].astype(jnp.int32)
    return [held[:, m * SEQS + i : m * SEQS + i + 1] for i in range(SEQS)]


def attend_all(acts, masks):
    scores = [dot(query, key, NT) for _, _, query, key in acts]
    logistics = [jax.nn.sigmoid(score) for score in scores]
    attention = [(a * b * mask).astype(bf16) for a, b, mask in zip(scores, logistics, masks)]
    mixed = [dot(a, act[1], NN) for a, act in zip(attention, acts)]
    back = [slope_of(a, b) * mask for a, b, mask in zip(scores, logistics, masks)]
    normed = [row_norm(one) for one in mixed]
    return [(a, b, n, jnp.broadcast_to(i, n.shape)) for a, b, (n, i) in zip(attention, back, normed)]


def my_head():
    return pl.ds(pl.multiple_of(member("y") * HEAD_DIM, HEAD_DIM), HEAD_DIM)


def head_weight_kernel(weight_in, out_ref, part_ref, flat_ref, sem):
    copy = pltpu.make_async_copy(weight_in.at[:, :, my_head()], part_ref, sem)
    copy.start()
    copy.wait()
    flat_ref[...] = part_ref[...].astype(f32).reshape(flat_ref.shape)
    depth, parts = weight_in.shape[:2]
    for t in range(parts):
        out_ref[:, t * HEAD_DIM : (t + 1) * HEAD_DIM] = flat_ref[pl.ds(t, depth, stride=parts), :].astype(bf16)


def group_forward_kernel(*refs):
    *norm_ins, weight_in, act_ref, slope_ref, att_ref, back_ref, out_ref, inverse_ref, prod_ref = refs[:-3]
    weight_ref, norm_ref, sem = refs[-3:]
    pairs = [(weight_in, weight_ref)] + [(one, norm_ref.at[s]) for s, one in enumerate(norm_ins)]
    copies = [pltpu.make_async_copy(a, b, sem.at[i]) for i, (a, b) in enumerate(pairs)]
    for copy in copies:
        copy.start()
    for copy in copies:
        copy.wait()
    rows = att_ref.shape[1]
    total = out_ref.shape[0] // len(norm_ins)
    weight = weight_ref[...]
    acts, masks, spans = [], [], []
    for s in range(len(norm_ins)):
        for m in range(total // rows):
            lines = pl.ds(s * total + m * rows, rows)
            pre_act = dot(norm_ref[s, m * rows : (m + 1) * rows, :], weight, NN)
            logistic = jax.nn.sigmoid(pre_act)
            act = (pre_act * logistic).astype(bf16)
            act_ref[lines, :] = act
            slope_ref[lines, :] = slope_of(pre_act, logistic)
            spans.append(lines)
            masks.append(seq_mask(held_sizes(norm_ref[s, total:, :128], m), rows))
            acts.append([act[:, t * HEAD_DIM : (t + 1) * HEAD_DIM] for t in range(4)])
    for lines, act, result in zip(spans, acts, attend_all(acts, masks)):
        att_ref[lines, :], back_ref[lines, :], out_ref[lines, :], inverse_ref[lines, :] = result
        prod_ref[lines, :] = (result[2] * act[0].astype(f32)).astype(bf16)


def attend_back_all(incoming, acts, results):
    mixed = [
        norm_back(a * act[0].astype(f32), normed, inverse).astype(bf16)
        for a, act, (_, _, normed, inverse) in zip(incoming, acts, results)
    ]
    grads = [dot(a, act[1], NT) for a, act in zip(mixed, acts)]
    values = [dot(result[0], a, TN) for result, a in zip(results, mixed)]
    grads = [(a * result[1]).astype(bf16) for a, result in zip(grads, results)]
    queries = [dot(a, act[3], NN) for a, act in zip(grads, acts)]
    keys = [dot(a, act[2], TN) for a, act in zip(grads, acts)]
    gates = [a * result[2] for a, result in zip(incoming, results)]
    return list(zip(gates, values, queries, keys))


def rows_kernel(slot_ref, returned_ref, out_ref):
    micro, rows = slot_ref.shape
    for m in range(micro):
        lines = pl.ds(m * rows, rows)
        pick = one_hot(slot_ref[m : m + 1], returned_ref.shape[0])
        out_ref[lines, :] = dot(pick, returned_ref[...], TN)


def add_kernel(mine_ref, other_ref, top_ref, out_ref):
    out_ref[...] = (mine_ref[...] + other_ref[...] + top_ref[...]).astype(bf16)


def trunk_kernel(length_ref, norm_ref, row_ref, proj_ref, mix_ref, weight_in, og_ref, part_ref, pre_ref, weight_ref, sem):
    copies = [pltpu.make_async_copy(weight_in.at[t], weight_ref.at[t], sem.at[t]) for t in range(4)]
    for copy in copies:
        copy.start()
    rows = HEAD_DIM
    total, cols = row_ref.shape[0], weight_ref.shape[2]
    out_grad = dot(row_ref[...], proj_ref[...], NT).astype(bf16)
    og_ref[...] = out_grad
    grad_product = dot(out_grad, mix_ref[...], NT)
    for copy in copies:
        copy.wait()
    for m in range(total // rows):
        lines = pl.ds(m * rows, rows)
        normed = norm_ref[lines, :]
        acts, slopes = [], []
        for t in range(4):
            pre_act = dot(normed, weight_ref[t], NN)
            logistic = jax.nn.sigmoid(pre_act)
            acts.append((pre_act * logistic).astype(bf16))
            slopes.append(slope_of(pre_act, logistic))
        heads = [slice(h * HEAD_DIM, (h + 1) * HEAD_DIM) for h in range(cols // HEAD_DIM)]
        acts = [[act[:, lanes] for act in acts] for lanes in heads]
        masks = [seq_mask([length_ref[m, 0, i] for i in range(SEQS)], rows)] * len(heads)
        incoming = [grad_product[m * rows : (m + 1) * rows, lanes] for lanes in heads]
        for lanes, grads in zip(heads, attend_back_all(incoming, acts, attend_all(acts, masks))):
            for t, grad in enumerate(grads):
                pre_ref[t, lines, lanes] = (grad * slopes[t][:, lanes]).astype(bf16)
    part_ref[...] = sum(dot(pre_ref[t], weight_ref[t], NT) for t in range(4))


def inputs_kernel(input_ref, og_ref, mine_ref, other_ref, out_ref):
    micro, rows, _ = input_ref.shape
    for m in range(micro):
        lines = pl.ds(m * rows, rows)
        normed, inverse = row_norm(input_ref[m].astype(f32))
        grad = norm_back(mine_ref[lines, :] + other_ref[lines, :], normed, inverse)
        out_ref[m] = (og_ref[lines, :].astype(f32) + grad).astype(bf16)


def weights_kernel(group, owners, *refs):
    row_refs, norm_refs = refs[:group], refs[group : 2 * group]
    act_ref, slope_ref, att_ref, back_ref, out_ref, inverse_ref, prod_ref, proj_ref, mix_ref, table_ref, packed_ref = refs[2 * group :]
    total = row_refs[0].shape[0]
    rows = att_ref.shape[1]
    cols = act_ref.shape[1]
    count = total // rows
    mix = mix_ref[my_head(), :]
    mixing, expand = 0.0, 0.0
    spans, incoming = [], []
    for s in range(group):
        out_grad = dot(row_refs[s][...], proj_ref[...], NT).astype(bf16)
        mixing += dot(out_grad, prod_ref[s * total : (s + 1) * total, :], TN)
        grad_product = dot(out_grad, mix, NT)
        for m in range(count):
            spans.append(pl.ds(s * total + m * rows, rows))
            incoming.append(grad_product[m * rows : (m + 1) * rows])
    packed_ref[:, :, cols : cols + HEAD_DIM] = mixing.reshape(owners, -1, HEAD_DIM).astype(bf16)
    packed_ref[:, :, cols + HEAD_DIM :] = table_ref[...]
    acts = [[act_ref[lines, t * HEAD_DIM : (t + 1) * HEAD_DIM] for t in range(4)] for lines in spans]
    results = [(att_ref[lines, :], back_ref[lines, :], out_ref[lines, :], inverse_ref[lines, :]) for lines in spans]
    grads = attend_back_all(incoming, acts, results)
    pre = [(jnp.concatenate(grad, axis=1) * slope_ref[lines, :]).astype(bf16) for grad, lines in zip(grads, spans)]
    for s in range(group):
        expand += dot(norm_refs[s][:total, :], jnp.concatenate(pre[s * count : (s + 1) * count], axis=0), TN)
    packed_ref[:, :, :cols] = expand.reshape(owners, -1, cols).astype(bf16)


def final_kernel(group, in_ref, expand_ref, mixing_ref, table_ref):
    cols = expand_ref.shape[2]
    side = range(group)
    for g in side:
        sources = [(y * group + z) * group + x for y in side for z in side for x in side if x % 2 + 2 * (y % 2) == g]
        total = sum(in_ref[i, :, : cols + HEAD_DIM].astype(f32) for i in sources)
        head = pl.ds(g * HEAD_DIM, HEAD_DIM)
        for t in range(4):
            expand_ref[:, t, head] = total[:, t * HEAD_DIM : (t + 1) * HEAD_DIM]
        mixing_ref[:, head] = total[:, cols:]
    lanes = pl.ds(cols + HEAD_DIM, HEAD_DIM)
    for q in side:
        sources = [(y * group + z) * group + x for y in side for z in side for x in side if x % 2 + 2 * (z % 2) == q]
        total = sum(in_ref[i, :, lanes].astype(f32) for i in sources)
        half = total.shape[0] // 2
        table_ref[q * half : (q + 1) * half, :HEAD_DIM] = total[:half]
        table_ref[q * half : (q + 1) * half, HEAD_DIM:] = total[half:]


def body(
    inputs,
    lengths,
    expand_weight,
    mixing_weight,
    projection,
    saved_rows,
    cluster_ids,
    item_ids,
    top_table,
    codebook,
):
    micro, rows, model_width = inputs.shape
    total = micro * rows
    owners = lax.axis_size(DEV)
    group = lax.axis_size("x")
    half_clusters, width = top_table.shape
    books, items, _ = codebook.shape
    cols = expand_weight.shape[2]
    slots = owners * micro * CAP
    own = half_clusters // owners
    saved = saved_rows.reshape(total, width)

    sent, slot_ids, marks = call(
        functools.partial(dispatch_kernel, owners, books, items),
        "dispatch",
        [((slots, width + 128), bf16), ((micro, rows), jnp.int32), ((total, 128), f32)],
        (cluster_ids, item_ids, saved_rows),
        "HHH HVH", limit=56,
    )
    got = lax.all_to_all(sent.reshape(owners, slots // owners, -1), DEV, 0, 0, tiled=True).reshape(slots, -1)

    normed, logits, stats, table = call(
        functools.partial(first_kernel, group, owners),
        "norms_and_logits",
        [
            ((total + 16, model_width), bf16),
            ((total, half_clusters), f32),
            ((total, 128), f32),
            (top_table.shape, bf16),
        ],
        (lengths, inputs, saved, top_table),
        "SHHH VVVV",
        limit=FIRST_LIMIT,
        after=(slot_ids,),
    )
    normed_all = [normed] + [from_member(normed, "y", s) for s in range(1, group)]
    row_top, *top_grads, top_token = call(
        functools.partial(top_grad_kernel, group, own),
        "top_grads",
        [((total, width), f32)] + [((total, half_clusters // group + width), bf16)] * group,
        (logits, stats, swap(stats), marks, table, saved),
        "VVVHHH " + "H" * (1 + group),
        limit=40,
        token=True,
    )
    top_all = [top_grads[0]] + [from_member(top_grads[s], "z", s) for s in range(1, group)]

    leaf, leaf_stats, got_held, book_held = leaf_scores(got, codebook, (top_token, normed[:8, :128]))
    back, leaf_grad = leaf_back(
        got_held, leaf, leaf_stats, swap(leaf_stats), book_held, ()
    )
    returned = lax.all_to_all(back.reshape(owners, slots // owners, width), DEV, 0, 0, tiled=True)

    row_top = row_top + swap(row_top)
    head_weight, head_token = call(
        head_weight_kernel,
        "head_weight",
        [((model_width, 4 * HEAD_DIM), bf16)],
        (expand_weight,),
        "R H",
        scratch=[
            pltpu.VMEM((model_width, 4, HEAD_DIM), bf16),
            pltpu.VMEM((model_width * 4, HEAD_DIM), f32),
            pltpu.SemaphoreType.DMA,
        ],
        after=(back, sum(a[:8, :128] for a in normed_all[1:])),
        token=True,
    )

    table_part, table_token = call(
        functools.partial(table_kernel, owners),
        "table_part",
        [((owners, 16, 128), bf16)],
        top_all,
        "V" * group + " V",
        limit=16,
        after=(back, head_token),
        token=True,
    )

    (row_part,) = call(
        rows_kernel,
        "rows",
        [((total, width), f32)],
        (slot_ids, returned.reshape(slots, width)),
        "VH V",
        limit=28,
        after=(table_token,),
    )
    (row_grad,) = call(add_kernel, "row_grad", [((total, width), bf16)], (row_part, swap(row_part), row_top), "VVV V", limit=28)
    row_all = [row_grad] + [from_member(row_grad, "y", s) for s in range(1, group)]

    group_rows = group * total
    group_forward = call(
        group_forward_kernel,
        "group_forward",
        [
            ((group_rows, 4 * HEAD_DIM), bf16),
            ((group_rows, 4 * HEAD_DIM), f32),
            ((group_rows, rows), bf16),
            ((group_rows, rows), f32),
            ((group_rows, HEAD_DIM), f32),
            ((group_rows, HEAD_DIM), f32),
            ((group_rows, HEAD_DIM), bf16),
        ],
        (*normed_all, head_weight),
        "R" * (group + 1) + " " + "V" * 7,
        limit=GROUP_LIMIT,
        after=(row_grad,),
        scratch=[
            pltpu.VMEM(head_weight.shape, bf16),
            pltpu.VMEM((group, total + 16, model_width), bf16),
            pltpu.SemaphoreType.DMA((group + 1,)),
        ],
    )

    (packed,) = call(
        functools.partial(weights_kernel, group, owners),
        "weight_parts",
        [((owners, model_width // owners, cols + 2 * HEAD_DIM), bf16)],
        (*row_all, *normed_all, *group_forward, projection, mixing_weight, table_part),
        "V" * (2 * group + 10) + " H",
        limit=28,
    )
    arrived = lax.all_to_all(packed, DEV, 0, 0, tiled=True)

    late_weight, _ = lax.optimization_barrier((expand_weight, packed))
    weight = late_weight.swapaxes(0, 1)
    out_grad, grad_part = call(
        trunk_kernel,
        "trunk",
        [((total, model_width), bf16), ((total, model_width), f32)],
        (lengths, normed, row_grad, projection, mixing_weight, weight),
        "SHHHHR VV",
        limit=48,
        scratch=[pltpu.VMEM((4, total, cols), bf16), pltpu.VMEM(weight.shape, bf16), pltpu.SemaphoreType.DMA((4,))],
        after=(packed,),
    )
    (grad_inputs,) = call(
        inputs_kernel, "input_grads", [(inputs.shape, bf16)], (inputs, out_grad, grad_part, swap(grad_part)), "HVVV H", limit=48
    )
    book_grads = leaf_book(got, leaf_grad, books, width, (packed,))
    share = model_width // owners
    expand, mixing, table_share = call(
        functools.partial(final_kernel, group),
        "weight_sums",
        [((share, 4, cols), f32), ((share, cols), f32), ((own, width), f32)],
        (arrived,),
        "V HHH",
        limit=28,
    )
    return grad_inputs, expand, mixing.T, table_share, book_grads


def solution(mesh):
    grid = Mesh(mesh.devices.reshape(2, 4, 4, 4), ("section",) + DEV)
    return jax.shard_map(
        body,
        mesh=grid,
        in_specs=(
            P(None, DEV, None),
            P(None, DEV, None),
            P(None, None, "section"),
            P("section", None),
            P(),
            P(None, DEV, None),
            P(None, DEV),
            P(None, DEV),
            P("section", None),
            P(DEV, "section", None),
        ),
        out_specs=(
            P(None, DEV, None),
            P(DEV, None, "section"),
            P("section", DEV),
            P(("section",) + DEV, None),
            P(DEV, "section", None),
        ),
        check_vma=False,
    )
```

```python
import functools

import jax
import jax.numpy as jnp
from jax import lax
from jax.experimental import pallas as pl
from jax.experimental.pallas import tpu as pltpu
from jax.sharding import Mesh
from jax.sharding import PartitionSpec as P

HEAD_DIM = 128
SEQ_MOST = 64
SEQS = 4
CAP = 4
eps = 1e-05
DEV = ("y", "z", "x")
f32 = jnp.float32
bf16 = jnp.bfloat16
NN = ((1,), (0,))
NT = ((1,), (1,))
TN = ((0,), (0,))


def swap(part):
    return lax.ppermute(part, "section", [(0, 1), (1, 0)])


def shifted(part, axis, step):
    count = lax.axis_size(axis)
    return lax.ppermute(part, axis, [(i, (i + step) % count) for i in range(count)])


def member():
    return lax.rem(lax.axis_index("x"), 2) + 2 * lax.rem(lax.axis_index("y"), 2)


def from_member(part, other):
    count = lax.axis_size("x")
    flip = count * (other // 2) + other % 2
    return lax.ppermute(part, ("y", "x"), [(i, i ^ flip) for i in range(lax.axis_size("y") * count)])


def dot(left, right, dims):
    return lax.dot_general(left, right, (dims, ((), ())), preferred_element_type=f32)


def iota(shape, dim):
    return lax.broadcasted_iota(jnp.int32, shape, dim)


def row_norm(argument):
    row_mean = jnp.mean(argument, axis=-1, keepdims=True)
    centered = argument - row_mean
    variance = jnp.mean(centered * centered, axis=-1, keepdims=True)
    inverse = lax.rsqrt(variance + eps)
    return (centered * inverse, inverse)


def norm_back(incoming, normed, inverse):
    mean_in = jnp.mean(incoming, axis=-1, keepdims=True)
    mean_dot = jnp.mean(incoming * normed, axis=-1, keepdims=True)
    return (incoming - mean_in - normed * mean_dot) * inverse


def call(kernel, name, outs, args, kinds, after=(), scratch=(), limit=56, flops=0, token=False):
    in_kinds, out_kinds = kinds.split()
    if token:
        outs, out_kinds = [*outs, ((8, 128), f32)], out_kinds + "V"
    assert len(in_kinds) == len(args) and len(out_kinds) == len(outs), name
    spaces = {"V": pltpu.VMEM, "S": pltpu.SMEM, "H": pl.ANY, "R": pl.ANY}
    held = [pltpu.VMEM(a.shape, a.dtype) for a, k in zip(args, in_kinds) if k == "H"]
    held += [pltpu.VMEM(s, d) for (s, d), k in zip(outs, out_kinds) if k == "H"]
    sems = [pltpu.SemaphoreType.DMA((len(held),))] if held else []

    def run(*refs):
        ins = list(refs[: len(args)])
        refs = refs[len(args) + len(after) :]
        results = list(refs[: len(outs)])
        buffers = list(refs[len(outs) : len(outs) + len(held)])
        rest = refs[len(outs) + len(held) + len(sems) :]
        sem = refs[len(outs) + len(held)] if held else None
        count = 0
        first, last = [], []
        for i, kind in enumerate(in_kinds):
            if kind == "H":
                first.append(pltpu.make_async_copy(ins[i], buffers[count], sem.at[count]))
                first[-1].start()
                ins[i] = buffers[count]
                count += 1
        for i, kind in enumerate(out_kinds):
            if kind == "H":
                last.append(pltpu.make_async_copy(buffers[count], results[i], sem.at[count]))
                results[i] = buffers[count]
                count += 1
        for copy in first:
            copy.wait()
        if token:
            results.pop()[...] = jnp.zeros((8, 128), f32)
        kernel(*ins, *results, *rest)
        for copy in last:
            copy.start()
        for copy in last:
            copy.wait()

    return pl.pallas_call(
        run,
        in_specs=[pl.BlockSpec(memory_space=spaces[k]) for k in in_kinds] + [pl.BlockSpec(memory_space=pl.ANY)] * len(after),
        out_specs=[pl.BlockSpec(memory_space=spaces[k]) for k in out_kinds],
        out_shape=[jax.ShapeDtypeStruct(s, d) for s, d in outs],
        scratch_shapes=held + sems + list(scratch),
        compiler_params=pltpu.CompilerParams(vmem_limit_bytes=limit * 2**20),
        cost_estimate=pl.CostEstimate(flops=flops, bytes_accessed=0, transcendentals=0),
        name=name,
    )(*args, *after)


def one_hot(slots_row, count):
    return jnp.where(iota((count, slots_row.shape[1]), 0) == slots_row, 1.0, 0.0).astype(bf16)


def dispatch_kernel(owners, books, half, cluster_ref, item_ref, saved_ref, sent_ref, slot_ref, mark_ref):
    micro, rows = cluster_ref.shape
    width = saved_ref.shape[2]
    each = micro * CAP
    before = jnp.where(iota((rows, rows), 0) < iota((rows, rows), 1), 1.0, 0.0).astype(bf16)
    same = jnp.where(iota((rows, rows), 0) == iota((rows, rows), 1), 1.0, 0.0).astype(bf16)
    kind = iota((128, rows), 0)
    rows_out, codes_out = 0.0, 0.0
    for m in range(micro):
        target, item = cluster_ref[m : m + 1], item_ref[m : m + 1]
        owner, local = target // books, target % books
        marks = jnp.where(iota((owners, rows), 0) == owner, 1.0, 0.0)
        earlier = dot(marks.astype(bf16), before, NN)
        rank = jnp.sum(earlier * marks, axis=0, keepdims=True).astype(jnp.int32)
        slot = owner * each + m * CAP + rank
        slot_ref[m : m + 1] = slot
        code = jnp.where(
            kind == 0,
            local + 1,
            jnp.where(kind == 1, item // half, jnp.where(kind == 2, item % half, jnp.where(kind == 3, owner, 0))),
        )
        code = code.astype(f32).astype(bf16)
        pick = one_hot(slot, owners * each)
        rows_out += dot(pick, saved_ref[m], NN)
        codes_out += dot(pick, code, NT)
        turned = dot(same, code, NT)
        mark_ref[m * rows : (m + 1) * rows] = jnp.broadcast_to(
            turned[:, 3:4] * books + turned[:, 0:1] - 1.0, (rows, 128)
        )
    sent_ref[:, :width] = rows_out.astype(bf16)
    sent_ref[:, width:] = codes_out.astype(bf16)


def first_kernel(group, owners, length_ref, input_ref, saved_ref, table_ref, norm_ref, logit_ref, stat_ref, turned_ref):
    micro, count, depth = input_ref.shape
    for m in range(micro):
        norm_ref[m * count : (m + 1) * count] = row_norm(input_ref[m].astype(f32))[0].astype(bf16)
    lane = iota((16, depth), 1)
    held = jnp.zeros((16, depth), f32)
    for m in range(micro):
        for i in range(SEQS):
            held = jnp.where(lane == m * SEQS + i, length_ref[m, 0, i].astype(f32), held)
    norm_ref[micro * count :] = held.astype(bf16)
    half, width = table_ref.shape
    rows = table_ref[...].astype(f32).reshape(owners, group, half // owners // group, width)
    turned = jnp.concatenate([rows[:, q].reshape(half // group, width) for q in range(group)], axis=0).astype(bf16)
    turned_ref[...] = turned
    logits = dot(saved_ref[...], turned, NT)
    logit_ref[...] = logits
    peak = jnp.max(logits, axis=1, keepdims=True)
    mass = jnp.sum(jnp.exp(logits - peak), axis=1, keepdims=True)
    stat_ref[...] = jnp.where(iota(stat_ref.shape, 1) == 0, peak, mass)


def joined(mine_ref, other_ref):
    peak_a, mass_a = mine_ref[:, 0:1], mine_ref[:, 1:2]
    peak_b, mass_b = other_ref[:, 0:1], other_ref[:, 1:2]
    peak = jnp.maximum(peak_a, peak_b)
    return peak, mass_a * jnp.exp(peak_a - peak) + mass_b * jnp.exp(peak_b - peak)


def top_grad_kernel(group, own, logit_ref, mine_ref, other_ref, mark_ref, table_ref, saved_ref, *out_refs):
    row_ref, grad_refs = out_refs[0], out_refs[1:]
    half = table_ref.shape[0]
    quarter = half // group
    piece = own // group
    base = lax.axis_index("section") * half
    me = lax.axis_index("z")
    peak, mass = joined(mine_ref, other_ref)
    target = mark_ref[:, 0:1].astype(jnp.int32) - base
    total = 0.0
    column = iota((mark_ref.shape[0], quarter), 1)
    for q in range(group):
        index = (column // piece) * own + q * piece + column % piece
        cols = pl.ds(q * quarter, quarter)
        probs = jnp.exp(logit_ref[:, cols] - peak) / mass
        grad = (probs - jnp.where(index == target, 1.0, 0.0)).astype(bf16)
        total += dot(grad, table_ref[cols, :], NN)
        for s in range(group):

            @pl.when(lax.rem(me + s, group) == q)
            def _(s=s, grad=grad):
                grad_refs[s][:, :quarter] = grad
                grad_refs[s][:, quarter:] = saved_ref[...]

    row_ref[...] = total


def table_kernel(owners, *refs):
    *in_refs, out_ref = refs
    quarter = in_refs[0].shape[1] - 256
    total = sum(dot(r[:, :quarter], r[:, quarter:], TN) for r in in_refs)
    left = total[:, :128].reshape(owners, -1, 128)
    right = total[:, 128:].reshape(owners, -1, 128)
    out_ref[...] = jnp.concatenate([left, right], axis=1).astype(bf16)


def masked_product(code_ref, left_ref, width, book_ref, out_ref, dims, group, ready):
    lines = 256
    out_ref[...] = jnp.zeros_like(out_ref)

    def step(i, carry):
        ready(i)
        books = book_ref[pl.ds(i * group, group)]
        if dims == NT:
            right = jnp.concatenate([books[k] for k in range(group)], axis=1)
        else:
            right = books.reshape(-1, books.shape[2])
        for r in range(0, out_ref.shape[0], lines):
            some = pl.ds(r, lines)
            left, code = left_ref[some, :width], code_ref[some, :]
            parts = []
            for k in range(group):
                here = code == (i * group + k + 1).astype(f32).astype(bf16)
                parts.append(jnp.where(here, left, jnp.zeros_like(left)))
            out_ref[some, :] += dot(jnp.concatenate(parts, axis=1), right, dims)
        return carry

    lax.fori_loop(0, book_ref.shape[0] // group, step, 0)


FIRST_LIMIT = 40
GROUP_LIMIT = 40
BOOK_GROUP = 16
BOOK_COPIES = 4


def leaf_scores_kernel(got_in, book_in, out_ref, stat_ref, got_ref, book_ref, code_ref, got_sem, sem):
    width = book_ref.shape[2]
    steps = book_ref.shape[0] // BOOK_GROUP
    piece = BOOK_GROUP // BOOK_COPIES

    def copies(i):
        for j in range(BOOK_COPIES):
            some = pl.ds(i * BOOK_GROUP + j * piece, piece)
            yield pltpu.make_async_copy(book_in.at[some], book_ref.at[some], sem.at[i, j])

    got_copy = pltpu.make_async_copy(got_in, got_ref, got_sem)
    got_copy.start()
    for i in range(2):
        for copy in copies(i):
            copy.start()
    got_copy.wait()
    code_ref[...] = jnp.broadcast_to(got_ref[:, width : width + 1], code_ref.shape)

    def ready(i):
        for copy in copies(i):
            copy.wait()

        @pl.when(i + 2 < steps)
        def _():
            for copy in copies(i + 2):
                copy.start()

    masked_product(code_ref, got_ref, width, book_ref, out_ref, NT, BOOK_GROUP, ready)
    scores = out_ref[...]
    peak = jnp.max(scores, axis=1, keepdims=True)
    mass = jnp.sum(jnp.exp(scores - peak), axis=1, keepdims=True)
    stat_ref[...] = jnp.where(iota(stat_ref.shape, 1) == 0, peak, mass)


def leaf_back_kernel(got_ref, score_ref, mine_ref, other_ref, book_ref, back_ref, grad_ref, code_ref, total_ref):
    items, width = book_ref.shape[1:]
    code = got_ref[:, width : width + 1]
    code_ref[...] = jnp.broadcast_to(code, code_ref.shape)
    high = got_ref[:, width + 1 : width + 2].astype(f32).astype(jnp.int32)
    low = got_ref[:, width + 2 : width + 3].astype(f32).astype(jnp.int32)
    peak, mass = joined(mine_ref, other_ref)
    probs = jnp.exp(score_ref[...] - peak) / mass
    hit = (iota(probs.shape, 1) == low) & (high == lax.axis_index("section"))
    grad = jnp.where(code.astype(f32) > 0, probs - jnp.where(hit, 1.0, 0.0), 0.0)
    grad_ref[...] = grad.astype(bf16)
    masked_product(code_ref, grad_ref, items, book_ref, total_ref, NN, 32, lambda i: None)
    back_ref[...] = total_ref[...].astype(bf16)


def leaf_book_kernel(got_ref, grad_ref, out_ref, code_ref, turned_ref, held_ref, sem):
    books, items, width = out_ref.shape
    group = books // sem.shape[0]
    slots = got_ref.shape[0]
    turned_ref[...] = grad_ref[...].astype(f32).T.astype(bf16)
    code_ref[...] = jnp.broadcast_to(got_ref[:, width : width + 1].astype(f32), (slots, items)).T.astype(bf16)
    rows = got_ref[:, :width]
    copies = []
    for i in range(books // group):
        some = pl.ds(i * group, group)
        turned, code = turned_ref[...], code_ref[...]
        parts = []
        for k in range(group):
            here = code == (i * group + k + 1)
            parts.append(jnp.where(here, turned, jnp.zeros_like(turned)))
        grads = dot(jnp.concatenate(parts, axis=0), rows, NN)
        held_ref[some] = grads.reshape(group, items, width).astype(bf16)
        copies.append(pltpu.make_async_copy(held_ref.at[some], out_ref.at[some], sem.at[i]))
        copies[-1].start()
    for copy in copies:
        copy.wait()


def leaf_scores(got, book, after):
    books, items, width = book.shape
    slots = got.shape[0]
    return call(
        leaf_scores_kernel,
        "leaf_scores",
        [((slots, items), f32), ((slots, 128), f32), (got.shape, bf16), (book.shape, bf16)],
        (got, book),
        "RR VVVV", limit=42,
        flops=2 * slots * books * items * width,
        scratch=[
            pltpu.VMEM((slots, width), bf16),
            pltpu.SemaphoreType.DMA,
            pltpu.SemaphoreType.DMA((books // BOOK_GROUP, BOOK_COPIES)),
        ],
        after=after,
    )


def leaf_back(got, scores, mine, other, book, after):
    books, items, width = book.shape
    slots = got.shape[0]
    return call(
        leaf_back_kernel,
        "leaf_back",
        [((slots, width), bf16), ((slots, items), bf16)],
        (got, scores, mine, other, book),
        "VVVVV HH",
        limit=28,
        scratch=[pltpu.VMEM((slots, items), bf16), pltpu.VMEM((slots, width), f32)],
        after=after,
    )


def leaf_book(got, grads, books, width, after):
    slots, items = grads.shape
    group = 4
    return call(
        leaf_book_kernel,
        "leaf_book",
        [((books, items, width), bf16)],
        (got, grads),
        "HH R",
        scratch=[
            pltpu.VMEM((items, slots), bf16),
            pltpu.VMEM((items, slots), bf16),
            pltpu.VMEM((books, items, width), bf16),
            pltpu.SemaphoreType.DMA((books // group,)),
        ],
        after=after,
    )[0]


def slope_of(argument, logistic):
    return logistic * (1.0 + argument * (1.0 - logistic))


def seq_mask(sizes, rows):
    row, col = iota((rows, rows), 0), iota((rows, rows), 1)
    row_seg, col_seg, end = 0, 0, 0
    for size in sizes:
        end = end + size
        row_seg += jnp.where(row >= end, 1, 0)
        col_seg += jnp.where(col >= end, 1, 0)
    return jnp.where((row_seg == col_seg) & (col <= row), 1.0 / SEQ_MOST, 0.0)


def held_sizes(held, m):
    held = held.astype(f32)[0:1].astype(jnp.int32)
    return [held[:, m * SEQS + i : m * SEQS + i + 1] for i in range(SEQS)]


def attend_all(acts, masks):
    scores = [dot(query, key, NT) for _, _, query, key in acts]
    logistics = [jax.nn.sigmoid(score) for score in scores]
    attention = [(a * b * mask).astype(bf16) for a, b, mask in zip(scores, logistics, masks)]
    mixed = [dot(a, act[1], NN) for a, act in zip(attention, acts)]
    back = [slope_of(a, b) * mask for a, b, mask in zip(scores, logistics, masks)]
    normed = [row_norm(one) for one in mixed]
    return [(a, b, n, jnp.broadcast_to(i, n.shape)) for a, b, (n, i) in zip(attention, back, normed)]


def my_head():
    return pl.ds(pl.multiple_of(member() * HEAD_DIM, HEAD_DIM), HEAD_DIM)


def head_weight_kernel(weight_in, out_ref, part_ref, flat_ref, sem):
    copy = pltpu.make_async_copy(weight_in.at[:, :, my_head()], part_ref, sem)
    copy.start()
    copy.wait()
    flat_ref[...] = part_ref[...].astype(f32).reshape(flat_ref.shape)
    depth, parts = weight_in.shape[:2]
    for t in range(parts):
        out_ref[:, t * HEAD_DIM : (t + 1) * HEAD_DIM] = flat_ref[pl.ds(t, depth, stride=parts), :].astype(bf16)


def group_forward_kernel(*refs):
    *norm_ins, weight_in, act_ref, slope_ref, att_ref, back_ref, out_ref, inverse_ref, prod_ref = refs[:-3]
    weight_ref, norm_ref, sem = refs[-3:]
    pairs = [(weight_in, weight_ref)] + [(one, norm_ref.at[s]) for s, one in enumerate(norm_ins)]
    copies = [pltpu.make_async_copy(a, b, sem.at[i]) for i, (a, b) in enumerate(pairs)]
    for copy in copies:
        copy.start()
    for copy in copies:
        copy.wait()
    rows = att_ref.shape[1]
    total = out_ref.shape[0] // len(norm_ins)
    weight = weight_ref[...]
    acts, masks, spans = [], [], []
    for s in range(len(norm_ins)):
        for m in range(total // rows):
            lines = pl.ds(s * total + m * rows, rows)
            pre_act = dot(norm_ref[s, m * rows : (m + 1) * rows, :], weight, NN)
            logistic = jax.nn.sigmoid(pre_act)
            act = (pre_act * logistic).astype(bf16)
            act_ref[lines, :] = act
            slope_ref[lines, :] = slope_of(pre_act, logistic)
            spans.append(lines)
            masks.append(seq_mask(held_sizes(norm_ref[s, total:, :128], m), rows))
            acts.append([act[:, t * HEAD_DIM : (t + 1) * HEAD_DIM] for t in range(4)])
    for lines, act, result in zip(spans, acts, attend_all(acts, masks)):
        att_ref[lines, :], back_ref[lines, :], out_ref[lines, :], inverse_ref[lines, :] = result
        prod_ref[lines, :] = (result[2] * act[0].astype(f32)).astype(bf16)


def attend_back_all(incoming, acts, results):
    mixed = [
        norm_back(a * act[0].astype(f32), normed, inverse).astype(bf16)
        for a, act, (_, _, normed, inverse) in zip(incoming, acts, results)
    ]
    grads = [dot(a, act[1], NT) for a, act in zip(mixed, acts)]
    values = [dot(result[0], a, TN) for result, a in zip(results, mixed)]
    grads = [(a * result[1]).astype(bf16) for a, result in zip(grads, results)]
    queries = [dot(a, act[3], NN) for a, act in zip(grads, acts)]
    keys = [dot(a, act[2], TN) for a, act in zip(grads, acts)]
    gates = [a * result[2] for a, result in zip(incoming, results)]
    return list(zip(gates, values, queries, keys))


def rows_kernel(slot_ref, returned_ref, out_ref):
    micro, rows = slot_ref.shape
    for m in range(micro):
        lines = pl.ds(m * rows, rows)
        pick = one_hot(slot_ref[m : m + 1], returned_ref.shape[0])
        out_ref[lines, :] = dot(pick, returned_ref[...], TN)


def add_kernel(mine_ref, other_ref, top_ref, out_ref):
    out_ref[...] = (mine_ref[...] + other_ref[...] + top_ref[...]).astype(bf16)


def trunk_kernel(length_ref, norm_ref, row_ref, proj_ref, mix_ref, weight_in, og_ref, part_ref, pre_ref, weight_ref, sem):
    copies = [pltpu.make_async_copy(weight_in.at[t], weight_ref.at[t], sem.at[t]) for t in range(4)]
    for copy in copies:
        copy.start()
    rows = HEAD_DIM
    total, cols = row_ref.shape[0], weight_ref.shape[2]
    out_grad = dot(row_ref[...], proj_ref[...], NT).astype(bf16)
    og_ref[...] = out_grad
    grad_product = dot(out_grad, mix_ref[...], NT)
    for copy in copies:
        copy.wait()
    for m in range(total // rows):
        lines = pl.ds(m * rows, rows)
        normed = norm_ref[lines, :]
        acts, slopes = [], []
        for t in range(4):
            pre_act = dot(normed, weight_ref[t], NN)
            logistic = jax.nn.sigmoid(pre_act)
            acts.append((pre_act * logistic).astype(bf16))
            slopes.append(slope_of(pre_act, logistic))
        heads = [slice(h * HEAD_DIM, (h + 1) * HEAD_DIM) for h in range(cols // HEAD_DIM)]
        acts = [[act[:, lanes] for act in acts] for lanes in heads]
        masks = [seq_mask([length_ref[m, 0, i] for i in range(SEQS)], rows)] * len(heads)
        incoming = [grad_product[m * rows : (m + 1) * rows, lanes] for lanes in heads]
        for lanes, grads in zip(heads, attend_back_all(incoming, acts, attend_all(acts, masks))):
            for t, grad in enumerate(grads):
                pre_ref[t, lines, lanes] = (grad * slopes[t][:, lanes]).astype(bf16)
    part_ref[...] = sum(dot(pre_ref[t], weight_ref[t], NT) for t in range(4))


def inputs_kernel(input_ref, og_ref, mine_ref, other_ref, out_ref):
    micro, rows, _ = input_ref.shape
    for m in range(micro):
        lines = pl.ds(m * rows, rows)
        normed, inverse = row_norm(input_ref[m].astype(f32))
        grad = norm_back(mine_ref[lines, :] + other_ref[lines, :], normed, inverse)
        out_ref[m] = (og_ref[lines, :].astype(f32) + grad).astype(bf16)


def weights_kernel(group, owners, *refs):
    row_refs, norm_refs = refs[:group], refs[group : 2 * group]
    act_ref, slope_ref, att_ref, back_ref, out_ref, inverse_ref, prod_ref, proj_ref, mix_ref, table_ref, packed_ref = refs[2 * group :]
    total = row_refs[0].shape[0]
    rows = att_ref.shape[1]
    cols = act_ref.shape[1]
    count = total // rows
    mix = mix_ref[my_head(), :]
    mixing, expand = 0.0, 0.0
    spans, incoming = [], []
    for s in range(group):
        out_grad = dot(row_refs[s][...], proj_ref[...], NT).astype(bf16)
        mixing += dot(out_grad, prod_ref[s * total : (s + 1) * total, :], TN)
        grad_product = dot(out_grad, mix, NT)
        for m in range(count):
            spans.append(pl.ds(s * total + m * rows, rows))
            incoming.append(grad_product[m * rows : (m + 1) * rows])
    packed_ref[:, :, cols : cols + HEAD_DIM] = mixing.reshape(owners, -1, HEAD_DIM).astype(bf16)
    packed_ref[:, :, cols + HEAD_DIM :] = table_ref[...]
    acts = [[act_ref[lines, t * HEAD_DIM : (t + 1) * HEAD_DIM] for t in range(4)] for lines in spans]
    results = [(att_ref[lines, :], back_ref[lines, :], out_ref[lines, :], inverse_ref[lines, :]) for lines in spans]
    grads = attend_back_all(incoming, acts, results)
    pre = [(jnp.concatenate(grad, axis=1) * slope_ref[lines, :]).astype(bf16) for grad, lines in zip(grads, spans)]
    for s in range(group):
        expand += dot(norm_refs[s][:total, :], jnp.concatenate(pre[s * count : (s + 1) * count], axis=0), TN)
    packed_ref[:, :, :cols] = expand.reshape(owners, -1, cols).astype(bf16)


def final_kernel(group, in_ref, expand_ref, mixing_ref, table_ref):
    cols = expand_ref.shape[2]
    side = range(group)
    for g in side:
        sources = [(y * group + z) * group + x for y in side for z in side for x in side if x % 2 + 2 * (y % 2) == g]
        total = sum(in_ref[i, :, : cols + HEAD_DIM].astype(f32) for i in sources)
        head = pl.ds(g * HEAD_DIM, HEAD_DIM)
        for t in range(4):
            expand_ref[:, t, head] = total[:, t * HEAD_DIM : (t + 1) * HEAD_DIM]
        mixing_ref[:, head] = total[:, cols:]
    lanes = pl.ds(cols + HEAD_DIM, HEAD_DIM)
    for q in side:
        sources = [(y * group + q) * group + x for y in side for x in side]
        total = sum(in_ref[i, :, lanes].astype(f32) for i in sources)
        half = total.shape[0] // 2
        table_ref[q * half : (q + 1) * half, :HEAD_DIM] = total[:half]
        table_ref[q * half : (q + 1) * half, HEAD_DIM:] = total[half:]


def body(
    inputs,
    lengths,
    expand_weight,
    mixing_weight,
    projection,
    saved_rows,
    cluster_ids,
    item_ids,
    top_table,
    codebook,
):
    micro, rows, model_width = inputs.shape
    total = micro * rows
    owners = lax.axis_size(DEV)
    group = lax.axis_size("x")
    half_clusters, width = top_table.shape
    books, items, _ = codebook.shape
    cols = expand_weight.shape[2]
    slots = owners * micro * CAP
    own = half_clusters // owners
    saved = saved_rows.reshape(total, width)

    sent, slot_ids, marks = call(
        functools.partial(dispatch_kernel, owners, books, items),
        "dispatch",
        [((slots, width + 128), bf16), ((micro, rows), jnp.int32), ((total, 128), f32)],
        (cluster_ids, item_ids, saved_rows),
        "HHH HVH", limit=56,
    )
    got = lax.all_to_all(sent.reshape(owners, slots // owners, -1), DEV, 0, 0, tiled=True).reshape(slots, -1)

    normed, logits, stats, table = call(
        functools.partial(first_kernel, group, owners),
        "norms_and_logits",
        [
            ((total + 16, model_width), bf16),
            ((total, half_clusters), f32),
            ((total, 128), f32),
            (top_table.shape, bf16),
        ],
        (lengths, inputs, saved, top_table),
        "SHHH VVVV",
        limit=FIRST_LIMIT,
        after=(slot_ids,),
    )
    normed_all = [normed] + [from_member(normed, s) for s in range(1, group)]
    row_top, *top_grads, top_token = call(
        functools.partial(top_grad_kernel, group, own),
        "top_grads",
        [((total, width), f32)] + [((total, half_clusters // group + width), bf16)] * group,
        (logits, stats, swap(stats), marks, table, saved),
        "VVVHHH " + "H" * (1 + group),
        limit=40,
        token=True,
    )
    top_all = [top_grads[0]] + [shifted(top_grads[s], "z", s) for s in range(1, group)]

    leaf, leaf_stats, got_held, book_held = leaf_scores(got, codebook, (top_token, normed[:8, :128]))
    back, leaf_grad = leaf_back(
        got_held, leaf, leaf_stats, swap(leaf_stats), book_held, ()
    )
    returned = lax.all_to_all(back.reshape(owners, slots // owners, width), DEV, 0, 0, tiled=True)

    row_top = row_top + swap(row_top)
    head_weight, head_token = call(
        head_weight_kernel,
        "head_weight",
        [((model_width, 4 * HEAD_DIM), bf16)],
        (expand_weight,),
        "R H",
        scratch=[
            pltpu.VMEM((model_width, 4, HEAD_DIM), bf16),
            pltpu.VMEM((model_width * 4, HEAD_DIM), f32),
            pltpu.SemaphoreType.DMA,
        ],
        after=(back, sum(a[:8, :128] for a in normed_all[1:])),
        token=True,
    )

    table_part, table_token = call(
        functools.partial(table_kernel, owners),
        "table_part",
        [((owners, 16, 128), bf16)],
        top_all,
        "V" * group + " V",
        limit=16,
        after=(back, head_token),
        token=True,
    )

    (row_part,) = call(
        rows_kernel,
        "rows",
        [((total, width), f32)],
        (slot_ids, returned.reshape(slots, width)),
        "VH V",
        limit=28,
        after=(table_token,),
    )
    (row_grad,) = call(add_kernel, "row_grad", [((total, width), bf16)], (row_part, swap(row_part), row_top), "VVV V", limit=28)
    row_all = [row_grad] + [from_member(row_grad, s) for s in range(1, group)]

    group_rows = group * total
    group_forward = call(
        group_forward_kernel,
        "group_forward",
        [
            ((group_rows, 4 * HEAD_DIM), bf16),
            ((group_rows, 4 * HEAD_DIM), f32),
            ((group_rows, rows), bf16),
            ((group_rows, rows), f32),
            ((group_rows, HEAD_DIM), f32),
            ((group_rows, HEAD_DIM), f32),
            ((group_rows, HEAD_DIM), bf16),
        ],
        (*normed_all, head_weight),
        "R" * (group + 1) + " " + "V" * 7,
        limit=GROUP_LIMIT,
        after=(row_grad,),
        scratch=[
            pltpu.VMEM(head_weight.shape, bf16),
            pltpu.VMEM((group, total + 16, model_width), bf16),
            pltpu.SemaphoreType.DMA((group + 1,)),
        ],
    )

    (packed,) = call(
        functools.partial(weights_kernel, group, owners),
        "weight_parts",
        [((owners, model_width // owners, cols + 2 * HEAD_DIM), bf16)],
        (*row_all, *normed_all, *group_forward, projection, mixing_weight, table_part),
        "V" * (2 * group + 10) + " H",
        limit=28,
    )
    arrived = lax.all_to_all(packed, DEV, 0, 0, tiled=True)

    late_weight, _ = lax.optimization_barrier((expand_weight, packed))
    weight = late_weight.swapaxes(0, 1)
    out_grad, grad_part = call(
        trunk_kernel,
        "trunk",
        [((total, model_width), bf16), ((total, model_width), f32)],
        (lengths, normed, row_grad, projection, mixing_weight, weight),
        "SHHHHR VV",
        limit=48,
        scratch=[pltpu.VMEM((4, total, cols), bf16), pltpu.VMEM(weight.shape, bf16), pltpu.SemaphoreType.DMA((4,))],
        after=(packed,),
    )
    (grad_inputs,) = call(
        inputs_kernel, "input_grads", [(inputs.shape, bf16)], (inputs, out_grad, grad_part, swap(grad_part)), "HVVV H", limit=48
    )
    book_grads = leaf_book(got, leaf_grad, books, width, (packed,))
    share = model_width // owners
    expand, mixing, table_share = call(
        functools.partial(final_kernel, group),
        "weight_sums",
        [((share, 4, cols), f32), ((share, cols), f32), ((own, width), f32)],
        (arrived,),
        "V HHH",
        limit=28,
    )
    return grad_inputs, expand, mixing.T, table_share, book_grads


def solution(mesh):
    grid = Mesh(mesh.devices.reshape(2, 4, 4, 4), ("section",) + DEV)
    return jax.shard_map(
        body,
        mesh=grid,
        in_specs=(
            P(None, DEV, None),
            P(None, DEV, None),
            P(None, None, "section"),
            P("section", None),
            P(),
            P(None, DEV, None),
            P(None, DEV),
            P(None, DEV),
            P("section", None),
            P(DEV, "section", None),
        ),
        out_specs=(
            P(None, DEV, None),
            P(DEV, None, "section"),
            P("section", DEV),
            P(("section",) + DEV, None),
            P(DEV, "section", None),
        ),
        check_vma=False,
    )
```

```python
import functools

import jax
import jax.numpy as jnp
from jax import lax
from jax.experimental import pallas as pl
from jax.experimental.pallas import tpu as pltpu
from jax.sharding import Mesh
from jax.sharding import PartitionSpec as P

HEAD_DIM = 128
SEQ_MOST = 64
SEQS = 4
CAP = 4
PARTS = 2
eps = 1e-05
DEV = ("y", "z", "x")
f32 = jnp.float32
bf16 = jnp.bfloat16
NN = ((1,), (0,))
NT = ((1,), (1,))
TN = ((0,), (0,))


def swap(part):
    return lax.ppermute(part, "section", [(0, 1), (1, 0)])


def from_pair(part, axis):
    count = lax.axis_size(axis)
    return lax.ppermute(part, axis, [(i, i ^ 1) for i in range(count)])


def member():
    return lax.rem(lax.axis_index("x"), 2) + 2 * lax.rem(lax.axis_index("y"), 2)


def from_member(part, other):
    count = lax.axis_size("x")
    flip = count * (other // 2) + other % 2
    return lax.ppermute(part, ("y", "x"), [(i, i ^ flip) for i in range(lax.axis_size("y") * count)])


def dot(left, right, dims):
    return lax.dot_general(left, right, (dims, ((), ())), preferred_element_type=f32)


def iota(shape, dim):
    return lax.broadcasted_iota(jnp.int32, shape, dim)


def row_norm(argument):
    row_mean = jnp.mean(argument, axis=-1, keepdims=True)
    centered = argument - row_mean
    variance = jnp.mean(centered * centered, axis=-1, keepdims=True)
    inverse = lax.rsqrt(variance + eps)
    return (centered * inverse, inverse)


def norm_back(incoming, normed, inverse):
    mean_in = jnp.mean(incoming, axis=-1, keepdims=True)
    mean_dot = jnp.mean(incoming * normed, axis=-1, keepdims=True)
    return (incoming - mean_in - normed * mean_dot) * inverse


def call(kernel, name, outs, args, kinds, after=(), scratch=(), limit=56, flops=0, token=False):
    in_kinds, out_kinds = kinds.split()
    if token:
        outs, out_kinds = [*outs, ((8, 128), f32)], out_kinds + "V"
    assert len(in_kinds) == len(args) and len(out_kinds) == len(outs), name
    spaces = {"V": pltpu.VMEM, "S": pltpu.SMEM, "H": pl.ANY, "R": pl.ANY}
    held = [pltpu.VMEM(a.shape, a.dtype) for a, k in zip(args, in_kinds) if k == "H"]
    held += [pltpu.VMEM(s, d) for (s, d), k in zip(outs, out_kinds) if k == "H"]
    sems = [pltpu.SemaphoreType.DMA((len(held),))] if held else []

    def run(*refs):
        ins = list(refs[: len(args)])
        refs = refs[len(args) + len(after) :]
        results = list(refs[: len(outs)])
        buffers = list(refs[len(outs) : len(outs) + len(held)])
        rest = refs[len(outs) + len(held) + len(sems) :]
        sem = refs[len(outs) + len(held)] if held else None
        count = 0
        first, last = [], []
        for i, kind in enumerate(in_kinds):
            if kind == "H":
                first.append(pltpu.make_async_copy(ins[i], buffers[count], sem.at[count]))
                first[-1].start()
                ins[i] = buffers[count]
                count += 1
        for i, kind in enumerate(out_kinds):
            if kind == "H":
                last.append(pltpu.make_async_copy(buffers[count], results[i], sem.at[count]))
                results[i] = buffers[count]
                count += 1
        for copy in first:
            copy.wait()
        if token:
            results.pop()[...] = jnp.zeros((8, 128), f32)
        kernel(*ins, *results, *rest)
        for copy in last:
            copy.start()
        for copy in last:
            copy.wait()

    return pl.pallas_call(
        run,
        in_specs=[pl.BlockSpec(memory_space=spaces[k]) for k in in_kinds] + [pl.BlockSpec(memory_space=pl.ANY)] * len(after),
        out_specs=[pl.BlockSpec(memory_space=spaces[k]) for k in out_kinds],
        out_shape=[jax.ShapeDtypeStruct(s, d) for s, d in outs],
        scratch_shapes=held + sems + list(scratch),
        compiler_params=pltpu.CompilerParams(vmem_limit_bytes=limit * 2**20),
        cost_estimate=pl.CostEstimate(flops=flops, bytes_accessed=0, transcendentals=0),
        name=name,
    )(*args, *after)


def one_hot(slots_row, count):
    return jnp.where(iota((count, slots_row.shape[1]), 0) == slots_row, 1.0, 0.0).astype(bf16)


def dispatch_kernel(owners, books, half, cluster_ref, item_ref, saved_ref, sent_ref, slot_ref, mark_ref):
    micro, rows = cluster_ref.shape
    width = saved_ref.shape[2]
    each = micro * CAP
    before = jnp.where(iota((rows, rows), 0) < iota((rows, rows), 1), 1.0, 0.0).astype(bf16)
    same = jnp.where(iota((rows, rows), 0) == iota((rows, rows), 1), 1.0, 0.0).astype(bf16)
    kind = iota((128, rows), 0)
    rows_out, codes_out = 0.0, 0.0
    for m in range(micro):
        target, item = cluster_ref[m : m + 1], item_ref[m : m + 1]
        owner, local = target // books, target % books
        marks = jnp.where(iota((owners, rows), 0) == owner, 1.0, 0.0)
        earlier = dot(marks.astype(bf16), before, NN)
        rank = jnp.sum(earlier * marks, axis=0, keepdims=True).astype(jnp.int32)
        slot = owner * each + m * CAP + rank
        slot_ref[m : m + 1] = slot
        code = jnp.where(
            kind == 0,
            local + 1,
            jnp.where(kind == 1, item // half, jnp.where(kind == 2, item % half, jnp.where(kind == 3, owner, 0))),
        )
        code = code.astype(f32).astype(bf16)
        pick = one_hot(slot, owners * each)
        rows_out += dot(pick, saved_ref[m], NN)
        codes_out += dot(pick, code, NT)
        turned = dot(same, code, NT)
        mark_ref[m * rows : (m + 1) * rows] = jnp.broadcast_to(
            turned[:, 3:4] * books + turned[:, 0:1] - 1.0, (rows, 128)
        )
    sent_ref[:, :width] = rows_out.astype(bf16)
    sent_ref[:, width:] = codes_out.astype(bf16)


def first_kernel(group, owners, length_ref, input_ref, saved_ref, table_ref, norm_ref, logit_ref, stat_ref, turned_ref):
    micro, count, depth = input_ref.shape
    for m in range(micro):
        norm_ref[m * count : (m + 1) * count] = row_norm(input_ref[m].astype(f32))[0].astype(bf16)
    lane = iota((16, depth), 1)
    held = jnp.zeros((16, depth), f32)
    for m in range(micro):
        for i in range(SEQS):
            held = jnp.where(lane == m * SEQS + i, length_ref[m, 0, i].astype(f32), held)
    norm_ref[micro * count :] = held.astype(bf16)
    half, width = table_ref.shape
    rows = table_ref[...].astype(f32).reshape(owners, group, half // owners // group, width)
    turned = jnp.concatenate([rows[:, q].reshape(half // group, width) for q in range(group)], axis=0).astype(bf16)
    turned_ref[...] = turned
    logits = dot(saved_ref[...], turned, NT)
    logit_ref[...] = logits
    peak = jnp.max(logits, axis=1, keepdims=True)
    mass = jnp.sum(jnp.exp(logits - peak), axis=1, keepdims=True)
    stat_ref[...] = jnp.where(iota(stat_ref.shape, 1) == 0, peak, mass)


def joined(mine_ref, other_ref):
    peak_a, mass_a = mine_ref[:, 0:1], mine_ref[:, 1:2]
    peak_b, mass_b = other_ref[:, 0:1], other_ref[:, 1:2]
    peak = jnp.maximum(peak_a, peak_b)
    return peak, mass_a * jnp.exp(peak_a - peak) + mass_b * jnp.exp(peak_b - peak)


def top_grad_kernel(group, own, logit_ref, mine_ref, other_ref, mark_ref, table_ref, saved_ref, *out_refs):
    row_ref, grad_refs = out_refs[0], out_refs[1:]
    half = table_ref.shape[0]
    quarter = half // group
    piece = own // group
    base = lax.axis_index("section") * half
    me = lax.rem(lax.axis_index("z"), 2)
    peak, mass = joined(mine_ref, other_ref)
    target = mark_ref[:, 0:1].astype(jnp.int32) - base
    total = 0.0
    column = iota((mark_ref.shape[0], quarter), 1)
    for q in range(group):
        index = (column // piece) * own + q * piece + column % piece
        cols = pl.ds(q * quarter, quarter)
        probs = jnp.exp(logit_ref[:, cols] - peak) / mass
        grad = (probs - jnp.where(index == target, 1.0, 0.0)).astype(bf16)
        total += dot(grad, table_ref[cols, :], NN)
        for s in range(group):

            @pl.when(lax.rem(me + s, group) == q)
            def _(s=s, grad=grad):
                grad_refs[s][:, :quarter] = grad
                grad_refs[s][:, quarter:] = saved_ref[...]

    row_ref[...] = total


def table_kernel(owners, *refs):
    *in_refs, out_ref = refs
    width = out_ref.shape[2]
    part = in_refs[0].shape[1] - width
    total = sum(dot(r[:, :part], r[:, part:], TN) for r in in_refs)
    out_ref[...] = total.reshape(owners, -1, width).astype(bf16)


def masked_product(code_ref, left_ref, width, book_ref, out_ref, dims, group, ready):
    lines = 256
    out_ref[...] = jnp.zeros_like(out_ref)

    def step(i, carry):
        ready(i)
        books = book_ref[pl.ds(i * group, group)]
        if dims == NT:
            right = jnp.concatenate([books[k] for k in range(group)], axis=1)
        else:
            right = books.reshape(-1, books.shape[2])
        for r in range(0, out_ref.shape[0], lines):
            some = pl.ds(r, lines)
            left, code = left_ref[some, :width], code_ref[some, :]
            parts = []
            for k in range(group):
                here = code == (i * group + k + 1).astype(f32).astype(bf16)
                parts.append(jnp.where(here, left, jnp.zeros_like(left)))
            out_ref[some, :] += dot(jnp.concatenate(parts, axis=1), right, dims)
        return carry

    lax.fori_loop(0, book_ref.shape[0] // group, step, 0)


FIRST_LIMIT = 40
GROUP_LIMIT = 40
BOOK_GROUP = 16
BOOK_COPIES = 4


def leaf_scores_kernel(got_in, book_in, out_ref, stat_ref, got_ref, book_ref, code_ref, got_sem, sem):
    width = book_ref.shape[2]
    steps = book_ref.shape[0] // BOOK_GROUP
    piece = BOOK_GROUP // BOOK_COPIES

    def copies(i):
        for j in range(BOOK_COPIES):
            some = pl.ds(i * BOOK_GROUP + j * piece, piece)
            yield pltpu.make_async_copy(book_in.at[some], book_ref.at[some], sem.at[i, j])

    got_copy = pltpu.make_async_copy(got_in, got_ref, got_sem)
    got_copy.start()
    for i in range(2):
        for copy in copies(i):
            copy.start()
    got_copy.wait()
    code_ref[...] = jnp.broadcast_to(got_ref[:, width : width + 1], code_ref.shape)

    def ready(i):
        for copy in copies(i):
            copy.wait()

        @pl.when(i + 2 < steps)
        def _():
            for copy in copies(i + 2):
                copy.start()

    masked_product(code_ref, got_ref, width, book_ref, out_ref, NT, BOOK_GROUP, ready)
    scores = out_ref[...]
    peak = jnp.max(scores, axis=1, keepdims=True)
    mass = jnp.sum(jnp.exp(scores - peak), axis=1, keepdims=True)
    stat_ref[...] = jnp.where(iota(stat_ref.shape, 1) == 0, peak, mass)


def leaf_back_kernel(got_ref, score_ref, mine_ref, other_ref, book_ref, back_ref, grad_ref, code_ref, total_ref):
    items, width = book_ref.shape[1:]
    code = got_ref[:, width : width + 1]
    code_ref[...] = jnp.broadcast_to(code, code_ref.shape)
    high = got_ref[:, width + 1 : width + 2].astype(f32).astype(jnp.int32)
    low = got_ref[:, width + 2 : width + 3].astype(f32).astype(jnp.int32)
    peak, mass = joined(mine_ref, other_ref)
    probs = jnp.exp(score_ref[...] - peak) / mass
    hit = (iota(probs.shape, 1) == low) & (high == lax.axis_index("section"))
    grad = jnp.where(code.astype(f32) > 0, probs - jnp.where(hit, 1.0, 0.0), 0.0)
    grad_ref[...] = grad.astype(bf16)
    masked_product(code_ref, grad_ref, items, book_ref, total_ref, NN, 32, lambda i: None)
    back_ref[...] = total_ref[...].astype(bf16)


def leaf_book_kernel(got_ref, grad_ref, out_ref, code_ref, turned_ref, held_ref, sem):
    books, items, width = out_ref.shape
    group = books // sem.shape[0]
    slots = got_ref.shape[0]
    turned_ref[...] = grad_ref[...].astype(f32).T.astype(bf16)
    code_ref[...] = jnp.broadcast_to(got_ref[:, width : width + 1].astype(f32), (slots, items)).T.astype(bf16)
    rows = got_ref[:, :width]
    copies = []
    for i in range(books // group):
        some = pl.ds(i * group, group)
        turned, code = turned_ref[...], code_ref[...]
        parts = []
        for k in range(group):
            here = code == (i * group + k + 1)
            parts.append(jnp.where(here, turned, jnp.zeros_like(turned)))
        grads = dot(jnp.concatenate(parts, axis=0), rows, NN)
        held_ref[some] = grads.reshape(group, items, width).astype(bf16)
        copies.append(pltpu.make_async_copy(held_ref.at[some], out_ref.at[some], sem.at[i]))
        copies[-1].start()
    for copy in copies:
        copy.wait()


def leaf_scores(got, book, after):
    books, items, width = book.shape
    slots = got.shape[0]
    return call(
        leaf_scores_kernel,
        "leaf_scores",
        [((slots, items), f32), ((slots, 128), f32), (got.shape, bf16), (book.shape, bf16)],
        (got, book),
        "RR VVVV", limit=42,
        flops=2 * slots * books * items * width,
        scratch=[
            pltpu.VMEM((slots, width), bf16),
            pltpu.SemaphoreType.DMA,
            pltpu.SemaphoreType.DMA((books // BOOK_GROUP, BOOK_COPIES)),
        ],
        after=after,
    )


def leaf_back(got, scores, mine, other, book, after):
    books, items, width = book.shape
    slots = got.shape[0]
    return call(
        leaf_back_kernel,
        "leaf_back",
        [((slots, width), bf16), ((slots, items), bf16)],
        (got, scores, mine, other, book),
        "VVVVV HH",
        limit=28,
        scratch=[pltpu.VMEM((slots, items), bf16), pltpu.VMEM((slots, width), f32)],
        after=after,
    )


def leaf_book(got, grads, books, width, after):
    slots, items = grads.shape
    group = 4
    return call(
        leaf_book_kernel,
        "leaf_book",
        [((books, items, width), bf16)],
        (got, grads),
        "HH R",
        scratch=[
            pltpu.VMEM((items, slots), bf16),
            pltpu.VMEM((items, slots), bf16),
            pltpu.VMEM((books, items, width), bf16),
            pltpu.SemaphoreType.DMA((books // group,)),
        ],
        after=after,
    )[0]


def slope_of(argument, logistic):
    return logistic * (1.0 + argument * (1.0 - logistic))


def seq_mask(sizes, rows):
    row, col = iota((rows, rows), 0), iota((rows, rows), 1)
    row_seg, col_seg, end = 0, 0, 0
    for size in sizes:
        end = end + size
        row_seg += jnp.where(row >= end, 1, 0)
        col_seg += jnp.where(col >= end, 1, 0)
    return jnp.where((row_seg == col_seg) & (col <= row), 1.0 / SEQ_MOST, 0.0)


def held_sizes(held, m):
    held = held.astype(f32)[0:1].astype(jnp.int32)
    return [held[:, m * SEQS + i : m * SEQS + i + 1] for i in range(SEQS)]


def attend_all(acts, masks):
    scores = [dot(query, key, NT) for _, _, query, key in acts]
    logistics = [jax.nn.sigmoid(score) for score in scores]
    attention = [(a * b * mask).astype(bf16) for a, b, mask in zip(scores, logistics, masks)]
    mixed = [dot(a, act[1], NN) for a, act in zip(attention, acts)]
    back = [slope_of(a, b) * mask for a, b, mask in zip(scores, logistics, masks)]
    normed = [row_norm(one) for one in mixed]
    return [(a, b, n, jnp.broadcast_to(i, n.shape)) for a, b, (n, i) in zip(attention, back, normed)]


def my_head():
    return pl.ds(pl.multiple_of(member() * HEAD_DIM, HEAD_DIM), HEAD_DIM)


def head_weight_kernel(weight_in, out_ref, part_ref, flat_ref, sem):
    copy = pltpu.make_async_copy(weight_in.at[:, :, my_head()], part_ref, sem)
    copy.start()
    copy.wait()
    flat_ref[...] = part_ref[...].astype(f32).reshape(flat_ref.shape)
    depth, parts = weight_in.shape[:2]
    for t in range(parts):
        out_ref[:, t * HEAD_DIM : (t + 1) * HEAD_DIM] = flat_ref[pl.ds(t, depth, stride=parts), :].astype(bf16)


def group_forward_kernel(*refs):
    *norm_ins, weight_in, act_ref, slope_ref, att_ref, back_ref, out_ref, inverse_ref, prod_ref = refs[:-3]
    weight_ref, norm_ref, sem = refs[-3:]
    pairs = [(weight_in, weight_ref)] + [(one, norm_ref.at[s]) for s, one in enumerate(norm_ins)]
    copies = [pltpu.make_async_copy(a, b, sem.at[i]) for i, (a, b) in enumerate(pairs)]
    for copy in copies:
        copy.start()
    for copy in copies:
        copy.wait()
    rows = att_ref.shape[1]
    total = out_ref.shape[0] // len(norm_ins)
    weight = weight_ref[...]
    acts, masks, spans = [], [], []
    for s in range(len(norm_ins)):
        for m in range(total // rows):
            lines = pl.ds(s * total + m * rows, rows)
            pre_act = dot(norm_ref[s, m * rows : (m + 1) * rows, :], weight, NN)
            logistic = jax.nn.sigmoid(pre_act)
            act = (pre_act * logistic).astype(bf16)
            act_ref[lines, :] = act
            slope_ref[lines, :] = slope_of(pre_act, logistic)
            spans.append(lines)
            masks.append(seq_mask(held_sizes(norm_ref[s, total:, :128], m), rows))
            acts.append([act[:, t * HEAD_DIM : (t + 1) * HEAD_DIM] for t in range(4)])
    for lines, act, result in zip(spans, acts, attend_all(acts, masks)):
        att_ref[lines, :], back_ref[lines, :], out_ref[lines, :], inverse_ref[lines, :] = result
        prod_ref[lines, :] = (result[2] * act[0].astype(f32)).astype(bf16)


def attend_back_all(incoming, acts, results):
    mixed = [
        norm_back(a * act[0].astype(f32), normed, inverse).astype(bf16)
        for a, act, (_, _, normed, inverse) in zip(incoming, acts, results)
    ]
    grads = [dot(a, act[1], NT) for a, act in zip(mixed, acts)]
    values = [dot(result[0], a, TN) for result, a in zip(results, mixed)]
    grads = [(a * result[1]).astype(bf16) for a, result in zip(grads, results)]
    queries = [dot(a, act[3], NN) for a, act in zip(grads, acts)]
    keys = [dot(a, act[2], TN) for a, act in zip(grads, acts)]
    gates = [a * result[2] for a, result in zip(incoming, results)]
    return list(zip(gates, values, queries, keys))


def rows_kernel(slot_ref, returned_ref, out_ref):
    micro, rows = slot_ref.shape
    for m in range(micro):
        lines = pl.ds(m * rows, rows)
        pick = one_hot(slot_ref[m : m + 1], returned_ref.shape[0])
        out_ref[lines, :] = dot(pick, returned_ref[...], TN)


def add_kernel(mine_ref, other_ref, top_ref, out_ref):
    out_ref[...] = (mine_ref[...] + other_ref[...] + top_ref[...]).astype(bf16)


def trunk_kernel(length_ref, norm_ref, row_ref, proj_ref, mix_ref, weight_in, og_ref, part_ref, pre_ref, weight_ref, sem):
    copies = [pltpu.make_async_copy(weight_in.at[t], weight_ref.at[t], sem.at[t]) for t in range(4)]
    for copy in copies:
        copy.start()
    rows = HEAD_DIM
    total, cols = row_ref.shape[0], weight_ref.shape[2]
    out_grad = dot(row_ref[...], proj_ref[...], NT).astype(bf16)
    og_ref[...] = out_grad
    grad_product = dot(out_grad, mix_ref[...], NT)
    for copy in copies:
        copy.wait()
    for m in range(total // rows):
        lines = pl.ds(m * rows, rows)
        normed = norm_ref[lines, :]
        acts, slopes = [], []
        for t in range(4):
            pre_act = dot(normed, weight_ref[t], NN)
            logistic = jax.nn.sigmoid(pre_act)
            acts.append((pre_act * logistic).astype(bf16))
            slopes.append(slope_of(pre_act, logistic))
        heads = [slice(h * HEAD_DIM, (h + 1) * HEAD_DIM) for h in range(cols // HEAD_DIM)]
        acts = [[act[:, lanes] for act in acts] for lanes in heads]
        masks = [seq_mask([length_ref[m, 0, i] for i in range(SEQS)], rows)] * len(heads)
        incoming = [grad_product[m * rows : (m + 1) * rows, lanes] for lanes in heads]
        for lanes, grads in zip(heads, attend_back_all(incoming, acts, attend_all(acts, masks))):
            for t, grad in enumerate(grads):
                pre_ref[t, lines, lanes] = (grad * slopes[t][:, lanes]).astype(bf16)
    part_ref[...] = sum(dot(pre_ref[t], weight_ref[t], NT) for t in range(4))


def inputs_kernel(input_ref, og_ref, mine_ref, other_ref, out_ref):
    micro, rows, _ = input_ref.shape
    for m in range(micro):
        lines = pl.ds(m * rows, rows)
        normed, inverse = row_norm(input_ref[m].astype(f32))
        grad = norm_back(mine_ref[lines, :] + other_ref[lines, :], normed, inverse)
        out_ref[m] = (og_ref[lines, :].astype(f32) + grad).astype(bf16)


def weights_kernel(group, owners, *refs):
    row_refs, norm_refs = refs[:group], refs[group : 2 * group]
    act_ref, slope_ref, att_ref, back_ref, out_ref, inverse_ref, prod_ref, proj_ref, mix_ref, table_ref, packed_ref = refs[2 * group :]
    total = row_refs[0].shape[0]
    rows = att_ref.shape[1]
    cols = act_ref.shape[1]
    count = total // rows
    mix = mix_ref[my_head(), :]
    mixing, expand = 0.0, 0.0
    spans, incoming = [], []
    for s in range(group):
        out_grad = dot(row_refs[s][...], proj_ref[...], NT).astype(bf16)
        mixing += dot(out_grad, prod_ref[s * total : (s + 1) * total, :], TN)
        grad_product = dot(out_grad, mix, NT)
        for m in range(count):
            spans.append(pl.ds(s * total + m * rows, rows))
            incoming.append(grad_product[m * rows : (m + 1) * rows])
    packed_ref[:, :, cols : cols + HEAD_DIM] = mixing.reshape(owners, -1, HEAD_DIM).astype(bf16)
    packed_ref[:, :, cols + HEAD_DIM :] = table_ref[...]
    acts = [[act_ref[lines, t * HEAD_DIM : (t + 1) * HEAD_DIM] for t in range(4)] for lines in spans]
    results = [(att_ref[lines, :], back_ref[lines, :], out_ref[lines, :], inverse_ref[lines, :]) for lines in spans]
    grads = attend_back_all(incoming, acts, results)
    pre = [(jnp.concatenate(grad, axis=1) * slope_ref[lines, :]).astype(bf16) for grad, lines in zip(grads, spans)]
    for s in range(group):
        expand += dot(norm_refs[s][:total, :], jnp.concatenate(pre[s * count : (s + 1) * count], axis=0), TN)
    packed_ref[:, :, :cols] = expand.reshape(owners, -1, cols).astype(bf16)


def final_kernel(group, in_ref, expand_ref, mixing_ref, table_ref):
    cols = expand_ref.shape[2]
    side = range(group)
    for g in side:
        sources = [(y * group + z) * group + x for y in side for z in side for x in side if x % 2 + 2 * (y % 2) == g]
        total = sum(in_ref[i, :, : cols + HEAD_DIM].astype(f32) for i in sources)
        head = pl.ds(g * HEAD_DIM, HEAD_DIM)
        for t in range(4):
            expand_ref[:, t, head] = total[:, t * HEAD_DIM : (t + 1) * HEAD_DIM]
        mixing_ref[:, head] = total[:, cols:]
    lanes = pl.ds(cols + HEAD_DIM, table_ref.shape[1])
    for q in range(PARTS):
        sources = [(y * group + z) * group + x for y in side for z in side for x in side if z % PARTS == q]
        total = sum(in_ref[i, :, lanes].astype(f32) for i in sources)
        table_ref[q * total.shape[0] : (q + 1) * total.shape[0], :] = total


def body(
    inputs,
    lengths,
    expand_weight,
    mixing_weight,
    projection,
    saved_rows,
    cluster_ids,
    item_ids,
    top_table,
    codebook,
):
    micro, rows, model_width = inputs.shape
    total = micro * rows
    owners = lax.axis_size(DEV)
    group = lax.axis_size("x")
    half_clusters, width = top_table.shape
    books, items, _ = codebook.shape
    cols = expand_weight.shape[2]
    slots = owners * micro * CAP
    own = half_clusters // owners
    saved = saved_rows.reshape(total, width)

    sent, slot_ids, marks = call(
        functools.partial(dispatch_kernel, owners, books, items),
        "dispatch",
        [((slots, width + 128), bf16), ((micro, rows), jnp.int32), ((total, 128), f32)],
        (cluster_ids, item_ids, saved_rows),
        "HHH HVH", limit=56,
    )
    got = lax.all_to_all(sent.reshape(owners, slots // owners, -1), DEV, 0, 0, tiled=True).reshape(slots, -1)

    normed, logits, stats, table = call(
        functools.partial(first_kernel, PARTS, owners),
        "norms_and_logits",
        [
            ((total + 16, model_width), bf16),
            ((total, half_clusters), f32),
            ((total, 128), f32),
            (top_table.shape, bf16),
        ],
        (lengths, inputs, saved, top_table),
        "SHHH VVVV",
        limit=FIRST_LIMIT,
        after=(slot_ids,),
    )
    normed_all = [normed] + [from_member(normed, s) for s in range(1, group)]
    row_top, *top_grads, top_token = call(
        functools.partial(top_grad_kernel, PARTS, own),
        "top_grads",
        [((total, width), f32)] + [((total, half_clusters // PARTS + width), bf16)] * PARTS,
        (logits, stats, swap(stats), marks, table, saved),
        "VVVHHH " + "H" * (1 + PARTS),
        limit=40,
        token=True,
    )
    top_all = [top_grads[0], from_pair(top_grads[1], "z")]

    leaf, leaf_stats, got_held, book_held = leaf_scores(got, codebook, (top_token, normed[:8, :128]))
    back, leaf_grad = leaf_back(
        got_held, leaf, leaf_stats, swap(leaf_stats), book_held, ()
    )
    returned = lax.all_to_all(back.reshape(owners, slots // owners, width), DEV, 0, 0, tiled=True)

    row_top = row_top + swap(row_top)
    head_weight, head_token = call(
        head_weight_kernel,
        "head_weight",
        [((model_width, 4 * HEAD_DIM), bf16)],
        (expand_weight,),
        "R H",
        scratch=[
            pltpu.VMEM((model_width, 4, HEAD_DIM), bf16),
            pltpu.VMEM((model_width * 4, HEAD_DIM), f32),
            pltpu.SemaphoreType.DMA,
        ],
        after=(back, sum(a[:8, :128] for a in normed_all[1:])),
        token=True,
    )

    table_part, table_token = call(
        functools.partial(table_kernel, owners),
        "table_part",
        [((owners, own // PARTS, width), bf16)],
        top_all,
        "V" * PARTS + " V",
        limit=16,
        after=(back, head_token),
        token=True,
    )

    (row_part,) = call(
        rows_kernel,
        "rows",
        [((total, width), f32)],
        (slot_ids, returned.reshape(slots, width)),
        "VH V",
        limit=28,
        after=(table_token,),
    )
    (row_grad,) = call(add_kernel, "row_grad", [((total, width), bf16)], (row_part, swap(row_part), row_top), "VVV V", limit=28)
    row_all = [row_grad] + [from_member(row_grad, s) for s in range(1, group)]

    group_rows = group * total
    group_forward = call(
        group_forward_kernel,
        "group_forward",
        [
            ((group_rows, 4 * HEAD_DIM), bf16),
            ((group_rows, 4 * HEAD_DIM), f32),
            ((group_rows, rows), bf16),
            ((group_rows, rows), f32),
            ((group_rows, HEAD_DIM), f32),
            ((group_rows, HEAD_DIM), f32),
            ((group_rows, HEAD_DIM), bf16),
        ],
        (*normed_all, head_weight),
        "R" * (group + 1) + " " + "V" * 7,
        limit=GROUP_LIMIT,
        after=(row_grad,),
        scratch=[
            pltpu.VMEM(head_weight.shape, bf16),
            pltpu.VMEM((group, total + 16, model_width), bf16),
            pltpu.SemaphoreType.DMA((group + 1,)),
        ],
    )

    (packed,) = call(
        functools.partial(weights_kernel, group, owners),
        "weight_parts",
        [((owners, model_width // owners, cols + HEAD_DIM + width), bf16)],
        (*row_all, *normed_all, *group_forward, projection, mixing_weight, table_part),
        "V" * (2 * group + 10) + " H",
        limit=28,
    )
    arrived = lax.all_to_all(packed, DEV, 0, 0, tiled=True)

    late_weight, _ = lax.optimization_barrier((expand_weight, packed))
    weight = late_weight.swapaxes(0, 1)
    out_grad, grad_part = call(
        trunk_kernel,
        "trunk",
        [((total, model_width), bf16), ((total, model_width), f32)],
        (lengths, normed, row_grad, projection, mixing_weight, weight),
        "SHHHHR VV",
        limit=28,
        scratch=[pltpu.VMEM((4, total, cols), bf16), pltpu.VMEM(weight.shape, bf16), pltpu.SemaphoreType.DMA((4,))],
        after=(packed,),
    )
    (grad_inputs,) = call(
        inputs_kernel, "input_grads", [(inputs.shape, bf16)], (inputs, out_grad, grad_part, swap(grad_part)), "HVVV H", limit=48
    )
    book_grads = leaf_book(got, leaf_grad, books, width, (packed,))
    share = model_width // owners
    expand, mixing, table_share = call(
        functools.partial(final_kernel, group),
        "weight_sums",
        [((share, 4, cols), f32), ((share, cols), f32), ((own, width), f32)],
        (arrived,),
        "V HHH",
        limit=28,
    )
    return grad_inputs, expand, mixing.T, table_share, book_grads


def solution(mesh):
    grid = Mesh(mesh.devices.reshape(2, 4, 4, 4), ("section",) + DEV)
    return jax.shard_map(
        body,
        mesh=grid,
        in_specs=(
            P(None, DEV, None),
            P(None, DEV, None),
            P(None, None, "section"),
            P("section", None),
            P(),
            P(None, DEV, None),
            P(None, DEV),
            P(None, DEV),
            P("section", None),
            P(DEV, "section", None),
        ),
        out_specs=(
            P(None, DEV, None),
            P(DEV, None, "section"),
            P("section", DEV),
            P(("section",) + DEV, None),
            P(DEV, "section", None),
        ),
        check_vma=False,
    )
```

```python
import functools

import jax
import jax.numpy as jnp
from jax import lax
from jax.experimental import pallas as pl
from jax.experimental.pallas import tpu as pltpu
from jax.sharding import Mesh
from jax.sharding import PartitionSpec as P

HEAD_DIM = 128
SEQ_MOST = 64
SEQS = 4
CAP = 4
PARTS = 2
eps = 1e-05
DEV = ("y", "z", "x")
f32 = jnp.float32
bf16 = jnp.bfloat16
NN = ((1,), (0,))
NT = ((1,), (1,))
TN = ((0,), (0,))


def swap(part):
    return lax.ppermute(part, "section", [(0, 1), (1, 0)])


def from_pair(part, axis, other):
    count = lax.axis_size(axis)
    return lax.ppermute(part, axis, [(i, i ^ other) for i in range(count)])


def member():
    return lax.rem(lax.axis_index("x"), 2) + 2 * lax.rem(lax.axis_index("y"), 2)


def from_member(part, other):
    count = lax.axis_size("x")
    flip = count * (other // 2) + other % 2
    return lax.ppermute(part, ("y", "x"), [(i, i ^ flip) for i in range(lax.axis_size("y") * count)])


def dot(left, right, dims):
    return lax.dot_general(left, right, (dims, ((), ())), preferred_element_type=f32)


def iota(shape, dim):
    return lax.broadcasted_iota(jnp.int32, shape, dim)


def row_norm(argument):
    row_mean = jnp.mean(argument, axis=-1, keepdims=True)
    centered = argument - row_mean
    variance = jnp.mean(centered * centered, axis=-1, keepdims=True)
    inverse = lax.rsqrt(variance + eps)
    return (centered * inverse, inverse)


def norm_back(incoming, normed, inverse):
    mean_in = jnp.mean(incoming, axis=-1, keepdims=True)
    mean_dot = jnp.mean(incoming * normed, axis=-1, keepdims=True)
    return (incoming - mean_in - normed * mean_dot) * inverse


def call(kernel, name, outs, args, kinds, after=(), scratch=(), limit=56, flops=0, token=False):
    in_kinds, out_kinds = kinds.split()
    if token:
        outs, out_kinds = [*outs, ((8, 128), f32)], out_kinds + "V"
    assert len(in_kinds) == len(args) and len(out_kinds) == len(outs), name
    spaces = {"V": pltpu.VMEM, "S": pltpu.SMEM, "H": pl.ANY, "R": pl.ANY}
    held = [pltpu.VMEM(a.shape, a.dtype) for a, k in zip(args, in_kinds) if k == "H"]
    held += [pltpu.VMEM(s, d) for (s, d), k in zip(outs, out_kinds) if k == "H"]
    sems = [pltpu.SemaphoreType.DMA((len(held),))] if held else []

    def run(*refs):
        ins = list(refs[: len(args)])
        refs = refs[len(args) + len(after) :]
        results = list(refs[: len(outs)])
        buffers = list(refs[len(outs) : len(outs) + len(held)])
        rest = refs[len(outs) + len(held) + len(sems) :]
        sem = refs[len(outs) + len(held)] if held else None
        count = 0
        first, last = [], []
        for i, kind in enumerate(in_kinds):
            if kind == "H":
                first.append(pltpu.make_async_copy(ins[i], buffers[count], sem.at[count]))
                first[-1].start()
                ins[i] = buffers[count]
                count += 1
        for i, kind in enumerate(out_kinds):
            if kind == "H":
                last.append(pltpu.make_async_copy(buffers[count], results[i], sem.at[count]))
                results[i] = buffers[count]
                count += 1
        for copy in first:
            copy.wait()
        if token:
            results.pop()[...] = jnp.zeros((8, 128), f32)
        kernel(*ins, *results, *rest)
        for copy in last:
            copy.start()
        for copy in last:
            copy.wait()

    return pl.pallas_call(
        run,
        in_specs=[pl.BlockSpec(memory_space=spaces[k]) for k in in_kinds] + [pl.BlockSpec(memory_space=pl.ANY)] * len(after),
        out_specs=[pl.BlockSpec(memory_space=spaces[k]) for k in out_kinds],
        out_shape=[jax.ShapeDtypeStruct(s, d) for s, d in outs],
        scratch_shapes=held + sems + list(scratch),
        compiler_params=pltpu.CompilerParams(vmem_limit_bytes=limit * 2**20),
        cost_estimate=pl.CostEstimate(flops=flops, bytes_accessed=0, transcendentals=0),
        name=name,
    )(*args, *after)


def one_hot(slots_row, count):
    return jnp.where(iota((count, slots_row.shape[1]), 0) == slots_row, 1.0, 0.0).astype(bf16)


def dispatch_kernel(owners, books, half, cluster_ref, item_ref, saved_ref, sent_ref, slot_ref, mark_ref):
    micro, rows = cluster_ref.shape
    width = saved_ref.shape[2]
    each = micro * CAP
    before = jnp.where(iota((rows, rows), 0) < iota((rows, rows), 1), 1.0, 0.0).astype(bf16)
    same = jnp.where(iota((rows, rows), 0) == iota((rows, rows), 1), 1.0, 0.0).astype(bf16)
    kind = iota((128, rows), 0)
    rows_out, codes_out = 0.0, 0.0
    for m in range(micro):
        target, item = cluster_ref[m : m + 1], item_ref[m : m + 1]
        owner, local = target // books, target % books
        marks = jnp.where(iota((owners, rows), 0) == owner, 1.0, 0.0)
        earlier = dot(marks.astype(bf16), before, NN)
        rank = jnp.sum(earlier * marks, axis=0, keepdims=True).astype(jnp.int32)
        slot = owner * each + m * CAP + rank
        slot_ref[m : m + 1] = slot
        code = jnp.where(
            kind == 0,
            local + 1,
            jnp.where(kind == 1, item // half, jnp.where(kind == 2, item % half, jnp.where(kind == 3, owner, 0))),
        )
        code = code.astype(f32).astype(bf16)
        pick = one_hot(slot, owners * each)
        rows_out += dot(pick, saved_ref[m], NN)
        codes_out += dot(pick, code, NT)
        turned = dot(same, code, NT)
        mark_ref[m * rows : (m + 1) * rows] = jnp.broadcast_to(
            turned[:, 3:4] * books + turned[:, 0:1] - 1.0, (rows, 128)
        )
    sent_ref[:, :width] = rows_out.astype(bf16)
    sent_ref[:, width:] = codes_out.astype(bf16)


def first_kernel(group, owners, length_ref, input_ref, saved_ref, table_ref, norm_ref, logit_ref, stat_ref, turned_ref):
    micro, count, depth = input_ref.shape
    for m in range(micro):
        norm_ref[m * count : (m + 1) * count] = row_norm(input_ref[m].astype(f32))[0].astype(bf16)
    lane = iota((16, depth), 1)
    held = jnp.zeros((16, depth), f32)
    for m in range(micro):
        for i in range(SEQS):
            held = jnp.where(lane == m * SEQS + i, length_ref[m, 0, i].astype(f32), held)
    norm_ref[micro * count :] = held.astype(bf16)
    half, width = table_ref.shape
    rows = table_ref[...].astype(f32).reshape(owners, group, half // owners // group, width)
    turned = jnp.concatenate([rows[:, q].reshape(half // group, width) for q in range(group)], axis=0).astype(bf16)
    turned_ref[...] = turned
    logits = dot(saved_ref[...], turned, NT)
    logit_ref[...] = logits
    peak = jnp.max(logits, axis=1, keepdims=True)
    mass = jnp.sum(jnp.exp(logits - peak), axis=1, keepdims=True)
    stat_ref[...] = jnp.where(iota(stat_ref.shape, 1) == 0, peak, mass)


def joined(mine_ref, other_ref):
    peak_a, mass_a = mine_ref[:, 0:1], mine_ref[:, 1:2]
    peak_b, mass_b = other_ref[:, 0:1], other_ref[:, 1:2]
    peak = jnp.maximum(peak_a, peak_b)
    return peak, mass_a * jnp.exp(peak_a - peak) + mass_b * jnp.exp(peak_b - peak)


def top_grad_kernel(group, own, logit_ref, mine_ref, other_ref, mark_ref, table_ref, saved_ref, *out_refs):
    row_ref, grad_refs = out_refs[0], out_refs[1:]
    half = table_ref.shape[0]
    quarter = half // group
    piece = own // group
    base = lax.axis_index("section") * half
    me = lax.rem(lax.axis_index("z"), 2)
    peak, mass = joined(mine_ref, other_ref)
    target = mark_ref[:, 0:1].astype(jnp.int32) - base
    total = 0.0
    column = iota((mark_ref.shape[0], quarter), 1)
    for q in range(group):
        index = (column // piece) * own + q * piece + column % piece
        cols = pl.ds(q * quarter, quarter)
        probs = jnp.exp(logit_ref[:, cols] - peak) / mass
        grad = (probs - jnp.where(index == target, 1.0, 0.0)).astype(bf16)
        total += dot(grad, table_ref[cols, :], NN)
        for s in range(group):

            @pl.when(lax.rem(me + s, group) == q)
            def _(s=s, grad=grad):
                grad_refs[s][:, :quarter] = grad
                grad_refs[s][:, quarter:] = saved_ref[...]

    row_ref[...] = total


def table_kernel(owners, *refs):
    *in_refs, keep_ref, send_ref = refs
    lanes = keep_ref.shape[2]
    part = in_refs[0].shape[1] - 2 * lanes
    total = sum(dot(r[:, :part], r[:, part:], TN) for r in in_refs)
    halves = [total[:, i * lanes : (i + 1) * lanes].reshape(owners, -1, lanes).astype(bf16) for i in range(2)]
    bit = lax.axis_index("z") // 2
    for mine in range(2):

        @pl.when(bit == mine)
        def _(mine=mine):
            keep_ref[...] = halves[mine]
            send_ref[...] = halves[1 - mine]


def masked_product(code_ref, left_ref, width, book_ref, out_ref, dims, group, ready):
    lines = 256
    out_ref[...] = jnp.zeros_like(out_ref)

    def step(i, carry):
        ready(i)
        books = book_ref[pl.ds(i * group, group)]
        if dims == NT:
            right = jnp.concatenate([books[k] for k in range(group)], axis=1)
        else:
            right = books.reshape(-1, books.shape[2])
        for r in range(0, out_ref.shape[0], lines):
            some = pl.ds(r, lines)
            left, code = left_ref[some, :width], code_ref[some, :]
            parts = []
            for k in range(group):
                here = code == (i * group + k + 1).astype(f32).astype(bf16)
                parts.append(jnp.where(here, left, jnp.zeros_like(left)))
            out_ref[some, :] += dot(jnp.concatenate(parts, axis=1), right, dims)
        return carry

    lax.fori_loop(0, book_ref.shape[0] // group, step, 0)


FIRST_LIMIT = 40
GROUP_LIMIT = 40
BOOK_GROUP = 16
BOOK_COPIES = 4


def leaf_scores_kernel(got_in, book_in, out_ref, stat_ref, got_ref, book_ref, code_ref, got_sem, sem):
    width = book_ref.shape[2]
    steps = book_ref.shape[0] // BOOK_GROUP
    piece = BOOK_GROUP // BOOK_COPIES

    def copies(i):
        for j in range(BOOK_COPIES):
            some = pl.ds(i * BOOK_GROUP + j * piece, piece)
            yield pltpu.make_async_copy(book_in.at[some], book_ref.at[some], sem.at[i, j])

    got_copy = pltpu.make_async_copy(got_in, got_ref, got_sem)
    got_copy.start()
    for copy in copies(0):
        copy.start()
    got_copy.wait()
    code_ref[...] = jnp.broadcast_to(got_ref[:, width : width + 1], code_ref.shape)
    for copy in copies(1):
        copy.start()

    def ready(i):
        for copy in copies(i):
            copy.wait()

        @pl.when(i + 2 < steps)
        def _():
            for copy in copies(i + 2):
                copy.start()

    masked_product(code_ref, got_ref, width, book_ref, out_ref, NT, BOOK_GROUP, ready)
    scores = out_ref[...]
    peak = jnp.max(scores, axis=1, keepdims=True)
    mass = jnp.sum(jnp.exp(scores - peak), axis=1, keepdims=True)
    stat_ref[...] = jnp.where(iota(stat_ref.shape, 1) == 0, peak, mass)


def leaf_back_kernel(got_ref, score_ref, mine_ref, other_ref, book_ref, back_ref, grad_ref, code_ref, total_ref):
    items, width = book_ref.shape[1:]
    code = got_ref[:, width : width + 1]
    code_ref[...] = jnp.broadcast_to(code, code_ref.shape)
    high = got_ref[:, width + 1 : width + 2].astype(f32).astype(jnp.int32)
    low = got_ref[:, width + 2 : width + 3].astype(f32).astype(jnp.int32)
    peak, mass = joined(mine_ref, other_ref)
    probs = jnp.exp(score_ref[...] - peak) / mass
    hit = (iota(probs.shape, 1) == low) & (high == lax.axis_index("section"))
    grad = jnp.where(code.astype(f32) > 0, probs - jnp.where(hit, 1.0, 0.0), 0.0)
    grad_ref[...] = grad.astype(bf16)
    masked_product(code_ref, grad_ref, items, book_ref, total_ref, NN, 32, lambda i: None)
    back_ref[...] = total_ref[...].astype(bf16)


def leaf_book_kernel(got_ref, grad_ref, out_ref, code_ref, turned_ref, held_ref, sem):
    books, items, width = out_ref.shape
    group = books // sem.shape[0]
    slots = got_ref.shape[0]
    turned_ref[...] = grad_ref[...].astype(f32).T.astype(bf16)
    code_ref[...] = jnp.broadcast_to(got_ref[:, width : width + 1].astype(f32), (slots, items)).T.astype(bf16)
    rows = got_ref[:, :width]
    copies = []
    for i in range(books // group):
        some = pl.ds(i * group, group)
        turned, code = turned_ref[...], code_ref[...]
        parts = []
        for k in range(group):
            here = code == (i * group + k + 1)
            parts.append(jnp.where(here, turned, jnp.zeros_like(turned)))
        grads = dot(jnp.concatenate(parts, axis=0), rows, NN)
        held_ref[some] = grads.reshape(group, items, width).astype(bf16)
        copies.append(pltpu.make_async_copy(held_ref.at[some], out_ref.at[some], sem.at[i]))
        copies[-1].start()
    for copy in copies:
        copy.wait()


def leaf_scores(got, book, after):
    books, items, width = book.shape
    slots = got.shape[0]
    return call(
        leaf_scores_kernel,
        "leaf_scores",
        [((slots, items), f32), ((slots, 128), f32), (got.shape, bf16), (book.shape, bf16)],
        (got, book),
        "RR VVVV", limit=42,
        flops=2 * slots * books * items * width,
        scratch=[
            pltpu.VMEM((slots, width), bf16),
            pltpu.SemaphoreType.DMA,
            pltpu.SemaphoreType.DMA((books // BOOK_GROUP, BOOK_COPIES)),
        ],
        after=after,
    )


def leaf_back(got, scores, mine, other, book, after):
    books, items, width = book.shape
    slots = got.shape[0]
    return call(
        leaf_back_kernel,
        "leaf_back",
        [((slots, width), bf16), ((slots, items), bf16)],
        (got, scores, mine, other, book),
        "VVVVV HH",
        limit=28,
        scratch=[pltpu.VMEM((slots, items), bf16), pltpu.VMEM((slots, width), f32)],
        after=after,
    )


def leaf_book(got, grads, books, width, after):
    slots, items = grads.shape
    group = 4
    return call(
        leaf_book_kernel,
        "leaf_book",
        [((books, items, width), bf16)],
        (got, grads),
        "HH R",
        scratch=[
            pltpu.VMEM((items, slots), bf16),
            pltpu.VMEM((items, slots), bf16),
            pltpu.VMEM((books, items, width), bf16),
            pltpu.SemaphoreType.DMA((books // group,)),
        ],
        after=after,
    )[0]


def slope_of(argument, logistic):
    return logistic * (1.0 + argument * (1.0 - logistic))


def seq_mask(sizes, rows):
    row, col = iota((rows, rows), 0), iota((rows, rows), 1)
    row_seg, col_seg, end = 0, 0, 0
    for size in sizes:
        end = end + size
        row_seg += jnp.where(row >= end, 1, 0)
        col_seg += jnp.where(col >= end, 1, 0)
    return jnp.where((row_seg == col_seg) & (col <= row), 1.0 / SEQ_MOST, 0.0)


def held_sizes(held, m):
    held = held.astype(f32)[0:1].astype(jnp.int32)
    return [held[:, m * SEQS + i : m * SEQS + i + 1] for i in range(SEQS)]


def attend_all(acts, masks):
    scores = [dot(query, key, NT) for _, _, query, key in acts]
    logistics = [jax.nn.sigmoid(score) for score in scores]
    attention = [(a * b * mask).astype(bf16) for a, b, mask in zip(scores, logistics, masks)]
    mixed = [dot(a, act[1], NN) for a, act in zip(attention, acts)]
    back = [slope_of(a, b) * mask for a, b, mask in zip(scores, logistics, masks)]
    normed = [row_norm(one) for one in mixed]
    return [(a, b, n, jnp.broadcast_to(i, n.shape)) for a, b, (n, i) in zip(attention, back, normed)]


def my_head():
    return pl.ds(pl.multiple_of(member() * HEAD_DIM, HEAD_DIM), HEAD_DIM)


def head_weight_kernel(weight_in, out_ref, part_ref, flat_ref, sem):
    copy = pltpu.make_async_copy(weight_in.at[:, :, my_head()], part_ref, sem)
    copy.start()
    copy.wait()
    flat_ref[...] = part_ref[...].astype(f32).reshape(flat_ref.shape)
    depth, parts = weight_in.shape[:2]
    for t in range(parts):
        out_ref[:, t * HEAD_DIM : (t + 1) * HEAD_DIM] = flat_ref[pl.ds(t, depth, stride=parts), :].astype(bf16)


def group_forward_kernel(*refs):
    *norm_ins, weight_in, act_ref, slope_ref, att_ref, back_ref, out_ref, inverse_ref, prod_ref = refs[:-3]
    weight_ref, norm_ref, sem = refs[-3:]
    pairs = [(weight_in, weight_ref)] + [(one, norm_ref.at[s]) for s, one in enumerate(norm_ins)]
    copies = [pltpu.make_async_copy(a, b, sem.at[i]) for i, (a, b) in enumerate(pairs)]
    for copy in copies:
        copy.start()
    for copy in copies:
        copy.wait()
    rows = att_ref.shape[1]
    total = out_ref.shape[0] // len(norm_ins)
    weight = weight_ref[...]
    acts, masks, spans = [], [], []
    for s in range(len(norm_ins)):
        for m in range(total // rows):
            lines = pl.ds(s * total + m * rows, rows)
            pre_act = dot(norm_ref[s, m * rows : (m + 1) * rows, :], weight, NN)
            logistic = jax.nn.sigmoid(pre_act)
            act = (pre_act * logistic).astype(bf16)
            act_ref[lines, :] = act
            slope_ref[lines, :] = slope_of(pre_act, logistic)
            spans.append(lines)
            masks.append(seq_mask(held_sizes(norm_ref[s, total:, :128], m), rows))
            acts.append([act[:, t * HEAD_DIM : (t + 1) * HEAD_DIM] for t in range(4)])
    for lines, act, result in zip(spans, acts, attend_all(acts, masks)):
        att_ref[lines, :], back_ref[lines, :], out_ref[lines, :], inverse_ref[lines, :] = result
        prod_ref[lines, :] = (result[2] * act[0].astype(f32)).astype(bf16)


def attend_back_all(incoming, acts, results):
    mixed = [
        norm_back(a * act[0].astype(f32), normed, inverse).astype(bf16)
        for a, act, (_, _, normed, inverse) in zip(incoming, acts, results)
    ]
    grads = [dot(a, act[1], NT) for a, act in zip(mixed, acts)]
    values = [dot(result[0], a, TN) for result, a in zip(results, mixed)]
    grads = [(a * result[1]).astype(bf16) for a, result in zip(grads, results)]
    queries = [dot(a, act[3], NN) for a, act in zip(grads, acts)]
    keys = [dot(a, act[2], TN) for a, act in zip(grads, acts)]
    gates = [a * result[2] for a, result in zip(incoming, results)]
    return list(zip(gates, values, queries, keys))


def rows_kernel(slot_ref, returned_ref, out_ref):
    micro, rows = slot_ref.shape
    for m in range(micro):
        lines = pl.ds(m * rows, rows)
        pick = one_hot(slot_ref[m : m + 1], returned_ref.shape[0])
        out_ref[lines, :] = dot(pick, returned_ref[...], TN)


def add_kernel(mine_ref, other_ref, top_ref, out_ref):
    out_ref[...] = (mine_ref[...] + other_ref[...] + top_ref[...]).astype(bf16)


def trunk_kernel(length_ref, norm_ref, row_ref, proj_ref, mix_ref, weight_in, og_ref, part_ref, pre_ref, weight_ref, sem):
    copies = [pltpu.make_async_copy(weight_in.at[t], weight_ref.at[t], sem.at[t]) for t in range(4)]
    for copy in copies:
        copy.start()
    rows = HEAD_DIM
    total, cols = row_ref.shape[0], weight_ref.shape[2]
    out_grad = dot(row_ref[...], proj_ref[...], NT).astype(bf16)
    og_ref[...] = out_grad
    grad_product = dot(out_grad, mix_ref[...], NT)
    for copy in copies:
        copy.wait()
    for m in range(total // rows):
        lines = pl.ds(m * rows, rows)
        normed = norm_ref[lines, :]
        acts, slopes = [], []
        for t in range(4):
            pre_act = dot(normed, weight_ref[t], NN)
            logistic = jax.nn.sigmoid(pre_act)
            acts.append((pre_act * logistic).astype(bf16))
            slopes.append(slope_of(pre_act, logistic))
        heads = [slice(h * HEAD_DIM, (h + 1) * HEAD_DIM) for h in range(cols // HEAD_DIM)]
        acts = [[act[:, lanes] for act in acts] for lanes in heads]
        masks = [seq_mask([length_ref[m, 0, i] for i in range(SEQS)], rows)] * len(heads)
        incoming = [grad_product[m * rows : (m + 1) * rows, lanes] for lanes in heads]
        for lanes, grads in zip(heads, attend_back_all(incoming, acts, attend_all(acts, masks))):
            for t, grad in enumerate(grads):
                pre_ref[t, lines, lanes] = (grad * slopes[t][:, lanes]).astype(bf16)
    part_ref[...] = sum(dot(pre_ref[t], weight_ref[t], NT) for t in range(4))


def inputs_kernel(input_ref, og_ref, mine_ref, other_ref, out_ref):
    micro, rows, _ = input_ref.shape
    for m in range(micro):
        lines = pl.ds(m * rows, rows)
        normed, inverse = row_norm(input_ref[m].astype(f32))
        grad = norm_back(mine_ref[lines, :] + other_ref[lines, :], normed, inverse)
        out_ref[m] = (og_ref[lines, :].astype(f32) + grad).astype(bf16)


def weights_kernel(group, owners, *refs):
    row_refs, norm_refs = refs[:group], refs[group : 2 * group]
    act_ref, slope_ref, att_ref, back_ref, out_ref, inverse_ref, prod_ref, proj_ref, mix_ref, *table_refs, packed_ref = refs[2 * group :]
    total = row_refs[0].shape[0]
    rows = att_ref.shape[1]
    cols = act_ref.shape[1]
    count = total // rows
    mix = mix_ref[my_head(), :]
    mixing, expand = 0.0, 0.0
    spans, incoming = [], []
    for s in range(group):
        out_grad = dot(row_refs[s][...], proj_ref[...], NT).astype(bf16)
        mixing += dot(out_grad, prod_ref[s * total : (s + 1) * total, :], TN)
        grad_product = dot(out_grad, mix, NT)
        for m in range(count):
            spans.append(pl.ds(s * total + m * rows, rows))
            incoming.append(grad_product[m * rows : (m + 1) * rows])
    packed_ref[:, :, cols : cols + HEAD_DIM] = mixing.reshape(owners, -1, HEAD_DIM).astype(bf16)
    table = table_refs[0][...].astype(f32) + table_refs[1][...].astype(f32)
    packed_ref[:, :, cols + HEAD_DIM :] = table.astype(bf16)
    acts = [[act_ref[lines, t * HEAD_DIM : (t + 1) * HEAD_DIM] for t in range(4)] for lines in spans]
    results = [(att_ref[lines, :], back_ref[lines, :], out_ref[lines, :], inverse_ref[lines, :]) for lines in spans]
    grads = attend_back_all(incoming, acts, results)
    pre = [(jnp.concatenate(grad, axis=1) * slope_ref[lines, :]).astype(bf16) for grad, lines in zip(grads, spans)]
    for s in range(group):
        expand += dot(norm_refs[s][:total, :], jnp.concatenate(pre[s * count : (s + 1) * count], axis=0), TN)
    packed_ref[:, :, :cols] = expand.reshape(owners, -1, cols).astype(bf16)


def final_kernel(group, in_ref, expand_ref, mixing_ref, table_ref):
    cols = expand_ref.shape[2]
    side = range(group)
    for g in side:
        sources = [(y * group + z) * group + x for y in side for z in side for x in side if x % 2 + 2 * (y % 2) == g]
        total = sum(in_ref[i, :, : cols + HEAD_DIM].astype(f32) for i in sources)
        head = pl.ds(g * HEAD_DIM, HEAD_DIM)
        for t in range(4):
            expand_ref[:, t, head] = total[:, t * HEAD_DIM : (t + 1) * HEAD_DIM]
        mixing_ref[:, head] = total[:, cols:]
    width = table_ref.shape[1] // 2
    for z in side:
        total = sum(in_ref[(y * group + z) * group + x, :, cols + HEAD_DIM :].astype(f32) for y in side for x in side)
        part, half, count = z % PARTS, z // PARTS, total.shape[0]
        table_ref[part * count : (part + 1) * count, half * width : (half + 1) * width] = total


def body(
    inputs,
    lengths,
    expand_weight,
    mixing_weight,
    projection,
    saved_rows,
    cluster_ids,
    item_ids,
    top_table,
    codebook,
):
    micro, rows, model_width = inputs.shape
    total = micro * rows
    owners = lax.axis_size(DEV)
    group = lax.axis_size("x")
    half_clusters, width = top_table.shape
    books, items, _ = codebook.shape
    cols = expand_weight.shape[2]
    slots = owners * micro * CAP
    own = half_clusters // owners
    saved = saved_rows.reshape(total, width)

    sent, slot_ids, marks = call(
        functools.partial(dispatch_kernel, owners, books, items),
        "dispatch",
        [((slots, width + 128), bf16), ((micro, rows), jnp.int32), ((total, 128), f32)],
        (cluster_ids, item_ids, saved_rows),
        "HHH HVH", limit=56,
    )
    got = lax.all_to_all(sent.reshape(owners, slots // owners, -1), DEV, 0, 0, tiled=True).reshape(slots, -1)

    normed, logits, stats, table = call(
        functools.partial(first_kernel, PARTS, owners),
        "norms_and_logits",
        [
            ((total + 16, model_width), bf16),
            ((total, half_clusters), f32),
            ((total, 128), f32),
            (top_table.shape, bf16),
        ],
        (lengths, inputs, saved, top_table),
        "SHHH VVVV",
        limit=FIRST_LIMIT,
        after=(slot_ids,),
    )
    normed_all = [normed] + [from_member(normed, s) for s in range(1, group)]
    row_top, *top_grads, top_token = call(
        functools.partial(top_grad_kernel, PARTS, own),
        "top_grads",
        [((total, width), f32)] + [((total, half_clusters // PARTS + width), bf16)] * PARTS,
        (logits, stats, swap(stats), marks, table, saved),
        "VVVHHH " + "H" * (1 + PARTS),
        limit=40,
        token=True,
    )
    top_all = [top_grads[0], from_pair(top_grads[1], "z", 1)]

    leaf, leaf_stats, got_held, book_held = leaf_scores(got, codebook, (top_token, normed[:8, :128]))
    back, leaf_grad = leaf_back(
        got_held, leaf, leaf_stats, swap(leaf_stats), book_held, ()
    )
    returned = lax.all_to_all(back.reshape(owners, slots // owners, width), DEV, 0, 0, tiled=True)

    row_top = row_top + swap(row_top)
    head_weight, head_token = call(
        head_weight_kernel,
        "head_weight",
        [((model_width, 4 * HEAD_DIM), bf16)],
        (expand_weight,),
        "R H",
        scratch=[
            pltpu.VMEM((model_width, 4, HEAD_DIM), bf16),
            pltpu.VMEM((model_width * 4, HEAD_DIM), f32),
            pltpu.SemaphoreType.DMA,
        ],
        after=(back, sum(a[:8, :128] for a in normed_all[1:])),
        token=True,
    )

    table_keep, table_send, table_token = call(
        functools.partial(table_kernel, owners),
        "table_part",
        [((owners, own // PARTS, width // 2), bf16)] * 2,
        top_all,
        "V" * PARTS + " VV",
        limit=16,
        after=(back, head_token),
        token=True,
    )

    table_other = from_pair(table_send, "z", 2)

    (row_part,) = call(
        rows_kernel,
        "rows",
        [((total, width), f32)],
        (slot_ids, returned.reshape(slots, width)),
        "VH V",
        limit=28,
        after=(table_token,),
    )
    (row_grad,) = call(add_kernel, "row_grad", [((total, width), bf16)], (row_part, swap(row_part), row_top), "VVV V", limit=28)
    row_all = [row_grad] + [from_member(row_grad, s) for s in range(1, group)]

    group_rows = group * total
    group_forward = call(
        group_forward_kernel,
        "group_forward",
        [
            ((group_rows, 4 * HEAD_DIM), bf16),
            ((group_rows, 4 * HEAD_DIM), f32),
            ((group_rows, rows), bf16),
            ((group_rows, rows), f32),
            ((group_rows, HEAD_DIM), f32),
            ((group_rows, HEAD_DIM), f32),
            ((group_rows, HEAD_DIM), bf16),
        ],
        (*normed_all, head_weight),
        "R" * (group + 1) + " " + "V" * 7,
        limit=GROUP_LIMIT,
        after=(row_grad,),
        scratch=[
            pltpu.VMEM(head_weight.shape, bf16),
            pltpu.VMEM((group, total + 16, model_width), bf16),
            pltpu.SemaphoreType.DMA((group + 1,)),
        ],
    )

    (packed,) = call(
        functools.partial(weights_kernel, group, owners),
        "weight_parts",
        [((owners, model_width // owners, cols + HEAD_DIM + width // 2), bf16)],
        (*row_all, *normed_all, *group_forward, projection, mixing_weight, table_keep, table_other),
        "V" * (2 * group + 11) + " H",
        limit=28,
    )
    arrived = lax.all_to_all(packed, DEV, 0, 0, tiled=True)

    late_weight, _ = lax.optimization_barrier((expand_weight, packed))
    weight = late_weight.swapaxes(0, 1)
    out_grad, grad_part = call(
        trunk_kernel,
        "trunk",
        [((total, model_width), bf16), ((total, model_width), f32)],
        (lengths, normed, row_grad, projection, mixing_weight, weight),
        "SHHHHR VV",
        limit=28,
        scratch=[pltpu.VMEM((4, total, cols), bf16), pltpu.VMEM(weight.shape, bf16), pltpu.SemaphoreType.DMA((4,))],
        after=(packed,),
    )
    (grad_inputs,) = call(
        inputs_kernel, "input_grads", [(inputs.shape, bf16)], (inputs, out_grad, grad_part, swap(grad_part)), "HVVV H", limit=48
    )
    book_grads = leaf_book(got, leaf_grad, books, width, (packed,))
    share = model_width // owners
    expand, mixing, table_share = call(
        functools.partial(final_kernel, group),
        "weight_sums",
        [((share, 4, cols), f32), ((share, cols), f32), ((own, width), f32)],
        (arrived,),
        "V HHH",
        limit=28,
    )
    return grad_inputs, expand, mixing.T, table_share, book_grads


def solution(mesh):
    grid = Mesh(mesh.devices.reshape(2, 4, 4, 4), ("section",) + DEV)
    return jax.shard_map(
        body,
        mesh=grid,
        in_specs=(
            P(None, DEV, None),
            P(None, DEV, None),
            P(None, None, "section"),
            P("section", None),
            P(),
            P(None, DEV, None),
            P(None, DEV),
            P(None, DEV),
            P("section", None),
            P(DEV, "section", None),
        ),
        out_specs=(
            P(None, DEV, None),
            P(DEV, None, "section"),
            P("section", DEV),
            P(("section",) + DEV, None),
            P(DEV, "section", None),
        ),
        check_vma=False,
    )
```

```python
import functools

import jax
import jax.numpy as jnp
from jax import lax
from jax.experimental import pallas as pl
from jax.experimental.pallas import tpu as pltpu
from jax.sharding import Mesh
from jax.sharding import PartitionSpec as P

HEAD_DIM = 128
SEQ_MOST = 64
SEQS = 4
CAP = 4
PARTS = 2
eps = 1e-05
DEV = ("y", "z", "x")
f32 = jnp.float32
bf16 = jnp.bfloat16
NN = ((1,), (0,))
NT = ((1,), (1,))
TN = ((0,), (0,))


def swap(part):
    return lax.ppermute(part, "section", [(0, 1), (1, 0)])


def from_pair(part, axis, other):
    count = lax.axis_size(axis)
    return lax.ppermute(part, axis, [(i, i ^ other) for i in range(count)])


def member():
    return lax.rem(lax.axis_index("x"), 2) + 2 * lax.rem(lax.axis_index("y"), 2)


def from_member(part, other):
    count = lax.axis_size("x")
    flip = count * (other // 2) + other % 2
    return lax.ppermute(part, ("y", "x"), [(i, i ^ flip) for i in range(lax.axis_size("y") * count)])


def dot(left, right, dims):
    return lax.dot_general(left, right, (dims, ((), ())), preferred_element_type=f32)


def iota(shape, dim):
    return lax.broadcasted_iota(jnp.int32, shape, dim)


def row_norm(argument):
    row_mean = jnp.mean(argument, axis=-1, keepdims=True)
    centered = argument - row_mean
    variance = jnp.mean(centered * centered, axis=-1, keepdims=True)
    inverse = lax.rsqrt(variance + eps)
    return (centered * inverse, inverse)


def norm_back(incoming, normed, inverse):
    mean_in = jnp.mean(incoming, axis=-1, keepdims=True)
    mean_dot = jnp.mean(incoming * normed, axis=-1, keepdims=True)
    return (incoming - mean_in - normed * mean_dot) * inverse


def call(kernel, name, outs, args, kinds, after=(), scratch=(), limit=56, flops=0, token=False):
    in_kinds, out_kinds = kinds.split()
    if token:
        outs, out_kinds = [*outs, ((8, 128), f32)], out_kinds + "V"
    assert len(in_kinds) == len(args) and len(out_kinds) == len(outs), name
    spaces = {"V": pltpu.VMEM, "S": pltpu.SMEM, "H": pl.ANY, "R": pl.ANY}
    held = [pltpu.VMEM(a.shape, a.dtype) for a, k in zip(args, in_kinds) if k == "H"]
    held += [pltpu.VMEM(s, d) for (s, d), k in zip(outs, out_kinds) if k == "H"]
    sems = [pltpu.SemaphoreType.DMA((len(held),))] if held else []

    def run(*refs):
        ins = list(refs[: len(args)])
        refs = refs[len(args) + len(after) :]
        results = list(refs[: len(outs)])
        buffers = list(refs[len(outs) : len(outs) + len(held)])
        rest = refs[len(outs) + len(held) + len(sems) :]
        sem = refs[len(outs) + len(held)] if held else None
        count = 0
        first, last = [], []
        for i, kind in enumerate(in_kinds):
            if kind == "H":
                first.append(pltpu.make_async_copy(ins[i], buffers[count], sem.at[count]))
                first[-1].start()
                ins[i] = buffers[count]
                count += 1
        for i, kind in enumerate(out_kinds):
            if kind == "H":
                last.append(pltpu.make_async_copy(buffers[count], results[i], sem.at[count]))
                results[i] = buffers[count]
                count += 1
        for copy in first:
            copy.wait()
        if token:
            results.pop()[...] = jnp.zeros((8, 128), f32)
        kernel(*ins, *results, *rest)
        for copy in last:
            copy.start()
        for copy in last:
            copy.wait()

    return pl.pallas_call(
        run,
        in_specs=[pl.BlockSpec(memory_space=spaces[k]) for k in in_kinds] + [pl.BlockSpec(memory_space=pl.ANY)] * len(after),
        out_specs=[pl.BlockSpec(memory_space=spaces[k]) for k in out_kinds],
        out_shape=[jax.ShapeDtypeStruct(s, d) for s, d in outs],
        scratch_shapes=held + sems + list(scratch),
        compiler_params=pltpu.CompilerParams(vmem_limit_bytes=limit * 2**20),
        cost_estimate=pl.CostEstimate(flops=flops, bytes_accessed=0, transcendentals=0),
        name=name,
    )(*args, *after)


def one_hot(slots_row, count):
    return jnp.where(iota((count, slots_row.shape[1]), 0) == slots_row, 1.0, 0.0).astype(bf16)


def dispatch_kernel(owners, books, half, cluster_ref, item_ref, saved_ref, sent_ref, slot_ref, mark_ref):
    micro, rows = cluster_ref.shape
    width = saved_ref.shape[2]
    each = micro * CAP
    before = jnp.where(iota((rows, rows), 0) < iota((rows, rows), 1), 1.0, 0.0).astype(bf16)
    same = jnp.where(iota((rows, rows), 0) == iota((rows, rows), 1), 1.0, 0.0).astype(bf16)
    kind = iota((128, rows), 0)
    rows_out, codes_out = 0.0, 0.0
    for m in range(micro):
        target, item = cluster_ref[m : m + 1], item_ref[m : m + 1]
        owner, local = target // books, target % books
        marks = jnp.where(iota((owners, rows), 0) == owner, 1.0, 0.0)
        earlier = dot(marks.astype(bf16), before, NN)
        rank = jnp.sum(earlier * marks, axis=0, keepdims=True).astype(jnp.int32)
        slot = owner * each + m * CAP + rank
        slot_ref[m : m + 1] = slot
        code = jnp.where(
            kind == 0,
            local + 1,
            jnp.where(kind == 1, item // half, jnp.where(kind == 2, item % half, jnp.where(kind == 3, owner, 0))),
        )
        code = code.astype(f32).astype(bf16)
        pick = one_hot(slot, owners * each)
        rows_out += dot(pick, saved_ref[m], NN)
        codes_out += dot(pick, code, NT)
        turned = dot(same, code, NT)
        mark_ref[m * rows : (m + 1) * rows] = jnp.broadcast_to(
            turned[:, 3:4] * books + turned[:, 0:1] - 1.0, (rows, 128)
        )
    sent_ref[:, :width] = rows_out.astype(bf16)
    sent_ref[:, width:] = codes_out.astype(bf16)


def first_kernel(group, owners, length_ref, input_ref, saved_ref, table_ref, norm_ref, logit_ref, stat_ref, turned_ref):
    micro, count, depth = input_ref.shape
    for m in range(micro):
        norm_ref[m * count : (m + 1) * count] = row_norm(input_ref[m].astype(f32))[0].astype(bf16)
    lane = iota((16, depth), 1)
    held = jnp.zeros((16, depth), f32)
    for m in range(micro):
        for i in range(SEQS):
            held = jnp.where(lane == m * SEQS + i, length_ref[m, 0, i].astype(f32), held)
    norm_ref[micro * count :] = held.astype(bf16)
    half, width = table_ref.shape
    rows = table_ref[...].astype(f32).reshape(owners, group, half // owners // group, width)
    turned = jnp.concatenate([rows[:, q].reshape(half // group, width) for q in range(group)], axis=0).astype(bf16)
    turned_ref[...] = turned
    logits = dot(saved_ref[...], turned, NT)
    logit_ref[...] = logits
    peak = jnp.max(logits, axis=1, keepdims=True)
    mass = jnp.sum(jnp.exp(logits - peak), axis=1, keepdims=True)
    stat_ref[...] = jnp.where(iota(stat_ref.shape, 1) == 0, peak, mass)


def joined(mine_ref, other_ref):
    peak_a, mass_a = mine_ref[:, 0:1], mine_ref[:, 1:2]
    peak_b, mass_b = other_ref[:, 0:1], other_ref[:, 1:2]
    peak = jnp.maximum(peak_a, peak_b)
    return peak, mass_a * jnp.exp(peak_a - peak) + mass_b * jnp.exp(peak_b - peak)


def top_grad_kernel(group, own, logit_ref, mine_ref, other_ref, mark_ref, table_ref, saved_ref, *out_refs):
    row_ref, grad_refs = out_refs[0], out_refs[1:]
    half = table_ref.shape[0]
    quarter = half // group
    piece = own // group
    base = lax.axis_index("section") * half
    me = lax.rem(lax.axis_index("z"), 2)
    peak, mass = joined(mine_ref, other_ref)
    target = mark_ref[:, 0:1].astype(jnp.int32) - base
    total = 0.0
    column = iota((mark_ref.shape[0], quarter), 1)
    for q in range(group):
        index = (column // piece) * own + q * piece + column % piece
        cols = pl.ds(q * quarter, quarter)
        probs = jnp.exp(logit_ref[:, cols] - peak) / mass
        grad = (probs - jnp.where(index == target, 1.0, 0.0)).astype(bf16)
        total += dot(grad, table_ref[cols, :], NN)
        for s in range(group):

            @pl.when(lax.rem(me + s, group) == q)
            def _(s=s, grad=grad):
                grad_refs[s][:, :quarter] = grad
                grad_refs[s][:, quarter:] = saved_ref[...]

    row_ref[...] = total


def table_kernel(owners, *refs):
    *in_refs, keep_ref, send_ref = refs
    lanes = keep_ref.shape[2]
    part = in_refs[0].shape[1] - 2 * lanes
    total = sum(dot(r[:, :part], r[:, part:], TN) for r in in_refs)
    halves = [total[:, i * lanes : (i + 1) * lanes].reshape(owners, -1, lanes).astype(bf16) for i in range(2)]
    bit = lax.axis_index("z") // 2
    for mine in range(2):

        @pl.when(bit == mine)
        def _(mine=mine):
            keep_ref[...] = halves[mine]
            send_ref[...] = halves[1 - mine]


def masked_product(code_ref, left_ref, width, book_ref, out_ref, dims, group, ready):
    lines = 256
    out_ref[...] = jnp.zeros_like(out_ref)

    def step(i, carry):
        ready(i)
        books = book_ref[pl.ds(i * group, group)]
        if dims == NT:
            right = jnp.concatenate([books[k] for k in range(group)], axis=1)
        else:
            right = books.reshape(-1, books.shape[2])
        for r in range(0, out_ref.shape[0], lines):
            some = pl.ds(r, lines)
            left, code = left_ref[some, :width], code_ref[some, :]
            parts = []
            for k in range(group):
                here = code == (i * group + k + 1).astype(f32).astype(bf16)
                parts.append(jnp.where(here, left, jnp.zeros_like(left)))
            out_ref[some, :] += dot(jnp.concatenate(parts, axis=1), right, dims)
        return carry

    lax.fori_loop(0, book_ref.shape[0] // group, step, 0)


FIRST_LIMIT = 40
GROUP_LIMIT = 40
BOOK_GROUP = 16
BOOK_COPIES = 4


def leaf_scores_kernel(got_in, book_in, out_ref, stat_ref, got_ref, book_ref, code_ref, got_sem, sem):
    width = book_ref.shape[2]
    steps = book_ref.shape[0] // BOOK_GROUP
    piece = BOOK_GROUP // BOOK_COPIES

    def copies(i):
        for j in range(BOOK_COPIES):
            some = pl.ds(i * BOOK_GROUP + j * piece, piece)
            yield pltpu.make_async_copy(book_in.at[some], book_ref.at[some], sem.at[i, j])

    got_copy = pltpu.make_async_copy(got_in, got_ref, got_sem)
    got_copy.start()
    for copy in copies(0):
        copy.start()
    got_copy.wait()
    code_ref[...] = jnp.broadcast_to(got_ref[:, width : width + 1], code_ref.shape)
    for copy in copies(1):
        copy.start()

    def ready(i):
        for copy in copies(i):
            copy.wait()

        @pl.when(i + 2 < steps)
        def _():
            for copy in copies(i + 2):
                copy.start()

    masked_product(code_ref, got_ref, width, book_ref, out_ref, NT, BOOK_GROUP, ready)
    scores = out_ref[...]
    peak = jnp.max(scores, axis=1, keepdims=True)
    mass = jnp.sum(jnp.exp(scores - peak), axis=1, keepdims=True)
    stat_ref[...] = jnp.where(iota(stat_ref.shape, 1) == 0, peak, mass)


def leaf_back_kernel(got_ref, score_ref, mine_ref, other_ref, book_ref, back_ref, grad_ref, code_ref, total_ref):
    items, width = book_ref.shape[1:]
    code = got_ref[:, width : width + 1]
    code_ref[...] = jnp.broadcast_to(code, code_ref.shape)
    high = got_ref[:, width + 1 : width + 2].astype(f32).astype(jnp.int32)
    low = got_ref[:, width + 2 : width + 3].astype(f32).astype(jnp.int32)
    peak, mass = joined(mine_ref, other_ref)
    probs = jnp.exp(score_ref[...] - peak) / mass
    hit = (iota(probs.shape, 1) == low) & (high == lax.axis_index("section"))
    grad = jnp.where(code.astype(f32) > 0, probs - jnp.where(hit, 1.0, 0.0), 0.0)
    grad_ref[...] = grad.astype(bf16)
    masked_product(code_ref, grad_ref, items, book_ref, total_ref, NN, 32, lambda i: None)
    back_ref[...] = total_ref[...].astype(bf16)


def leaf_book_kernel(got_ref, grad_ref, out_ref, code_ref, turned_ref, held_ref, sem):
    books, items, width = out_ref.shape
    group = books // sem.shape[0]
    slots = got_ref.shape[0]
    turned_ref[...] = grad_ref[...].astype(f32).T.astype(bf16)
    code_ref[...] = jnp.broadcast_to(got_ref[:, width : width + 1].astype(f32), (slots, items)).T.astype(bf16)
    rows = got_ref[:, :width]
    copies = []
    for i in range(books // group):
        some = pl.ds(i * group, group)
        turned, code = turned_ref[...], code_ref[...]
        parts = []
        for k in range(group):
            here = code == (i * group + k + 1)
            parts.append(jnp.where(here, turned, jnp.zeros_like(turned)))
        grads = dot(jnp.concatenate(parts, axis=0), rows, NN)
        held_ref[some] = grads.reshape(group, items, width).astype(bf16)
        copies.append(pltpu.make_async_copy(held_ref.at[some], out_ref.at[some], sem.at[i]))
        copies[-1].start()
    for copy in copies:
        copy.wait()


def leaf_scores(got, book, after):
    books, items, width = book.shape
    slots = got.shape[0]
    return call(
        leaf_scores_kernel,
        "leaf_scores",
        [((slots, items), f32), ((slots, 128), f32), (got.shape, bf16), (book.shape, bf16)],
        (got, book),
        "RR VVVV", limit=42,
        flops=2 * slots * books * items * width,
        scratch=[
            pltpu.VMEM((slots, width), bf16),
            pltpu.SemaphoreType.DMA,
            pltpu.SemaphoreType.DMA((books // BOOK_GROUP, BOOK_COPIES)),
        ],
        after=after,
    )


def leaf_back(got, scores, mine, other, book, after):
    books, items, width = book.shape
    slots = got.shape[0]
    return call(
        leaf_back_kernel,
        "leaf_back",
        [((slots, width), bf16), ((slots, items), bf16)],
        (got, scores, mine, other, book),
        "VVVVV HH",
        limit=28,
        scratch=[pltpu.VMEM((slots, items), bf16), pltpu.VMEM((slots, width), f32)],
        after=after,
    )


def leaf_book(got, grads, books, width, after):
    slots, items = grads.shape
    group = 4
    return call(
        leaf_book_kernel,
        "leaf_book",
        [((books, items, width), bf16)],
        (got, grads),
        "HH R",
        scratch=[
            pltpu.VMEM((items, slots), bf16),
            pltpu.VMEM((items, slots), bf16),
            pltpu.VMEM((books, items, width), bf16),
            pltpu.SemaphoreType.DMA((books // group,)),
        ],
        after=after,
    )[0]


def slope_of(argument, logistic):
    return logistic * (1.0 + argument * (1.0 - logistic))


def seq_mask(sizes, rows):
    row, col = iota((rows, rows), 0), iota((rows, rows), 1)
    row_seg, col_seg, end = 0, 0, 0
    for size in sizes:
        end = end + size
        row_seg += jnp.where(row >= end, 1, 0)
        col_seg += jnp.where(col >= end, 1, 0)
    return jnp.where((row_seg == col_seg) & (col <= row), 1.0 / SEQ_MOST, 0.0)


def held_sizes(held, m):
    held = held.astype(f32)[0:1].astype(jnp.int32)
    return [held[:, m * SEQS + i : m * SEQS + i + 1] for i in range(SEQS)]


def attend_all(acts, masks):
    scores = [dot(query, key, NT) for _, _, query, key in acts]
    logistics = [jax.nn.sigmoid(score) for score in scores]
    attention = [(a * b * mask).astype(bf16) for a, b, mask in zip(scores, logistics, masks)]
    mixed = [dot(a, act[1], NN) for a, act in zip(attention, acts)]
    back = [slope_of(a, b) * mask for a, b, mask in zip(scores, logistics, masks)]
    normed = [row_norm(one) for one in mixed]
    return [(a, b, n, jnp.broadcast_to(i, n.shape)) for a, b, (n, i) in zip(attention, back, normed)]


def my_head():
    return pl.ds(pl.multiple_of(member() * HEAD_DIM, HEAD_DIM), HEAD_DIM)


def head_weight_kernel(weight_in, out_ref, part_ref, flat_ref, sem):
    copy = pltpu.make_async_copy(weight_in.at[:, :, my_head()], part_ref, sem)
    copy.start()
    copy.wait()
    flat_ref[...] = part_ref[...].astype(f32).reshape(flat_ref.shape)
    depth, parts = weight_in.shape[:2]
    for t in range(parts):
        out_ref[:, t * HEAD_DIM : (t + 1) * HEAD_DIM] = flat_ref[pl.ds(t, depth, stride=parts), :].astype(bf16)


def group_forward_kernel(*refs):
    *norm_ins, weight_in, act_ref, slope_ref, att_ref, back_ref, out_ref, inverse_ref, prod_ref = refs[:-3]
    weight_ref, norm_ref, sem = refs[-3:]
    pairs = [(weight_in, weight_ref)] + [(one, norm_ref.at[s]) for s, one in enumerate(norm_ins)]
    copies = [pltpu.make_async_copy(a, b, sem.at[i]) for i, (a, b) in enumerate(pairs)]
    for copy in copies:
        copy.start()
    for copy in copies:
        copy.wait()
    rows = att_ref.shape[1]
    total = out_ref.shape[0] // len(norm_ins)
    weight = weight_ref[...]
    acts, masks, spans = [], [], []
    for s in range(len(norm_ins)):
        for m in range(total // rows):
            lines = pl.ds(s * total + m * rows, rows)
            pre_act = dot(norm_ref[s, m * rows : (m + 1) * rows, :], weight, NN)
            logistic = jax.nn.sigmoid(pre_act)
            act = (pre_act * logistic).astype(bf16)
            act_ref[lines, :] = act
            slope_ref[lines, :] = slope_of(pre_act, logistic)
            spans.append(lines)
            masks.append(seq_mask(held_sizes(norm_ref[s, total:, :128], m), rows))
            acts.append([act[:, t * HEAD_DIM : (t + 1) * HEAD_DIM] for t in range(4)])
    for lines, act, result in zip(spans, acts, attend_all(acts, masks)):
        att_ref[lines, :], back_ref[lines, :], out_ref[lines, :], inverse_ref[lines, :] = result
        prod_ref[lines, :] = (result[2] * act[0].astype(f32)).astype(bf16)


def attend_back_all(incoming, acts, results):
    mixed = [
        norm_back(a * act[0].astype(f32), normed, inverse).astype(bf16)
        for a, act, (_, _, normed, inverse) in zip(incoming, acts, results)
    ]
    grads = [dot(a, act[1], NT) for a, act in zip(mixed, acts)]
    values = [dot(result[0], a, TN) for result, a in zip(results, mixed)]
    grads = [(a * result[1]).astype(bf16) for a, result in zip(grads, results)]
    queries = [dot(a, act[3], NN) for a, act in zip(grads, acts)]
    keys = [dot(a, act[2], TN) for a, act in zip(grads, acts)]
    gates = [a * result[2] for a, result in zip(incoming, results)]
    return list(zip(gates, values, queries, keys))


def rows_kernel(slot_ref, returned_ref, out_ref):
    micro, rows = slot_ref.shape
    for m in range(micro):
        lines = pl.ds(m * rows, rows)
        pick = one_hot(slot_ref[m : m + 1], returned_ref.shape[0])
        out_ref[lines, :] = dot(pick, returned_ref[...], TN)


def add_kernel(mine_ref, other_ref, top_ref, out_ref):
    out_ref[...] = (mine_ref[...] + other_ref[...] + top_ref[...]).astype(bf16)


def trunk_kernel(length_ref, norm_ref, row_ref, proj_ref, mix_ref, weight_in, og_ref, part_ref, pre_ref, weight_ref, sem):
    copies = [pltpu.make_async_copy(weight_in.at[t], weight_ref.at[t], sem.at[t]) for t in range(4)]
    for copy in copies:
        copy.start()
    rows = HEAD_DIM
    total, cols = row_ref.shape[0], weight_ref.shape[2]
    out_grad = dot(row_ref[...], proj_ref[...], NT).astype(bf16)
    og_ref[...] = out_grad
    grad_product = dot(out_grad, mix_ref[...], NT)
    for copy in copies:
        copy.wait()
    for m in range(total // rows):
        lines = pl.ds(m * rows, rows)
        normed = norm_ref[lines, :]
        acts, slopes = [], []
        for t in range(4):
            pre_act = dot(normed, weight_ref[t], NN)
            logistic = jax.nn.sigmoid(pre_act)
            acts.append((pre_act * logistic).astype(bf16))
            slopes.append(slope_of(pre_act, logistic))
        heads = [slice(h * HEAD_DIM, (h + 1) * HEAD_DIM) for h in range(cols // HEAD_DIM)]
        acts = [[act[:, lanes] for act in acts] for lanes in heads]
        masks = [seq_mask([length_ref[m, 0, i] for i in range(SEQS)], rows)] * len(heads)
        incoming = [grad_product[m * rows : (m + 1) * rows, lanes] for lanes in heads]
        for lanes, grads in zip(heads, attend_back_all(incoming, acts, attend_all(acts, masks))):
            for t, grad in enumerate(grads):
                pre_ref[t, lines, lanes] = (grad * slopes[t][:, lanes]).astype(bf16)
    part_ref[...] = sum(dot(pre_ref[t], weight_ref[t], NT) for t in range(4))


def inputs_kernel(input_ref, og_ref, mine_ref, other_ref, out_ref):
    micro, rows, _ = input_ref.shape
    for m in range(micro):
        lines = pl.ds(m * rows, rows)
        normed, inverse = row_norm(input_ref[m].astype(f32))
        grad = norm_back(mine_ref[lines, :] + other_ref[lines, :], normed, inverse)
        out_ref[m] = (og_ref[lines, :].astype(f32) + grad).astype(bf16)


def weights_kernel(group, owners, *refs):
    row_refs, norm_refs = refs[:group], refs[group : 2 * group]
    act_ref, slope_ref, att_ref, back_ref, out_ref, inverse_ref, prod_ref, proj_ref, mix_ref, *table_refs, packed_ref = refs[2 * group :]
    total = row_refs[0].shape[0]
    rows = att_ref.shape[1]
    cols = act_ref.shape[1]
    count = total // rows
    mix = mix_ref[my_head(), :]
    mixing, expand = 0.0, 0.0
    spans, incoming = [], []
    for s in range(group):
        out_grad = dot(row_refs[s][...], proj_ref[...], NT).astype(bf16)
        mixing += dot(out_grad, prod_ref[s * total : (s + 1) * total, :], TN)
        grad_product = dot(out_grad, mix, NT)
        for m in range(count):
            spans.append(pl.ds(s * total + m * rows, rows))
            incoming.append(grad_product[m * rows : (m + 1) * rows])
    packed_ref[:, :, cols : cols + HEAD_DIM] = mixing.reshape(owners, -1, HEAD_DIM).astype(bf16)
    table = table_refs[0][...].astype(f32) + table_refs[1][...].astype(f32)
    packed_ref[:, :, cols + HEAD_DIM :] = table.astype(bf16)
    acts = [[act_ref[lines, t * HEAD_DIM : (t + 1) * HEAD_DIM] for t in range(4)] for lines in spans]
    results = [(att_ref[lines, :], back_ref[lines, :], out_ref[lines, :], inverse_ref[lines, :]) for lines in spans]
    grads = attend_back_all(incoming, acts, results)
    pre = [(jnp.concatenate(grad, axis=1) * slope_ref[lines, :]).astype(bf16) for grad, lines in zip(grads, spans)]
    for s in range(group):
        expand += dot(norm_refs[s][:total, :], jnp.concatenate(pre[s * count : (s + 1) * count], axis=0), TN)
    packed_ref[:, :, :cols] = expand.reshape(owners, -1, cols).astype(bf16)


def final_kernel(group, in_ref, expand_ref, mixing_ref, table_ref):
    cols = expand_ref.shape[2]
    side = range(group)
    for g in side:
        sources = [(y * group + z) * group + x for y in side for z in side for x in side if x % 2 + 2 * (y % 2) == g]
        total = sum(in_ref[i, :, : cols + HEAD_DIM].astype(f32) for i in sources)
        head = pl.ds(g * HEAD_DIM, HEAD_DIM)
        for t in range(4):
            expand_ref[:, t, head] = total[:, t * HEAD_DIM : (t + 1) * HEAD_DIM]
        mixing_ref[:, head] = total[:, cols:]
    width = table_ref.shape[1] // 2
    for z in side:
        total = sum(in_ref[(y * group + z) * group + x, :, cols + HEAD_DIM :].astype(f32) for y in side for x in side)
        part, half, count = z % PARTS, z // PARTS, total.shape[0]
        table_ref[part * count : (part + 1) * count, half * width : (half + 1) * width] = total


def body(
    inputs,
    lengths,
    expand_weight,
    mixing_weight,
    projection,
    saved_rows,
    cluster_ids,
    item_ids,
    top_table,
    codebook,
):
    micro, rows, model_width = inputs.shape
    total = micro * rows
    owners = lax.axis_size(DEV)
    group = lax.axis_size("x")
    half_clusters, width = top_table.shape
    books, items, _ = codebook.shape
    cols = expand_weight.shape[2]
    slots = owners * micro * CAP
    own = half_clusters // owners
    saved = saved_rows.reshape(total, width)

    sent, slot_ids, marks = call(
        functools.partial(dispatch_kernel, owners, books, items),
        "dispatch",
        [((slots, width + 128), bf16), ((micro, rows), jnp.int32), ((total, 128), f32)],
        (cluster_ids, item_ids, saved_rows),
        "HHH HVH", limit=56,
    )
    got = lax.all_to_all(sent.reshape(owners, slots // owners, -1), DEV, 0, 0, tiled=True).reshape(slots, -1)

    late_inputs, late_saved, _ = lax.optimization_barrier((inputs, saved, slot_ids))
    normed, logits, stats, table = call(
        functools.partial(first_kernel, PARTS, owners),
        "norms_and_logits",
        [
            ((total + 16, model_width), bf16),
            ((total, half_clusters), f32),
            ((total, 128), f32),
            (top_table.shape, bf16),
        ],
        (lengths, late_inputs, late_saved, top_table),
        "SHHH VVVV",
        limit=FIRST_LIMIT,
    )
    normed_all = [normed] + [from_member(normed, s) for s in range(1, group)]
    row_top, *top_grads, top_token = call(
        functools.partial(top_grad_kernel, PARTS, own),
        "top_grads",
        [((total, width), f32)] + [((total, half_clusters // PARTS + width), bf16)] * PARTS,
        (logits, stats, swap(stats), marks, table, saved),
        "VVVHHH " + "H" * (1 + PARTS),
        limit=40,
        token=True,
    )
    top_all = [top_grads[0], from_pair(top_grads[1], "z", 1)]

    leaf, leaf_stats, got_held, book_held = leaf_scores(got, codebook, (top_token, normed[:8, :128]))
    back, leaf_grad = leaf_back(
        got_held, leaf, leaf_stats, swap(leaf_stats), book_held, ()
    )
    returned = lax.all_to_all(back.reshape(owners, slots // owners, width), DEV, 0, 0, tiled=True)

    row_top = row_top + swap(row_top)
    head_weight, head_token = call(
        head_weight_kernel,
        "head_weight",
        [((model_width, 4 * HEAD_DIM), bf16)],
        (expand_weight,),
        "R H",
        scratch=[
            pltpu.VMEM((model_width, 4, HEAD_DIM), bf16),
            pltpu.VMEM((model_width * 4, HEAD_DIM), f32),
            pltpu.SemaphoreType.DMA,
        ],
        after=(back, sum(a[:8, :128] for a in normed_all[1:])),
        token=True,
    )

    table_keep, table_send, table_token = call(
        functools.partial(table_kernel, owners),
        "table_part",
        [((owners, own // PARTS, width // 2), bf16)] * 2,
        top_all,
        "V" * PARTS + " VV",
        limit=16,
        after=(back, head_token),
        token=True,
    )

    table_other = from_pair(table_send, "z", 2)

    (row_part,) = call(
        rows_kernel,
        "rows",
        [((total, width), f32)],
        (slot_ids, returned.reshape(slots, width)),
        "VH V",
        limit=28,
        after=(table_token,),
    )
    (row_grad,) = call(add_kernel, "row_grad", [((total, width), bf16)], (row_part, swap(row_part), row_top), "VVV V", limit=28)
    row_all = [row_grad] + [from_member(row_grad, s) for s in range(1, group)]

    group_rows = group * total
    group_forward = call(
        group_forward_kernel,
        "group_forward",
        [
            ((group_rows, 4 * HEAD_DIM), bf16),
            ((group_rows, 4 * HEAD_DIM), f32),
            ((group_rows, rows), bf16),
            ((group_rows, rows), f32),
            ((group_rows, HEAD_DIM), f32),
            ((group_rows, HEAD_DIM), f32),
            ((group_rows, HEAD_DIM), bf16),
        ],
        (*normed_all, head_weight),
        "R" * (group + 1) + " " + "V" * 7,
        limit=GROUP_LIMIT,
        after=(row_grad,),
        scratch=[
            pltpu.VMEM(head_weight.shape, bf16),
            pltpu.VMEM((group, total + 16, model_width), bf16),
            pltpu.SemaphoreType.DMA((group + 1,)),
        ],
    )

    (packed,) = call(
        functools.partial(weights_kernel, group, owners),
        "weight_parts",
        [((owners, model_width // owners, cols + HEAD_DIM + width // 2), bf16)],
        (*row_all, *normed_all, *group_forward, projection, mixing_weight, table_keep, table_other),
        "V" * (2 * group + 11) + " H",
        limit=28,
    )
    arrived = lax.all_to_all(packed, DEV, 0, 0, tiled=True)

    late_weight, _ = lax.optimization_barrier((expand_weight, packed))
    weight = late_weight.swapaxes(0, 1)
    out_grad, grad_part = call(
        trunk_kernel,
        "trunk",
        [((total, model_width), bf16), ((total, model_width), f32)],
        (lengths, normed, row_grad, projection, mixing_weight, weight),
        "SHHHHR VV",
        limit=28,
        scratch=[pltpu.VMEM((4, total, cols), bf16), pltpu.VMEM(weight.shape, bf16), pltpu.SemaphoreType.DMA((4,))],
        after=(packed,),
    )
    (grad_inputs,) = call(
        inputs_kernel, "input_grads", [(inputs.shape, bf16)], (inputs, out_grad, grad_part, swap(grad_part)), "HVVV H", limit=48
    )
    book_grads = leaf_book(got, leaf_grad, books, width, (packed,))
    share = model_width // owners
    expand, mixing, table_share = call(
        functools.partial(final_kernel, group),
        "weight_sums",
        [((share, 4, cols), f32), ((share, cols), f32), ((own, width), f32)],
        (arrived,),
        "V HHH",
        limit=28,
    )
    return grad_inputs, expand, mixing.T, table_share, book_grads


def solution(mesh):
    grid = Mesh(mesh.devices.reshape(2, 4, 4, 4), ("section",) + DEV)
    return jax.shard_map(
        body,
        mesh=grid,
        in_specs=(
            P(None, DEV, None),
            P(None, DEV, None),
            P(None, None, "section"),
            P("section", None),
            P(),
            P(None, DEV, None),
            P(None, DEV),
            P(None, DEV),
            P("section", None),
            P(DEV, "section", None),
        ),
        out_specs=(
            P(None, DEV, None),
            P(DEV, None, "section"),
            P("section", DEV),
            P(("section",) + DEV, None),
            P(DEV, "section", None),
        ),
        check_vma=False,
    )
```
